256 devices in a mesh: grp: 8 (over z), dev: 32 (over x, y, core).
Axes of the slice: x: 4, y: 4, z: 8, core: 2. Of those that a mesh axis runs over, the one named last changes fastest.
Arguments:
- rhs: float32 [2097152], P(('grp', 'dev')), may hold values from -6 to 6
- points: float32 [3, 2097152], P(None, ('grp', 'dev')), as said below
- leaf_basis: float32 [8192, 256, 64], P(('grp', 'dev')), may hold values from -0.375 to 0.375
- transfer: float32 [8192, 64, 64], P(('grp', 'dev')), may hold values from -0.75 to 0.75
- leaf_skel: float32 [3, 524288], P(None, ('grp', 'dev')), as said below
- node_skel: float32 [3, 16384], P(None, ('grp', 'dev')), as said below
- near_ids: int32 [8192, 8], P(('grp', 'dev')), may hold values from 0 to 8191, as said below
- near_count: int32 [8192], P(('grp', 'dev')), may hold values from 1 to 8, as said below
- far_leaf: int32 [8192, 16], P(('grp', 'dev')), may hold values from 0 to 8191, as said below
- far_node: int32 [256, 32], P(('grp', 'dev')), may hold values from 0 to 255
Outputs:
- solution: float32 [2097152], P(('grp', 'dev'))
- residual: float32 [2097152], P(('grp', 'dev'))
The draws below stay inside these ranges and needn't reach their ends.
Inputs may be any that keep to these rules, and one draw needn't show every extreme that they name: Each leaf's points lie about a centre of their own; leaves in Morton order. `leaf_skel`: skeleton points lie about their leaf's centre. `node_skel`: skeleton points lie about the centre of their node's leaves. `near_ids`: slot 0 is the leaf itself; every entry is a leaf of the leaf's own device or of the devices just before and after it in Morton order. `near_count`: slots at or past the count are ignored. `far_leaf`: every entry is a leaf of the same grp index as the leaf.
All inputs are finite; a program needn't handle non-finite values.
Results may differ from the reference program's by a relative error of at most 0.0003.
Values sent between devices are 32-bit elements; how exact they have to be, the bound alone decides.
No kernel may reach another device: no remote copies, remote signals or barrier semaphores. Data moves between devices by JAX's collectives and lax.ppermute only.
A program may use at most 64 MiB of HBM per device.

```python
import math
import jax
import jax.numpy as jnp
from jax import lax

LEAF = 256
RANK = 64
LEAF_DEV = 32
NEAR = 8
FAR_LEAF = 16
FAR_TOP = 32
ITERS = 2
NODES = 256
LEAVES = 8192
NPTS = 2097152
N_DEV = 32


def layout(key, lowest, highest):
    place = jnp.arange(LEAVES, dtype=jnp.float32) / LEAVES
    jitter = jax.random.normal(jax.random.fold_in(key, 101), (3, LEAVES), jnp.float32) * 0.01
    centre = jnp.stack([0.5 + 0.4 * jnp.sin(9.0 * place), 0.5 + 0.4 * jnp.sin(7.0 * place + 1.0), 0.5 + 0.4 * jnp.cos(5.0 * place)]) + jitter
    spread = jnp.exp(jax.random.uniform(jax.random.fold_in(key, 102), (LEAVES,), jnp.float32, math.log(lowest), math.log(highest)))
    return (centre, spread)


def scatter_noise(key, shape):
    return jax.random.normal(key, shape, jnp.float32)


def draw_points(key, part):
    centre, spread = layout(key, 0.25, 0.6)
    key = jax.random.fold_in(key, 1)
    noise = scatter_noise(key, (3, LEAVES, LEAF))
    return (centre[:, :, None] + spread[None, :, None] * noise).reshape(3, LEAVES * LEAF)


def draw_leaf_skel(key, part):
    centre, spread = layout(key, 0.25, 0.6)
    key = jax.random.fold_in(key, 2)
    noise = scatter_noise(key, (3, LEAVES, RANK))
    return (centre[:, :, None] + spread[None, :, None] * noise).reshape(3, LEAVES * RANK)


def draw_node_skel(key, part):
    centre, spread = layout(key, 0.25, 0.6)
    width = 0.45
    key = jax.random.fold_in(key, 3)
    middle = centre.reshape(3, NODES, LEAF_DEV).mean(axis=2)
    noise = scatter_noise(key, (3, NODES, RANK))
    return (middle[:, :, None] + width * noise).reshape(3, NODES * RANK)


def draw_near_ids(key, part):
    key = jax.random.fold_in(key, 4)
    leaf = jnp.arange(LEAVES, dtype=jnp.int32)
    device = leaf // LEAF_DEV
    offset = jax.random.randint(key, (LEAVES, NEAR), -LEAF_DEV, 2 * LEAF_DEV)
    cand = jnp.clip(device[:, None] * LEAF_DEV + offset, 0, LEAVES - 1)
    return cand.at[:, 0].set(leaf).astype(jnp.int32)


def draw_near_count(key, part):
    key = jax.random.fold_in(key, 5)
    caps = jax.random.randint(jax.random.fold_in(key, 1), (NODES,), 2, NEAR + 1)
    busy = jax.random.randint(jax.random.fold_in(key, 2), (), 0, NODES)
    caps = jnp.where(jnp.arange(NODES) == busy, NEAR, caps)
    leaf = jnp.arange(LEAVES, dtype=jnp.int32)
    device = leaf // LEAF_DEV
    counts = jax.random.randint(jax.random.fold_in(key, 3), (LEAVES,), 1, NEAR + 1)
    counts = jnp.minimum(counts, caps[device])
    counts = jnp.where(leaf % LEAF_DEV == 0, caps[device], counts)
    return counts.astype(jnp.int32)


def draw_far_leaf(key, part):
    key = jax.random.fold_in(key, 6)
    group_size = LEAF_DEV * N_DEV
    leaf = jnp.arange(LEAVES, dtype=jnp.int32)
    group = leaf // group_size
    pick = jax.random.randint(key, (LEAVES, FAR_LEAF), 0, group_size)
    return (group[:, None] * group_size + pick).astype(jnp.int32)


def touch_ends(drawn, stream_key, least, largest):
    longest = drawn.shape.index(max(drawn.shape))
    spots = []
    for shift in (0, 1):
        where = [jax.random.randint(jax.random.fold_in(stream_key, axis), (), 0, length) for axis, length in enumerate(drawn.shape)]
        where[longest] = (where[longest] + shift) % drawn.shape[longest]
        spots.append(tuple(where))
    return drawn.at[spots[0]].set(least).at[spots[1]].set(largest)


def block_levels(key, shape, split, smallest, largest):
    level = 1.0
    for axis_at, blocks in split:
        steps = jax.random.uniform(jax.random.fold_in(jax.random.fold_in(key, 6), axis_at), (blocks,), jnp.float32, smallest / len(split), largest / len(split))
        level = level * jnp.repeat(jnp.exp(steps), shape[axis_at] // blocks).reshape((-1,) + (1,) * (len(shape) - 1 - axis_at))
    return level


def normal_values(stream_key, extent, scale, limit, shards=(), held_as=jnp.bfloat16):
    level = block_levels(stream_key, extent, shards, -0.22, 0.18) if shards else 1.0
    array = jax.random.normal(stream_key, extent, jnp.float32) * scale * level
    return jnp.minimum(jnp.maximum(array, -limit), limit).astype(held_as)


def setup_inputs(seed: int = 0) -> dict:
    key_of = jax.random.split(jax.random.key(seed), 11)
    return {
        "rhs": normal_values(key_of[0], (NPTS,), 1.0, 6.0, ((0, 256),), jnp.float32),
        "points": draw_points(jax.random.fold_in(key_of[10], 71), 0),
        "leaf_basis": normal_values(key_of[2], (LEAVES, LEAF, RANK), LEAF ** -0.5, 0.375, ((0, 256),), jnp.float32),
        "transfer": normal_values(key_of[3], (LEAVES, RANK, RANK), RANK ** -0.5, 0.75, ((0, 256),), jnp.float32),
        "leaf_skel": draw_leaf_skel(jax.random.fold_in(key_of[10], 71), 0),
        "node_skel": draw_node_skel(jax.random.fold_in(key_of[10], 71), 0),
        "near_ids": draw_near_ids(jax.random.fold_in(key_of[10], 71), 0),
        "near_count": draw_near_count(jax.random.fold_in(key_of[10], 71), 0),
        "far_leaf": draw_far_leaf(jax.random.fold_in(key_of[10], 71), 0),
        "far_node": touch_ends(jax.random.randint(key_of[9], (NODES, FAR_TOP), 0, NODES), jax.random.fold_in(key_of[9], 1), 0, NODES - 1).astype(jnp.int32),
    }


HIGH = lax.Precision.HIGHEST
amplitude = 0.00390625
length_scale = 0.25
nugget = 2.0

def matern(left, right):
    dist_sq = jnp.zeros(left.shape[1:-1] + (left.shape[-1], right.shape[-1]), jnp.float32)
    for comp in range(3):
        diff = left[comp][..., :, None] - right[comp][..., None, :]
        dist_sq = dist_sq + diff * diff
    scaled = jnp.sqrt(dist_sq) * (math.sqrt(5.0) / length_scale)
    return amplitude * (1.0 + scaled + scaled * scaled / 3.0) * jnp.exp(-scaled)

def reference(rhs, points, leaf_basis, transfer, leaf_skel, node_skel, near_ids, near_count, far_leaf, far_node):
    pts = points.reshape(3, LEAVES, LEAF)
    leaf_sk = leaf_skel.reshape(3, LEAVES, RANK)
    node_sk = node_skel.reshape(3, NODES, RANK)
    blocks = jnp.arange(LEAVES, dtype=jnp.int32).reshape(NODES, LEAF_DEV)

    def apply(field):
        values = field.reshape(LEAVES, LEAF)
        weights = jnp.einsum('lpr,lp->lr', leaf_basis, values, precision=HIGH)
        upward = jnp.einsum('lrs,lr->ls', transfer, weights, precision=HIGH)
        upward = upward.reshape(NODES, LEAF_DEV, RANK).sum(axis=1)

        def node_far(node):
            partners = far_node[node]
            kern = matern(node_sk[:, node, :][:, None, :], node_sk[:, partners, :])
            return jnp.einsum('jrs,js->r', kern, upward[partners], precision=HIGH)
        downward = lax.map(node_far, jnp.arange(NODES, dtype=jnp.int32))

        def leaf_block(ids):
            partners = far_leaf[ids]
            kern = matern(leaf_sk[:, ids, :][:, :, None, :], leaf_sk[:, partners, :])
            local = jnp.einsum('ljrs,ljs->lr', kern, weights[partners], precision=HIGH)
            local = local + jnp.einsum('lrs,ls->lr', transfer[ids], downward[ids // LEAF_DEV], precision=HIGH)
            own = pts[:, ids, :]
            total = jnp.zeros((LEAF_DEV, LEAF), jnp.float32)
            for slot in range(NEAR):
                nbr = near_ids[ids, slot]
                block = matern(own, pts[:, nbr, :])
                part = jnp.einsum('lik,lk->li', block, values[nbr], precision=HIGH)
                total = total + jnp.where((slot < near_count[ids])[:, None], part, 0.0)
            far_part = jnp.einsum('lpr,lr->lp', leaf_basis[ids], local, precision=HIGH)
            return nugget * values[ids] + far_part + total
        return lax.map(leaf_block, blocks).reshape(-1)
    solution = jnp.zeros_like(rhs)
    residual, direction = (rhs, rhs)
    norm_now = jnp.sum(residual * residual)
    for step in range(ITERS):
        image = apply(direction)
        alpha = norm_now / jnp.sum(direction * image)
        solution = solution + alpha * direction
        residual = residual - alpha * image
        norm_next = jnp.sum(residual * residual)
        direction = residual + norm_next / norm_now * direction
        norm_now = norm_next
    return (solution, residual)
```

```python
import functools
import math

import jax
import jax.numpy as jnp
from jax import lax
from jax.experimental import pallas as pl
from jax.experimental.pallas import tpu as pltpu
from jax.sharding import PartitionSpec as P

AXES = ("grp", "dev")
F32 = jnp.float32
BF16 = jnp.bfloat16
LN2 = math.log(2.0)
AMPLITUDE = 0.00390625
LENGTH = 0.25
NUGGET = 2.0
SCALE = math.sqrt(5.0) / LENGTH / LN2
SHIFT = 1.5 / LN2
OFFSET = 0.75 / (LN2 * LN2)
FACTOR = AMPLITUDE * LN2 * LN2 / 3.0
SMEM = pl.BlockSpec(memory_space=pltpu.SMEM)
LEAVES, PTS, RANK = 32, 256, 64
DEPTH = 48
DUMMY = 96
STEP = 4
LIST = 272


def params():
    return pltpu.CompilerParams(vmem_limit_bytes=58 * 1024 * 1024)


def split(x):
    hi = x.astype(BF16).astype(F32)
    rest = x - hi
    mid = rest.astype(BF16).astype(F32)
    return hi, mid, rest - mid


def rows_of(shape):
    return lax.broadcasted_iota(jnp.int32, shape, 0)


def lanes_of(shape):
    return lax.broadcasted_iota(jnp.int32, shape, 1)


def source_stack(coords):
    row = rows_of(coords.shape)
    norm = jnp.sum(coords * coords, axis=0, keepdims=True)
    full = jnp.where(row < 3, coords, jnp.where(row == 3, norm, jnp.where(row == 4, 1.0, 0.0)))
    hi, mid, low = split(full)
    return jnp.concatenate([hi, hi, mid, mid, hi, low], axis=0).astype(BF16)


def target_stack(coords):
    row = rows_of(coords.shape)
    norm = jnp.sum(coords * coords, axis=0, keepdims=True)
    full = jnp.where(row < 3, -2.0 * coords, jnp.where(row == 3, 1.0, jnp.where(row == 4, norm, 0.0)))
    hi, mid, low = split(full)
    stack = jnp.concatenate([hi, mid, hi, mid, low, hi, jnp.zeros((128 - DEPTH,) + hi.shape[1:], F32)], axis=0)
    return stack.T.astype(BF16)


def weighted(dist_sq, weights):
    dist_sq = jnp.maximum(dist_sq, 1e-30)
    dist = dist_sq * lax.rsqrt(dist_sq)
    moved = dist + SHIFT
    value = (moved * moved + OFFSET) * jnp.exp2(-dist) * weights
    total = value[:, :128]
    for at in range(128, value.shape[1], 128):
        total = total + value[:, at : at + 128]
    return total


def centred(tile, centre):
    shape = tile.shape
    return jnp.where(rows_of(shape) < 3, (tile - centre) * SCALE, 0.0)


def eight(tile):
    return jnp.concatenate([tile, jnp.zeros((8 - tile.shape[0], tile.shape[1]), F32)], axis=0)


def row_of(ref, l):
    pair = ref[pl.ds(2 * l, 2), :]
    return jnp.concatenate([pair[:1], pair[1:]], axis=1)


def pair_of(row):
    return jnp.concatenate([row[:, :128], row[:, 128:]], axis=0)


def project(carry, l, row, basis_ref, transfer_ref):
    weights, node = carry
    column = jnp.sum(basis_ref[l] * row, axis=1, keepdims=True)
    return jnp.where(lanes_of(weights.shape) == l, column, weights), node + transfer_ref[l] * column


def project_start():
    return jnp.zeros((RANK, 128), F32), jnp.zeros((RANK, RANK), F32)


def project_end(carry):
    rows = carry[0].T
    return jnp.concatenate([rows[:16], rows[16:32]], axis=1), jnp.sum(carry[1], axis=0, keepdims=True)


def prepare_kernel(rhs_ref, points_ref, basis_ref, transfer_ref, leaf_skel_ref, node_skel_ref, near_ref, pay_ref):
    near_ref[:3, :] = points_ref[...]
    for half in range(2 * LEAVES):
        near_ref[3:4, half * 128 : (half + 1) * 128] = rhs_ref[half : half + 1, :]
    weights, node = project_end(
        lax.fori_loop(
            0, LEAVES, lambda l, c: project(c, l, row_of(rhs_ref, l), basis_ref, transfer_ref), project_start(), unroll=8
        )
    )
    skel = leaf_skel_ref[...]
    tiles = []
    for m in range(16):
        low = skel[:, m * RANK : (m + 1) * RANK]
        high = skel[:, (m + 16) * RANK : (m + 17) * RANK]
        tiles.append(jnp.concatenate([low, high], axis=1))
        tiles.append(weights[m : m + 1])
    own = node_skel_ref[...]
    tiles.append(jnp.concatenate([own[:1], own[1:2]], axis=1))
    tiles.append(jnp.concatenate([own[2:3], node], axis=1))
    tiles.append(jnp.zeros((6, 128), F32))
    payload = jnp.concatenate(tiles, axis=0)
    for d in range(32):
        pay_ref[d] = payload


def near_pairs(list_ref, target_ref, centre_ref, source_ref, acc_ref, dist_ref):
    def distances(code, slot):
        l = lax.shift_right_logical(code, 8)
        centre = centre_ref[l]
        coords = centred(source_ref[code & 255], jnp.concatenate([centre, centre], axis=1))
        dist_ref[slot] = jnp.dot(target_ref[l, :, :DEPTH], source_stack(coords), preferred_element_type=F32)

    def products(code, slot):
        l = lax.shift_right_logical(code, 8)
        weights = source_ref[code & 255, 3:4, :] * FACTOR
        for at in range(0, PTS, 64):
            acc_ref[l, at : at + 64, :] += weighted(dist_ref[slot, at : at + 64, :], weights)

    def step(i, carry):
        codes = [list_ref[STEP * i + k + 1] for k in range(STEP + 1)]
        for k in range(STEP):
            distances(codes[k + 1], (k + 1) % 2)
            products(codes[k], k % 2)
        return carry

    distances(list_ref[1], 0)
    lax.fori_loop(0, (list_ref[0] + STEP - 1) // STEP, step, 0)


def clear(acc_ref):
    def leaf(l, carry):
        acc_ref[l] = jnp.zeros((PTS, 128), F32)
        return carry

    lax.fori_loop(0, LEAVES, leaf, 0, unroll=2)


def near_rows(acc_ref, out_ref, add_ref):
    def leaf(l, carry):
        parts = [jnp.sum(acc_ref[l, h * 128 : (h + 1) * 128, :].T, axis=0, keepdims=True) for h in range(2)]
        value = jnp.concatenate(parts, axis=0)
        if add_ref is not None:
            value = value + add_ref[pl.ds(2 * l, 2), :]
        out_ref[pl.ds(2 * l, 2), :] = value
        return carry

    lax.fori_loop(0, LEAVES, leaf, 0, unroll=4)


def fill(source_ref, at, block_ref):
    for l in range(LEAVES):
        source_ref[at + l] = eight(block_ref[:, l * PTS : (l + 1) * PTS])
    source_ref[DUMMY] = jnp.zeros((8, PTS), F32)


def set_values(source_ref, at, block_ref):
    for l in range(LEAVES):
        pair = block_ref[2 * l : 2 * l + 2, :]
        source_ref[at + l, 3:4, :] = jnp.concatenate([pair[:1], pair[1:]], axis=1)


def skel_target(tile):
    wide = jnp.concatenate([eight(tile), jnp.zeros((8, 64), F32)], axis=1)
    centre = jnp.broadcast_to(jnp.sum(wide, axis=1, keepdims=True) * (1.0 / RANK), wide.shape)
    return centre, target_stack(centred(wide, centre))[:RANK]


def own_first_kernel(
    ids_ref, count_ref, pay_ref, skel_ref, target_ref, centre_ref, far_target_ref, far_centre_ref, own_list_ref, other_list_ref, out_ref,
    source_ref, acc_ref, dist_ref,
):
    here = lax.shift_right_logical(ids_ref[0, 0], 5)
    base = (here - 1) * LEAVES

    def leaf_slots(l, counts):
        def slot(j, counts):
            own, other = counts
            n = ids_ref[j, l]
            code = l * 256 + (n - base)
            is_own = (lax.shift_right_logical(n, 5) == here).astype(jnp.int32)
            own_list_ref[own] = code
            other_list_ref[other] = code
            return own + is_own, other + 1 - is_own

        return lax.fori_loop(0, jnp.minimum(count_ref[l], 8), slot, counts)

    own, other = lax.fori_loop(0, LEAVES, leaf_slots, (jnp.int32(1), jnp.int32(1)))
    for k in range(STEP + 1):
        own_list_ref[own + k] = DUMMY
        other_list_ref[other + k] = DUMMY
    own_list_ref[0] = own - 1
    other_list_ref[0] = other - 1
    fill(source_ref, LEAVES, pay_ref)
    clear(acc_ref)

    def targets(l, carry):
        tile = source_ref[LEAVES + l]
        centre = jnp.broadcast_to(jnp.sum(tile, axis=1, keepdims=True) * (1.0 / PTS), (8, 128))
        centre_ref[l] = centre
        target_ref[l] = target_stack(centred(tile, jnp.concatenate([centre, centre], axis=1)))
        return carry

    lax.fori_loop(0, LEAVES, targets, 0, unroll=4)
    near_pairs(own_list_ref, target_ref, centre_ref, source_ref, acc_ref, dist_ref)
    near_rows(acc_ref, out_ref, None)
    for l in range(LEAVES):
        far_centre_ref[l], far_target_ref[l] = skel_target(skel_ref[:, l * RANK : (l + 1) * RANK])


def own_next_kernel(own_list_ref, pay_ref, field_ref, target_ref, centre_ref, out_ref, source_ref, acc_ref, dist_ref):
    fill(source_ref, LEAVES, pay_ref)
    set_values(source_ref, LEAVES, field_ref)
    clear(acc_ref)
    near_pairs(own_list_ref, target_ref, centre_ref, source_ref, acc_ref, dist_ref)
    near_rows(acc_ref, out_ref, None)


def node_first_kernel(in_ref, out_ref):
    block = jnp.concatenate([in_ref[:, 0, :], in_ref[:, 1, :]], axis=0)
    for g in range(8):
        out_ref[g] = block


def node_next_kernel(in_ref, out_ref):
    for g in range(8):
        out_ref[g] = in_ref[:, 0, :]


def swap(tile):
    return pltpu.roll(tile, 64, 1)


def far_partners(far_leaf_ref, l, rows_at):
    low_lanes = lanes_of((1, 128)) < 64
    for j in range(8):
        tiles = []
        for k in range(2):
            p = far_leaf_ref[2 * j + k, l] & 1023
            tile = rows_at(lax.shift_right_logical(p, 5), p & 15)
            here = (lax.shift_right_logical(p, 4) & 1) == k
            tiles.append(jnp.where(here, tile, swap(tile)))
        yield jnp.where(low_lanes, tiles[0], tiles[1])


def far_sums(stack_ref, weight_ref, target_ref, out_ref, dist_ref):
    def distances(l, slot):
        for c in range(4):
            dist_ref[slot, c * RANK : (c + 1) * RANK, :] = jnp.dot(
                target_ref[l, :, :DEPTH], stack_ref[l, :, c * 256 : (c + 1) * 256], preferred_element_type=F32
            )

    def products(l, slot):
        total = jnp.zeros((RANK, 128), F32)
        for c in range(4):
            weights = weight_ref[l, :1, c * 256 : (c + 1) * 256]
            total = total + weighted(dist_ref[slot, c * RANK : (c + 1) * RANK, :], weights)
        out_ref[l] = total

    def step(i, carry):
        for k in range(STEP):
            distances(jnp.minimum(STEP * i + k + 1, LEAVES - 1), (k + 1) % 2)
            products(STEP * i + k, k % 2)
        return carry

    distances(0, 0)
    lax.fori_loop(0, LEAVES // STEP, step, 0)


def middle_first_kernel(
    other_list_ref, far_leaf_ref, prev_ref, next_ref, target_ref, centre_ref, own_ref, far_target_ref, far_centre_ref, group_ref,
    near_ref, far_ref, stack_ref, source_ref, acc_ref, dist_ref, weight_ref,
):
    def gather(l, carry):
        centre = far_centre_ref[l]
        rows = far_partners(far_leaf_ref, l, lambda d, m: group_ref[d, pl.ds(4 * m, 4), :])
        for j, tile in enumerate(rows):
            at = j * 128
            weight_ref[l, :1, at : at + 128] = tile[3:4] * FACTOR
            stack_ref[l, :, at : at + 128] = source_stack(centred(eight(tile), centre))
        return carry

    lax.fori_loop(0, LEAVES, gather, 0, unroll=2)
    far_sums(stack_ref, weight_ref, far_target_ref, far_ref, dist_ref)
    fill(source_ref, 0, prev_ref)
    fill(source_ref, 2 * LEAVES, next_ref)
    clear(acc_ref)
    near_pairs(other_list_ref, target_ref, centre_ref, source_ref, acc_ref, dist_ref)
    near_rows(acc_ref, near_ref, own_ref)


def middle_next_kernel(
    other_list_ref, far_leaf_ref, prev_ref, next_ref, prev_val_ref, next_val_ref, target_ref, centre_ref, own_ref, far_target_ref,
    stack_ref, group_ref, near_ref, far_ref, source_ref, acc_ref, dist_ref, weight_ref,
):
    def gather(l, carry):
        rows = far_partners(far_leaf_ref, l, lambda d, m: group_ref[d, pl.ds(m, 1), :])
        for j, tile in enumerate(rows):
            weight_ref[l, :1, j * 128 : (j + 1) * 128] = tile * FACTOR
        return carry

    lax.fori_loop(0, LEAVES, gather, 0, unroll=2)
    far_sums(stack_ref, weight_ref, far_target_ref, far_ref, dist_ref)
    fill(source_ref, 0, prev_ref)
    fill(source_ref, 2 * LEAVES, next_ref)
    set_values(source_ref, 0, prev_val_ref)
    set_values(source_ref, 2 * LEAVES, next_val_ref)
    clear(acc_ref)
    near_pairs(other_list_ref, target_ref, centre_ref, source_ref, acc_ref, dist_ref)
    near_rows(acc_ref, near_ref, own_ref)


def node_down(far_node_ref, node_skel_ref, nodes_ref, weight_ref):
    low_lanes = lanes_of((1, 128)) < 64
    own = node_skel_ref[...]
    centre, target = skel_target(jnp.concatenate([own[:1], own[2:3], own[1:2]], axis=0))
    total = jnp.zeros((RANK, 128), F32)
    for at in range(0, 32, 4):
        coords, weights = [], []
        for j in (at, at + 2):
            tiles = []
            for p in (far_node_ref[0, j], far_node_ref[0, j + 1]):
                g, d = lax.shift_right_logical(p, 5), p & 31
                rows = [nodes_ref[g, pl.ds(d, 1), :], nodes_ref[g, pl.ds(d + 32, 1), :]]
                if weight_ref is not None:
                    rows.append(weight_ref[g, pl.ds(d, 1), :])
                tiles.append(jnp.concatenate(rows, axis=0))
            even = jnp.where(low_lanes, tiles[0], swap(tiles[1]))
            odd = jnp.where(low_lanes, swap(tiles[0]), tiles[1])
            coords.append(eight(jnp.concatenate([even[:2], odd[:2]], axis=0)))
            weights.append(odd[1:2] if weight_ref is None else even[2:3])
        wide = jnp.concatenate([centre, centre], axis=1)
        sources = source_stack(centred(jnp.concatenate(coords, axis=1), wide))
        dist_sq = jnp.dot(target[:, :DEPTH], sources, preferred_element_type=F32)
        total = total + weighted(dist_sq, jnp.concatenate(weights, axis=1) * FACTOR)
    return jnp.sum(total.T, axis=0, keepdims=True)


def leaf_row(l, down, far_ref, near_ref, basis_ref, transfer_ref):
    moved = transfer_ref[l] * down
    total = far_ref[l] + jnp.concatenate([moved, jnp.zeros((RANK, 64), F32)], axis=1)
    column = jnp.sum(total, axis=1, keepdims=True)
    return row_of(near_ref, l) + jnp.sum(basis_ref[l] * column, axis=0, keepdims=True)


def scalars(values):
    lane = lanes_of((1, 128))
    out = jnp.zeros((1, 128), F32)
    for at, value in enumerate(values):
        out = jnp.where(lane == 64 + at, value, out)
    return out


def dot(a, b):
    return jnp.sum(jnp.sum(a * b, axis=0, keepdims=True), axis=1, keepdims=True)


def finish_first_kernel(
    far_node_ref, node_skel_ref, nodes_ref, near_ref, far_ref, rhs_ref, basis_ref, transfer_ref, out_ref, pay_ref
):
    down = node_down(far_node_ref, node_skel_ref, nodes_ref, None)

    def leaf(l, carry):
        row = leaf_row(l, down, far_ref, near_ref, basis_ref, transfer_ref)
        out_ref[pl.ds(2 * l, 2), :] = pair_of(row)
        return project(carry, l, row, basis_ref, transfer_ref)

    weights, node = project_end(lax.fori_loop(0, LEAVES, leaf, project_start(), unroll=8))
    rhs, image = rhs_ref[...], out_ref[...]
    extra = scalars([dot(rhs, rhs), dot(rhs, image)])
    last = jnp.where(lanes_of((1, 128)) < 64, jnp.concatenate([node, node], axis=1), extra)
    payload = jnp.concatenate([weights, last, jnp.zeros((7, 128), F32)], axis=0)
    for d in range(32):
        pay_ref[d] = payload


def lane(row, at):
    return jnp.sum(jnp.where(lanes_of(row.shape) == at, row, 0.0), axis=1, keepdims=True)


def first_scalars(node_ref):
    total = jnp.sum(jnp.sum(node_ref[...], axis=0), axis=0, keepdims=True)
    norm, inner = lane(total, 64), lane(total, 65)
    energy = NUGGET * norm + inner
    return norm, inner, energy, norm / energy


def finish_next_kernel(
    far_node_ref, node_skel_ref, nodes_ref, node_in_ref, near_ref, far_ref, rhs_ref, field_ref, basis_ref, transfer_ref, out_ref, pay_ref
):
    down = node_down(far_node_ref, node_skel_ref, nodes_ref, node_in_ref)

    def leaf(l, carry):
        out_ref[pl.ds(2 * l, 2), :] = pair_of(leaf_row(l, down, far_ref, near_ref, basis_ref, transfer_ref))
        return carry

    lax.fori_loop(0, LEAVES, leaf, 0, unroll=8)
    _, inner, energy, alpha = first_scalars(node_in_ref)
    rhs, field, field2 = rhs_ref[...], field_ref[...], out_ref[...]
    keep = inner / energy
    residual = keep * rhs - alpha * field
    image = NUGGET * residual + keep * field - alpha * field2
    base = NUGGET * rhs + field
    block = scalars([dot(residual, residual), dot(residual, image), dot(residual, base) + dot(rhs, image)])
    pay_ref[...] = jnp.broadcast_to(block[None], pay_ref.shape)


def last_kernel(rhs_ref, field_ref, field2_ref, node_ref, last_ref, solution_ref, residual_ref):
    norm, inner, energy, alpha = first_scalars(node_ref)
    total = jnp.sum(last_ref[...], axis=0)
    norm2 = lane(total, 64)
    beta = norm2 / norm
    alpha2 = norm2 / (lane(total, 65) + beta * lane(total, 66) + beta * beta * energy)
    rhs, field, field2 = rhs_ref[...], field_ref[...], field2_ref[...]
    keep = inner / energy
    residual = keep * rhs - alpha * field
    image = NUGGET * residual + keep * field - alpha * field2
    direction = residual + beta * rhs
    solution_ref[...] = alpha * rhs + alpha2 * direction
    residual_ref[...] = residual - alpha2 * (image + beta * (NUGGET * rhs + field))


def whole(shape):
    return pl.BlockSpec(shape, lambda i: (0,) * len(shape))


def call(kernel, name, outs, ins, scratch=(), work=0):
    def spec(shape, dtype):
        return SMEM if dtype == jnp.int32 else whole(shape)

    return pl.pallas_call(
        kernel,
        grid=(1,),
        out_shape=[jax.ShapeDtypeStruct(shape, dtype) for shape, dtype in outs],
        in_specs=[spec(array.shape, array.dtype) for array in ins],
        out_specs=[spec(shape, dtype) for shape, dtype in outs],
        scratch_shapes=list(scratch),
        compiler_params=params(),
        cost_estimate=pl.CostEstimate(flops=work * 1_000_000_000, bytes_accessed=1_000_000, transcendentals=0),
        name=name,
    )(*ins)


def neighbours(block):
    count = lax.axis_size("grp") * lax.axis_size("dev")
    up = [(i, i + 1) for i in range(count - 1)]
    down = [(i + 1, i) for i in range(count - 1)]
    return lax.ppermute(block, AXES, up), lax.ppermute(block, AXES, down)


def exchange(copies, axes):
    return lax.all_to_all(copies, axes, 0, 0, tiled=True)


def on_device(rhs, points, leaf_basis, transfer, leaf_skel, node_skel, near_ids, near_count, far_leaf, far_node):
    rhs = rhs.reshape(2 * LEAVES, 128)
    basis = jnp.swapaxes(leaf_basis, 1, 2)
    far_leaf = far_leaf.T
    I32 = jnp.int32
    vector = ((2 * LEAVES, 128), F32)
    distances = pltpu.VMEM((2, PTS, 256), F32)
    near_scratch = [pltpu.VMEM((DUMMY + 1, 8, PTS), F32), pltpu.VMEM((LEAVES, PTS, 128), F32), distances]
    far_scratch = [pltpu.VMEM((LEAVES, 8, 1024), F32)]
    near_pay, pay = call(
        prepare_kernel,
        "prepare",
        [((4, LEAVES * PTS), F32), ((32, 72, 128), F32)],
        [rhs, points, basis, transfer, leaf_skel, node_skel],
        work=4,
    )
    prev_pay, next_pay = neighbours(near_pay)
    group = exchange(pay, "dev")
    targets, centres, far_targets, far_centres, own_list, other_list, own_part = call(
        own_first_kernel,
        "own_first",
        [
            ((LEAVES, PTS, 128), BF16),
            ((LEAVES, 8, 128), F32),
            ((LEAVES, RANK, 128), BF16),
            ((LEAVES, 8, 128), F32),
            ((LIST,), I32),
            ((LIST,), I32),
            vector,
        ],
        [near_ids.T, near_count, near_pay, leaf_skel],
        near_scratch,
        work=15,
    )
    (node_pay,) = call(node_first_kernel, "node_first", [((8, 64, 128), F32)], [group[:, 64:72]], work=1)
    nodes = exchange(node_pay, "grp")
    near_part, far_part, stacks = call(
        middle_first_kernel,
        "middle_first",
        [vector, ((LEAVES, RANK, 128), F32), ((LEAVES, DEPTH, 1024), BF16)],
        [other_list, far_leaf, prev_pay, next_pay, targets, centres, own_part, far_targets, far_centres, group],
        near_scratch + far_scratch,
        work=20,
    )
    field, pay = call(
        finish_first_kernel,
        "finish_first",
        [vector, ((32, 24, 128), F32)],
        [far_node, node_skel, nodes, near_part, far_part, rhs, basis, transfer],
        work=4,
    )
    prev_val, next_val = neighbours(field)
    leaf_in = exchange(pay, "dev")
    (own_part,) = call(
        own_next_kernel, "own_next", [vector], [own_list, near_pay, field, targets, centres], near_scratch, work=10
    )
    (node_pay,) = call(node_next_kernel, "node_next", [((8, 32, 128), F32)], [leaf_in[:, 16:24]], work=1)
    node_in = exchange(node_pay, "grp")
    near_part, far_part = call(
        middle_next_kernel,
        "middle_next",
        [vector, ((LEAVES, RANK, 128), F32)],
        [
            other_list, far_leaf, prev_pay, next_pay, prev_val, next_val, targets, centres, own_part, far_targets, stacks, leaf_in,
        ],
        near_scratch + far_scratch,
        work=20,
    )
    field2, pay = call(
        finish_next_kernel,
        "finish_next",
        [vector, ((256, 1, 128), F32)],
        [far_node, node_skel, nodes, node_in, near_part, far_part, rhs, field, basis, transfer],
        work=4,
    )
    last = exchange(pay, AXES)
    answer, residual = call(last_kernel, "last", [vector, vector], [rhs, field, field2, node_in, last], work=1)
    return answer.reshape(-1), residual.reshape(-1)


def solution(mesh):
    placed = (
        P(AXES),
        P(None, AXES),
        P(AXES, None, None),
        P(AXES, None, None),
        P(None, AXES),
        P(None, AXES),
        P(AXES, None),
        P(AXES),
        P(AXES, None),
        P(AXES, None),
    )
    return jax.shard_map(on_device, mesh=mesh, in_specs=placed, out_specs=(P(AXES), P(AXES)), check_vma=False)
```

```python
import math

import jax
import jax.numpy as jnp
from jax import lax
from jax.experimental import pallas as pl
from jax.experimental.pallas import tpu as pltpu
from jax.sharding import PartitionSpec as P

AXES = ("grp", "dev")
F32 = jnp.float32
BF16 = jnp.bfloat16
LN2 = math.log(2.0)
AMPLITUDE = 0.00390625
LENGTH = 0.25
NUGGET = 2.0
SCALE = math.sqrt(5.0) / LENGTH / 3.0
POWER = -3.0 / LN2
FACTOR = AMPLITUDE * 3.0
SMEM = pl.BlockSpec(memory_space=pltpu.SMEM)
LEAVES, PTS, RANK = 32, 256, 64
DEPTH = 48
DUMMY = 96
STEP = 4
LIST = 272


def params():
    return pltpu.CompilerParams(vmem_limit_bytes=58 * 1024 * 1024)


def split(x):
    hi = x.astype(BF16).astype(F32)
    rest = x - hi
    mid = rest.astype(BF16).astype(F32)
    return hi, mid, rest - mid


def rows_of(shape):
    return lax.broadcasted_iota(jnp.int32, shape, 0)


def lanes_of(shape):
    return lax.broadcasted_iota(jnp.int32, shape, 1)


def source_stack(coords):
    row = rows_of(coords.shape)
    norm = jnp.sum(coords * coords, axis=0, keepdims=True)
    full = jnp.where(row < 3, coords, jnp.where(row == 3, norm, jnp.where(row == 4, 1.0, 0.0)))
    hi, mid, low = split(full)
    return jnp.concatenate([hi, hi, mid, mid, hi, low], axis=0).astype(BF16)


def target_stack(coords):
    row = rows_of(coords.shape)
    norm = jnp.sum(coords * coords, axis=0, keepdims=True)
    full = jnp.where(row < 3, -2.0 * coords, jnp.where(row == 3, 1.0, jnp.where(row == 4, norm, 0.0)))
    hi, mid, low = split(full)
    rest = jnp.zeros((128 - DEPTH,) + hi.shape[1:], F32)
    return jnp.concatenate([hi, mid, hi, mid, low, hi, rest], axis=0).T.astype(BF16)


def squares(targets, sources):
    return jnp.dot(targets[:, :DEPTH], sources, preferred_element_type=F32)


def weighted(dist_sq, weights):
    dist_sq = jnp.maximum(dist_sq, 1e-30)
    dist = dist_sq * lax.rsqrt(dist_sq)
    value = (dist_sq + (dist + 1.0 / 3.0)) * jnp.exp2(dist * POWER) * weights
    total = value[:, :128]
    for at in range(128, value.shape[1], 128):
        total = total + value[:, at : at + 128]
    return total


def centred(tile, centre):
    shape = tile.shape
    return jnp.where(rows_of(shape) < 3, (tile - centre) * SCALE, 0.0)


def eight(tile):
    return jnp.concatenate([tile, jnp.zeros((8 - tile.shape[0], tile.shape[1]), F32)], axis=0)


def row_of(ref, l):
    pair = ref[pl.ds(2 * l, 2), :]
    return jnp.concatenate([pair[:1], pair[1:]], axis=1)


def pair_of(row):
    return jnp.concatenate([row[:, :128], row[:, 128:]], axis=0)


def project(carry, l, row, basis_ref, transfer_ref):
    weights, node = carry
    column = jnp.sum(basis_ref[l] * row, axis=1, keepdims=True)
    return jnp.where(lanes_of(weights.shape) == l, column, weights), node + transfer_ref[l] * column


def project_start():
    return jnp.zeros((RANK, 128), F32), jnp.zeros((RANK, RANK), F32)


def project_end(carry):
    rows = carry[0].T
    return jnp.concatenate([rows[:16], rows[16:32]], axis=1), jnp.sum(carry[1], axis=0, keepdims=True)


def prepare_kernel(rhs_ref, points_ref, basis_ref, transfer_ref, leaf_skel_ref, node_skel_ref, near_ref, pay_ref):
    near_ref[:3, :] = points_ref[...]
    for half in range(2 * LEAVES):
        near_ref[3:4, half * 128 : (half + 1) * 128] = rhs_ref[half : half + 1, :]
    basis_ref.wait()
    transfer_ref.wait()
    weights, node = project_end(
        lax.fori_loop(
            0, LEAVES, lambda l, c: project(c, l, row_of(rhs_ref, l), basis_ref, transfer_ref), project_start(), unroll=8
        )
    )
    skel = leaf_skel_ref[...]
    tiles = []
    for m in range(16):
        low = skel[:, m * RANK : (m + 1) * RANK]
        high = skel[:, (m + 16) * RANK : (m + 17) * RANK]
        tiles.append(jnp.concatenate([low, high], axis=1))
        tiles.append(weights[m : m + 1])
    own = node_skel_ref[...]
    tiles.append(jnp.concatenate([own[:1], own[1:2]], axis=1))
    tiles.append(jnp.concatenate([own[2:3], node], axis=1))
    tiles.append(jnp.zeros((6, 128), F32))
    payload = jnp.concatenate(tiles, axis=0)
    for d in range(32):
        pay_ref[d] = payload


def near_parts(target_ref, centre_ref, source_ref, acc_ref, dist_ref):
    def distances(l, at, slot):
        centre = centre_ref[l]
        coords = centred(source_ref[at], jnp.concatenate([centre, centre], axis=1))
        dist_ref[slot] = squares(target_ref[l], source_stack(coords))

    def products(l, at, slot, first):
        weights = source_ref[at, 3:4, :] * FACTOR
        for row in range(0, PTS, 64):
            value = weighted(dist_ref[slot, row : row + 64, :], weights)
            if first:
                acc_ref[l, row : row + 64, :] = value
            else:
                acc_ref[l, row : row + 64, :] += value

    return distances, products


def near_self(target_ref, centre_ref, source_ref, acc_ref, dist_ref, beside, carry):
    distances, products = near_parts(target_ref, centre_ref, source_ref, acc_ref, dist_ref)

    def step(i, carry):
        for k in range(STEP):
            l = STEP * i + k
            later = jnp.minimum(l + 1, LEAVES - 1)
            distances(later, LEAVES + later, (k + 1) % 2)
            products(l, LEAVES + l, k % 2, True)
            carry = beside(l, carry)
        return carry

    distances(0, LEAVES, 0)
    return lax.fori_loop(0, LEAVES // STEP, step, carry)


def near_pairs(list_ref, target_ref, centre_ref, source_ref, acc_ref, dist_ref):
    distances, products = near_parts(target_ref, centre_ref, source_ref, acc_ref, dist_ref)

    def step(i, carry):
        codes = [list_ref[STEP * i + k + 1] for k in range(STEP + 1)]
        for k in range(STEP):
            distances(lax.shift_right_logical(codes[k + 1], 8), codes[k + 1] & 255, (k + 1) % 2)
            products(lax.shift_right_logical(codes[k], 8), codes[k] & 255, k % 2, False)
        return carry

    distances(lax.shift_right_logical(list_ref[1], 8), list_ref[1] & 255, 0)
    lax.fori_loop(0, (list_ref[0] + STEP - 1) // STEP, step, 0)


def clear(acc_ref):
    def leaf(l, carry):
        acc_ref[l] = jnp.zeros((PTS, 128), F32)
        return carry

    lax.fori_loop(0, LEAVES, leaf, 0, unroll=2)


def near_rows(acc_ref, out_ref, add_ref):
    def leaf(l, carry):
        parts = [jnp.sum(acc_ref[l, h * 128 : (h + 1) * 128, :].T, axis=0, keepdims=True) for h in range(2)]
        value = jnp.concatenate(parts, axis=0)
        if add_ref is not None:
            value = value + add_ref[pl.ds(2 * l, 2), :]
        out_ref[pl.ds(2 * l, 2), :] = value
        return carry

    lax.fori_loop(0, LEAVES, leaf, 0, unroll=4)


def fill(source_ref, at, block_ref):
    for l in range(LEAVES):
        source_ref[at + l] = eight(block_ref[:, l * PTS : (l + 1) * PTS])
    source_ref[DUMMY] = jnp.zeros((8, PTS), F32)


def set_values(source_ref, at, block_ref):
    for l in range(LEAVES):
        pair = block_ref[2 * l : 2 * l + 2, :]
        source_ref[at + l, 3:4, :] = jnp.concatenate([pair[:1], pair[1:]], axis=1)


def skel_target(tile):
    wide = jnp.concatenate([eight(tile), jnp.zeros((8, 64), F32)], axis=1)
    centre = jnp.broadcast_to(jnp.sum(wide, axis=1, keepdims=True) * (1.0 / RANK), wide.shape)
    return centre, target_stack(centred(wide, centre))[:RANK]


def own_first_kernel(
    ids_ref, count_ref, pay_ref, skel_ref, target_ref, centre_ref, far_target_ref, far_centre_ref, own_list_ref, other_list_ref, out_ref,
    source_ref, acc_ref, dist_ref,
):
    here = lax.shift_right_logical(ids_ref[0, 0], 5)
    base = (here - 1) * LEAVES

    fill(source_ref, LEAVES, pay_ref)

    def targets(l, carry):
        tile = source_ref[LEAVES + l]
        centre = jnp.broadcast_to(jnp.sum(tile, axis=1, keepdims=True) * (1.0 / PTS), (8, 128))
        centre_ref[l] = centre
        target_ref[l] = target_stack(centred(tile, jnp.concatenate([centre, centre], axis=1)))
        return carry

    lax.fori_loop(0, LEAVES, targets, 0, unroll=4)

    def slots(l, counts):
        own, other = counts
        used = count_ref[l]
        for j in range(1, 8):
            n = ids_ref[j, l]
            code = l * 256 + (n - base)
            own_list_ref[own] = code
            other_list_ref[other] = code
            is_used = (j < used).astype(jnp.int32)
            is_own = (lax.shift_right_logical(n, 5) == here).astype(jnp.int32) * is_used
            own, other = own + is_own, other + is_used - is_own
        return own, other

    one = jnp.int32(1)
    own, other = near_self(target_ref, centre_ref, source_ref, acc_ref, dist_ref, slots, (one, one))
    for k in range(STEP + 1):
        own_list_ref[own + k] = DUMMY
        other_list_ref[other + k] = DUMMY
    own_list_ref[0] = own - 1
    other_list_ref[0] = other - 1
    near_pairs(own_list_ref, target_ref, centre_ref, source_ref, acc_ref, dist_ref)
    near_rows(acc_ref, out_ref, None)
    for l in range(LEAVES):
        far_centre_ref[l], far_target_ref[l] = skel_target(skel_ref[:, l * RANK : (l + 1) * RANK])


def own_next_kernel(own_list_ref, pay_ref, field_ref, target_ref, centre_ref, out_ref, source_ref, acc_ref, dist_ref):
    fill(source_ref, LEAVES, pay_ref)
    set_values(source_ref, LEAVES, field_ref)
    near_self(target_ref, centre_ref, source_ref, acc_ref, dist_ref, lambda l, carry: carry, 0)
    near_pairs(own_list_ref, target_ref, centre_ref, source_ref, acc_ref, dist_ref)
    near_rows(acc_ref, out_ref, None)


def swap(tile):
    return pltpu.roll(tile, 64, 1)


def low_lanes():
    return lanes_of((1, 128)) < 64


def spread(tile):
    other = swap(tile)
    return jnp.where(low_lanes(), tile, other), jnp.where(low_lanes(), other, tile)


def far_partners(far_leaf_ref, l, rows_at):
    for j in range(0, 16, 2):
        yield jnp.where(low_lanes(), rows_at(far_leaf_ref[j, l] & 1023), rows_at(far_leaf_ref[j + 1, l] & 1023))


def far_sums(stack_ref, weight_ref, target_ref, out_ref, dist_ref):
    def distances(l, slot):
        for c in range(4):
            dist_ref[slot, c * RANK : (c + 1) * RANK, :] = squares(target_ref[l], stack_ref[l, :, c * 256 : (c + 1) * 256])

    def products(l, slot):
        total = jnp.zeros((RANK, 128), F32)
        for c in range(4):
            weights = weight_ref[l, :1, c * 256 : (c + 1) * 256]
            total = total + weighted(dist_ref[slot, c * RANK : (c + 1) * RANK, :], weights)
        column = jnp.sum(total, axis=1, keepdims=True)
        out_ref[...] = jnp.where(lanes_of((RANK, 128)) == l, column, out_ref[...])

    def step(i, carry):
        for k in range(STEP):
            distances(jnp.minimum(STEP * i + k + 1, LEAVES - 1), (k + 1) % 2)
            products(STEP * i + k, k % 2)
        return carry

    out_ref[...] = jnp.zeros((RANK, 128), F32)
    distances(0, 0)
    lax.fori_loop(0, LEAVES // STEP, step, 0)


def middle_first_kernel(
    other_list_ref, far_leaf_ref, prev_ref, next_ref, target_ref, centre_ref, own_ref, far_target_ref, far_centre_ref, group_ref,
    near_ref, far_ref, stack_out_ref, source_ref, acc_ref, dist_ref, weight_ref, table_ref, stack_ref, stack_sem,
):
    def table(d, carry):
        for m in range(0, 16, 2):
            low, high = spread(group_ref[d, 4 * m : 4 * m + 8, :])
            for k in range(2):
                table_ref[d * LEAVES + m + k] = low[4 * k : 4 * k + 4]
                table_ref[d * LEAVES + m + k + 16] = high[4 * k : 4 * k + 4]
        return carry

    lax.fori_loop(0, 32, table, 0, unroll=4)

    def gather(l, carry):
        centre = far_centre_ref[l]
        rows = far_partners(far_leaf_ref, l, lambda p: table_ref[p])
        for j, tile in enumerate(rows):
            at = j * 128
            weight_ref[l, :1, at : at + 128] = tile[3:4] * FACTOR
            stack_ref[l, :, at : at + 128] = source_stack(centred(eight(tile), centre))
        return carry

    lax.fori_loop(0, LEAVES, gather, 0, unroll=4)
    stack_copy = pltpu.make_async_copy(stack_ref, stack_out_ref, stack_sem)
    stack_copy.start()
    far_target_ref.wait()
    far_sums(stack_ref, weight_ref, far_target_ref, far_ref, dist_ref)
    for operand in (prev_ref, next_ref, target_ref, centre_ref, own_ref):
        operand.wait()
    fill(source_ref, 0, prev_ref)
    fill(source_ref, 2 * LEAVES, next_ref)
    clear(acc_ref)
    near_pairs(other_list_ref, target_ref, centre_ref, source_ref, acc_ref, dist_ref)
    near_rows(acc_ref, near_ref, own_ref)
    stack_copy.wait()


def middle_next_kernel(
    other_list_ref, far_leaf_ref, prev_ref, next_ref, prev_val_ref, next_val_ref, target_ref, centre_ref, own_ref, far_target_ref,
    stack_ref, group_ref, near_ref, far_ref, source_ref, acc_ref, dist_ref, weight_ref, table_ref,
):
    for d in range(32):
        low, high = spread(group_ref[d, :16, :])
        table_ref[d * LEAVES : d * LEAVES + 16, :] = low
        table_ref[d * LEAVES + 16 : d * LEAVES + 32, :] = high

    def gather(l, carry):
        rows = far_partners(far_leaf_ref, l, lambda p: table_ref[pl.ds(p, 1), :])
        for j, tile in enumerate(rows):
            weight_ref[l, :1, j * 128 : (j + 1) * 128] = tile * FACTOR
        return carry

    lax.fori_loop(0, LEAVES, gather, 0, unroll=4)
    for operand in (prev_ref, next_ref, prev_val_ref, next_val_ref, target_ref, centre_ref, own_ref):
        operand.wait()
    fill(source_ref, 0, prev_ref)
    fill(source_ref, 2 * LEAVES, next_ref)
    set_values(source_ref, 0, prev_val_ref)
    set_values(source_ref, 2 * LEAVES, next_val_ref)
    clear(acc_ref)
    near_pairs(other_list_ref, target_ref, centre_ref, source_ref, acc_ref, dist_ref)
    near_rows(acc_ref, near_ref, own_ref)
    far_target_ref.wait()
    stack_ref.wait()
    far_sums(stack_ref, weight_ref, far_target_ref, far_ref, dist_ref)


def node_down(far_node_ref, node_skel_ref, nodes_ref, weight_ref):
    own = node_skel_ref[...]
    centre, target = skel_target(jnp.concatenate([own[:1], own[2:3], own[1:2]], axis=0))
    total = jnp.zeros((RANK, 128), F32)
    for at in range(0, 32, 4):
        coords, weights = [], []
        for j in (at, at + 2):
            tiles = []
            for p in (far_node_ref[0, j], far_node_ref[0, j + 1]):
                g, d = lax.shift_right_logical(p, 5), p & 31
                rows = [nodes_ref[g, pl.ds(d, 1), :], nodes_ref[g, pl.ds(d + 32, 1), :]]
                if weight_ref is not None:
                    rows.append(weight_ref[g, pl.ds(d, 1), :])
                tiles.append(jnp.concatenate(rows, axis=0))
            even = jnp.where(low_lanes(), tiles[0], swap(tiles[1]))
            odd = jnp.where(low_lanes(), swap(tiles[0]), tiles[1])
            coords.append(eight(jnp.concatenate([even[:2], odd[:2]], axis=0)))
            weights.append(odd[1:2] if weight_ref is None else even[2:3])
        wide = jnp.concatenate([centre, centre], axis=1)
        sources = source_stack(centred(jnp.concatenate(coords, axis=1), wide))
        dist_sq = squares(target, sources)
        total = total + weighted(dist_sq, jnp.concatenate(weights, axis=1) * FACTOR)
    return jnp.sum(total.T, axis=0, keepdims=True)


def leaf_row(l, down, far_ref, near_ref, basis_ref, transfer_ref):
    moved = transfer_ref[l] * down
    total = jnp.where(lanes_of((RANK, 128)) == l, far_ref[...], 0.0) + jnp.concatenate([moved, jnp.zeros((RANK, 64), F32)], axis=1)
    column = jnp.sum(total, axis=1, keepdims=True)
    return row_of(near_ref, l) + jnp.sum(basis_ref[l] * column, axis=0, keepdims=True)


def scalars(values):
    lane = lanes_of((1, 128))
    out = jnp.zeros((1, 128), F32)
    for at, value in enumerate(values):
        out = jnp.where(lane == 64 + at, value, out)
    return out


def dot(a, b):
    return jnp.sum(jnp.sum(a * b, axis=0, keepdims=True), axis=1, keepdims=True)


def finish_first_kernel(
    far_node_ref, node_skel_ref, nodes_ref, near_ref, far_ref, rhs_ref, basis_ref, transfer_ref, out_ref, pay_ref
):
    down = node_down(far_node_ref, node_skel_ref, nodes_ref, None)
    for operand in (near_ref, far_ref, rhs_ref, basis_ref, transfer_ref):
        operand.wait()

    def leaf(l, carry):
        row = leaf_row(l, down, far_ref, near_ref, basis_ref, transfer_ref)
        out_ref[pl.ds(2 * l, 2), :] = pair_of(row)
        return project(carry, l, row, basis_ref, transfer_ref)

    weights, node = project_end(lax.fori_loop(0, LEAVES, leaf, project_start(), unroll=8))
    rhs, image = rhs_ref[...], out_ref[...]
    extra = scalars([dot(rhs, rhs), dot(rhs, image)])
    last = jnp.where(lanes_of((1, 128)) < 64, jnp.concatenate([node, node], axis=1), extra)
    payload = jnp.concatenate([weights, last, jnp.zeros((7, 128), F32)], axis=0)
    for d in range(32):
        pay_ref[d] = payload


def lane(row, at):
    return jnp.sum(jnp.where(lanes_of(row.shape) == at, row, 0.0), axis=1, keepdims=True)


def first_scalars(node_ref):
    total = jnp.sum(jnp.sum(node_ref[...], axis=0), axis=0, keepdims=True)
    norm, inner = lane(total, 64), lane(total, 65)
    energy = NUGGET * norm + inner
    return norm, inner, energy, norm / energy


def finish_next_kernel(
    far_node_ref, node_skel_ref, nodes_ref, node_in_ref, near_ref, far_ref, rhs_ref, field_ref, basis_ref, transfer_ref, out_ref, pay_ref
):
    down = node_down(far_node_ref, node_skel_ref, nodes_ref, node_in_ref)
    for operand in (near_ref, far_ref, rhs_ref, field_ref, basis_ref, transfer_ref):
        operand.wait()

    def leaf(l, carry):
        out_ref[pl.ds(2 * l, 2), :] = pair_of(leaf_row(l, down, far_ref, near_ref, basis_ref, transfer_ref))
        return carry

    lax.fori_loop(0, LEAVES, leaf, 0, unroll=8)
    _, inner, energy, alpha = first_scalars(node_in_ref)
    rhs, field, field2 = rhs_ref[...], field_ref[...], out_ref[...]
    keep = inner / energy
    residual = keep * rhs - alpha * field
    image = NUGGET * residual + keep * field - alpha * field2
    base = NUGGET * rhs + field
    block = scalars([dot(residual, residual), dot(residual, image), dot(residual, base) + dot(rhs, image)])
    pay_ref[...] = jnp.broadcast_to(block[None], pay_ref.shape)


def last_kernel(rhs_ref, field_ref, field2_ref, node_ref, last_ref, solution_ref, residual_ref):
    norm, inner, energy, alpha = first_scalars(node_ref)
    total = jnp.sum(last_ref[...], axis=0)
    norm2 = lane(total, 64)
    beta = norm2 / norm
    alpha2 = norm2 / (lane(total, 65) + beta * lane(total, 66) + beta * beta * energy)
    rhs, field, field2 = rhs_ref[...], field_ref[...], field2_ref[...]
    keep = inner / energy
    residual = keep * rhs - alpha * field
    image = NUGGET * residual + keep * field - alpha * field2
    direction = residual + beta * rhs
    solution_ref[...] = alpha * rhs + alpha2 * direction
    residual_ref[...] = residual - alpha2 * (image + beta * (NUGGET * rhs + field))


class Operand:
    def __init__(self, ref, copy):
        self.ref, self.copy = ref, copy
        self.shape = ref.shape

    def wait(self):
        self.copy.wait()

    def __getitem__(self, at):
        return self.ref[at]


def call(kernel, name, outs, ins, scratch=(), work=0, late=(), apart=()):
    floats = [at for at, array in enumerate(ins) if array.dtype != jnp.int32]

    def whole(shape):
        return pl.BlockSpec(shape, lambda i: (0,) * len(shape))

    def body(*refs):
        operands = list(refs[: len(ins)])
        buffers, sems = refs[-1 - len(floats) : -1], refs[-1]
        for k, at in enumerate(floats):
            operands[at] = Operand(buffers[k], pltpu.make_async_copy(operands[at], buffers[k], sems.at[k]))
        for at in [at for at in floats if at not in late] + list(late):
            operands[at].copy.start()
        for at in floats:
            if at not in late:
                operands[at].wait()
        kernel(*operands, *refs[len(ins) : -1 - len(floats)])

    return pl.pallas_call(
        body,
        grid=(1,),
        out_shape=[jax.ShapeDtypeStruct(shape, dtype) for shape, dtype in outs],
        in_specs=[SMEM if array.dtype == jnp.int32 else pl.BlockSpec(memory_space=pl.ANY) for array in ins],
        out_specs=[
            SMEM if dtype == jnp.int32 else pl.BlockSpec(memory_space=pl.ANY) if at in apart else whole(shape)
            for at, (shape, dtype) in enumerate(outs)
        ],
        scratch_shapes=list(scratch)
        + [pltpu.VMEM(ins[at].shape, ins[at].dtype) for at in floats]
        + [pltpu.SemaphoreType.DMA((len(floats),))],
        compiler_params=params(),
        cost_estimate=pl.CostEstimate(flops=work * 1_000_000_000, bytes_accessed=1_000_000, transcendentals=0),
        name=name,
    )(*ins)


def neighbours(block):
    count = lax.axis_size("grp") * lax.axis_size("dev")
    up = [(i, i + 1) for i in range(count - 1)]
    down = [(i + 1, i) for i in range(count - 1)]
    return lax.ppermute(block, AXES, up), lax.ppermute(block, AXES, down)


def exchange(copies, axes):
    return lax.all_to_all(copies, axes, 0, 0, tiled=True)


def on_device(rhs, points, leaf_basis, transfer, leaf_skel, node_skel, near_ids, near_count, far_leaf, far_node):
    rhs = rhs.reshape(2 * LEAVES, 128)
    basis = jnp.swapaxes(leaf_basis, 1, 2)
    far_leaf = far_leaf.T
    I32 = jnp.int32
    vector = ((2 * LEAVES, 128), F32)
    distances = pltpu.VMEM((2, PTS, 256), F32)
    near_scratch = [pltpu.VMEM((DUMMY + 1, 8, PTS), F32), pltpu.VMEM((LEAVES, PTS, 128), F32), distances]
    far_scratch = [pltpu.VMEM((LEAVES, 8, 1024), F32)]
    near_pay, pay = call(
        prepare_kernel,
        "prepare",
        [((4, LEAVES * PTS), F32), ((32, 72, 128), F32)],
        [rhs, points, basis, transfer, leaf_skel, node_skel],
        work=4,
        late=(2, 3),
    )
    prev_pay, next_pay = neighbours(near_pay)
    group = exchange(pay, "dev")
    targets, centres, far_targets, far_centres, own_list, other_list, own_part = call(
        own_first_kernel,
        "own_first",
        [
            ((LEAVES, PTS, 128), BF16),
            ((LEAVES, 8, 128), F32),
            ((LEAVES, RANK, 128), BF16),
            ((LEAVES, 8, 128), F32),
            ((LIST,), I32),
            ((LIST,), I32),
            vector,
        ],
        [near_ids.T, near_count, near_pay, leaf_skel],
        near_scratch,
        work=15,
    )
    rows = jnp.swapaxes(group[:, 64:66], 0, 1).reshape(1, 64, 128)
    node_pay = jnp.broadcast_to(rows, (8, 64, 128))
    nodes = exchange(node_pay, "grp")
    near_part, far_part, stacks = call(
        middle_first_kernel,
        "middle_first",
        [vector, ((RANK, 128), F32), ((LEAVES, DEPTH, 1024), BF16)],
        [other_list, far_leaf, prev_pay, next_pay, targets, centres, own_part, far_targets, far_centres, group],
        near_scratch + far_scratch + [pltpu.VMEM((1024, 4, 128), F32), pltpu.VMEM((LEAVES, DEPTH, 1024), BF16), pltpu.SemaphoreType.DMA],
        work=20,
        apart=(2,),
        late=(7, 2, 3, 4, 5, 6),
    )
    field, pay = call(
        finish_first_kernel,
        "finish_first",
        [vector, ((32, 24, 128), F32)],
        [far_node, node_skel, nodes, near_part, far_part, rhs, basis, transfer],
        work=4,
        late=(3, 4, 5, 6, 7),
    )
    prev_val, next_val = neighbours(field)
    leaf_in = exchange(pay, "dev")
    (own_part,) = call(
        own_next_kernel, "own_next", [vector], [own_list, near_pay, field, targets, centres], near_scratch, work=10
    )
    node_pay = jnp.broadcast_to(leaf_in[None, :, 16], (8, 32, 128))
    node_in = exchange(node_pay, "grp")
    near_part, far_part = call(
        middle_next_kernel,
        "middle_next",
        [vector, ((RANK, 128), F32)],
        [
            other_list, far_leaf, prev_pay, next_pay, prev_val, next_val, targets, centres, own_part, far_targets, stacks, leaf_in,
        ],
        near_scratch + far_scratch + [pltpu.VMEM((1024, 128), F32)],
        work=20,
        late=(6, 2, 3, 4, 5, 7, 8, 9, 10),
    )
    field2, pay = call(
        finish_next_kernel,
        "finish_next",
        [vector, ((256, 1, 128), F32)],
        [far_node, node_skel, nodes, node_in, near_part, far_part, rhs, field, basis, transfer],
        work=4,
        late=(4, 5, 6, 7, 8, 9),
    )
    last = exchange(pay, AXES)
    answer, residual = call(last_kernel, "last", [vector, vector], [rhs, field, field2, node_in, last], work=1)
    return answer.reshape(-1), residual.reshape(-1)


def solution(mesh):
    placed = (
        P(AXES),
        P(None, AXES),
        P(AXES, None, None),
        P(AXES, None, None),
        P(None, AXES),
        P(None, AXES),
        P(AXES, None),
        P(AXES),
        P(AXES, None),
        P(AXES, None),
    )
    return jax.shard_map(on_device, mesh=mesh, in_specs=placed, out_specs=(P(AXES), P(AXES)), check_vma=False)
```

```python
import math

import jax
import jax.numpy as jnp
from jax import lax
from jax.experimental import pallas as pl
from jax.experimental.pallas import tpu as pltpu
from jax.sharding import PartitionSpec as P

AXES = ("grp", "dev")
F32 = jnp.float32
BF16 = jnp.bfloat16
LN2 = math.log(2.0)
AMPLITUDE = 0.00390625
LENGTH = 0.25
NUGGET = 2.0
SCALE = math.sqrt(5.0) / LENGTH / 3.0
POWER = -3.0 / LN2
FACTOR = AMPLITUDE * 3.0
SMEM = pl.BlockSpec(memory_space=pltpu.SMEM)
LEAVES, PTS, RANK = 32, 256, 64
DEPTH = 48
DUMMY = 96
STEP = 4
LIST = 272


def params():
    return pltpu.CompilerParams(vmem_limit_bytes=58 * 1024 * 1024)


def split(x):
    hi = x.astype(BF16).astype(F32)
    rest = x - hi
    mid = rest.astype(BF16).astype(F32)
    return hi, mid, rest - mid


def rows_of(shape):
    return lax.broadcasted_iota(jnp.int32, shape, 0)


def lanes_of(shape):
    return lax.broadcasted_iota(jnp.int32, shape, 1)


def source_stack(coords):
    row = rows_of(coords.shape)
    norm = jnp.sum(coords * coords, axis=0, keepdims=True)
    full = jnp.where(row < 3, coords, jnp.where(row == 3, norm, jnp.where(row == 4, 1.0, 0.0)))
    hi, mid, low = split(full)
    return jnp.concatenate([hi, hi, mid, mid, hi, low], axis=0).astype(BF16)


def target_stack(coords):
    row = rows_of(coords.shape)
    norm = jnp.sum(coords * coords, axis=0, keepdims=True)
    full = jnp.where(row < 3, -2.0 * coords, jnp.where(row == 3, 1.0, jnp.where(row == 4, norm, 0.0)))
    hi, mid, low = split(full)
    rest = jnp.zeros((128 - DEPTH,) + hi.shape[1:], F32)
    return jnp.concatenate([hi, mid, hi, mid, low, hi, rest], axis=0).T.astype(BF16)


def squares(targets, sources):
    return jnp.dot(targets[:, :DEPTH], sources, preferred_element_type=F32)


def weighted(dist_sq, weights):
    dist_sq = jnp.maximum(dist_sq, 1e-30)
    dist = dist_sq * lax.rsqrt(dist_sq)
    value = (dist_sq + (dist + 1.0 / 3.0)) * jnp.exp2(dist * POWER) * weights
    total = value[:, :128]
    for at in range(128, value.shape[1], 128):
        total = total + value[:, at : at + 128]
    return total


def centred(tile, centre):
    shape = tile.shape
    return jnp.where(rows_of(shape) < 3, (tile - centre) * SCALE, 0.0)


def eight(tile):
    return jnp.concatenate([tile, jnp.zeros((8 - tile.shape[0], tile.shape[1]), F32)], axis=0)


def row_of(ref, l):
    pair = ref[pl.ds(2 * l, 2), :]
    return jnp.concatenate([pair[:1], pair[1:]], axis=1)


def pair_of(row):
    return jnp.concatenate([row[:, :128], row[:, 128:]], axis=0)


def project(carry, l, row, basis_ref, transfer_ref):
    weights, node = carry
    column = jnp.sum(basis_ref[l] * row, axis=1, keepdims=True)
    return jnp.where(lanes_of(weights.shape) == l, column, weights), node + transfer_ref[l] * column


def project_start():
    return jnp.zeros((RANK, 128), F32), jnp.zeros((RANK, RANK), F32)


def project_end(carry):
    rows = carry[0].T
    return jnp.concatenate([rows[:16], rows[16:32]], axis=1), jnp.sum(carry[1], axis=0, keepdims=True)


def prepare_kernel(rhs_ref, basis_ref, transfer_ref, leaf_skel_ref, node_skel_ref, pay_ref):
    weights, node = project_end(
        lax.fori_loop(
            0, LEAVES, lambda l, c: project(c, l, row_of(rhs_ref, l), basis_ref, transfer_ref), project_start(), unroll=8
        )
    )
    skel = leaf_skel_ref[...]
    tiles = []
    for m in range(16):
        low = skel[:, m * RANK : (m + 1) * RANK]
        high = skel[:, (m + 16) * RANK : (m + 17) * RANK]
        tiles.append(jnp.concatenate([low, high], axis=1))
        tiles.append(weights[m : m + 1])
    own = node_skel_ref[...]
    tiles.append(jnp.concatenate([own[:1], own[1:2]], axis=1))
    tiles.append(jnp.concatenate([own[2:3], node], axis=1))
    tiles.append(jnp.zeros((6, 128), F32))
    payload = jnp.concatenate(tiles, axis=0)
    for d in range(32):
        pay_ref[d] = payload


def near_parts(target_ref, centre_ref, source_ref, acc_ref, dist_ref):
    def distances(l, at, slot):
        centre = centre_ref[l]
        coords = centred(source_ref[at], jnp.concatenate([centre, centre], axis=1))
        dist_ref[slot] = squares(target_ref[l], source_stack(coords))

    def products(l, at, slot, first):
        weights = source_ref[at, 3:4, :] * FACTOR
        for row in range(0, PTS, 64):
            value = weighted(dist_ref[slot, row : row + 64, :], weights)
            if first:
                acc_ref[l, row : row + 64, :] = value
            else:
                acc_ref[l, row : row + 64, :] += value

    return distances, products


def near_self(target_ref, centre_ref, source_ref, acc_ref, dist_ref, beside, carry):
    distances, products = near_parts(target_ref, centre_ref, source_ref, acc_ref, dist_ref)

    def step(i, carry):
        for k in range(STEP):
            l = STEP * i + k
            later = jnp.minimum(l + 1, LEAVES - 1)
            distances(later, LEAVES + later, (k + 1) % 2)
            products(l, LEAVES + l, k % 2, True)
            carry = beside(l, carry)
        return carry

    distances(0, LEAVES, 0)
    return lax.fori_loop(0, LEAVES // STEP, step, carry)


def near_pairs(list_ref, target_ref, centre_ref, source_ref, acc_ref, dist_ref):
    distances, products = near_parts(target_ref, centre_ref, source_ref, acc_ref, dist_ref)

    def step(i, carry):
        codes = [list_ref[STEP * i + k + 1] for k in range(STEP + 1)]
        for k in range(STEP):
            distances(lax.shift_right_logical(codes[k + 1], 8), codes[k + 1] & 255, (k + 1) % 2)
            products(lax.shift_right_logical(codes[k], 8), codes[k] & 255, k % 2, False)
        return carry

    distances(lax.shift_right_logical(list_ref[1], 8), list_ref[1] & 255, 0)
    lax.fori_loop(0, (list_ref[0] + STEP - 1) // STEP, step, 0)


def clear(acc_ref):
    def leaf(l, carry):
        acc_ref[l] = jnp.zeros((PTS, 128), F32)
        return carry

    lax.fori_loop(0, LEAVES, leaf, 0, unroll=2)


def near_rows(acc_ref, out_ref, add_ref):
    def leaf(l, carry):
        parts = [jnp.sum(acc_ref[l, h * 128 : (h + 1) * 128, :].T, axis=0, keepdims=True) for h in range(2)]
        value = jnp.concatenate(parts, axis=0)
        if add_ref is not None:
            value = value + add_ref[pl.ds(2 * l, 2), :]
        out_ref[pl.ds(2 * l, 2), :] = value
        return carry

    lax.fori_loop(0, LEAVES, leaf, 0, unroll=4)


def fill(source_ref, at, block_ref):
    for l in range(LEAVES):
        source_ref[at + l] = eight(block_ref[:, l * PTS : (l + 1) * PTS])
    source_ref[DUMMY] = jnp.zeros((8, PTS), F32)


def set_values(source_ref, at, block_ref):
    for l in range(LEAVES):
        pair = block_ref[2 * l : 2 * l + 2, :]
        source_ref[at + l, 3:4, :] = jnp.concatenate([pair[:1], pair[1:]], axis=1)


def skel_target(tile):
    wide = jnp.concatenate([eight(tile), jnp.zeros((8, 64), F32)], axis=1)
    centre = jnp.broadcast_to(jnp.sum(wide, axis=1, keepdims=True) * (1.0 / RANK), wide.shape)
    return centre, target_stack(centred(wide, centre))[:RANK]


def own_first_kernel(
    ids_ref, count_ref, points_ref, rhs_ref, skel_ref, target_ref, centre_ref, far_target_ref, far_centre_ref, own_list_ref, other_list_ref, out_ref, near_ref,
    source_ref, acc_ref, dist_ref,
):
    here = lax.shift_right_logical(ids_ref[0, 0], 5)
    base = (here - 1) * LEAVES

    near_ref[:3, :] = points_ref[...]
    for half in range(2 * LEAVES):
        near_ref[3:4, half * 128 : (half + 1) * 128] = rhs_ref[half : half + 1, :]
    fill(source_ref, LEAVES, points_ref)
    set_values(source_ref, LEAVES, rhs_ref)

    def targets(l, carry):
        tile = source_ref[LEAVES + l]
        centre = jnp.broadcast_to(jnp.sum(tile, axis=1, keepdims=True) * (1.0 / PTS), (8, 128))
        centre_ref[l] = centre
        target_ref[l] = target_stack(centred(tile, jnp.concatenate([centre, centre], axis=1)))
        return carry

    lax.fori_loop(0, LEAVES, targets, 0, unroll=4)

    def slots(l, counts):
        own, other = counts
        used = count_ref[l]
        for j in range(1, 8):
            n = ids_ref[j, l]
            code = l * 256 + (n - base)
            own_list_ref[own] = code
            other_list_ref[other] = code
            is_used = (j < used).astype(jnp.int32)
            is_own = (lax.shift_right_logical(n, 5) == here).astype(jnp.int32) * is_used
            own, other = own + is_own, other + is_used - is_own
        return own, other

    one = jnp.int32(1)
    own, other = near_self(target_ref, centre_ref, source_ref, acc_ref, dist_ref, slots, (one, one))
    for k in range(STEP + 1):
        own_list_ref[own + k] = DUMMY
        other_list_ref[other + k] = DUMMY
    own_list_ref[0] = own - 1
    other_list_ref[0] = other - 1
    near_pairs(own_list_ref, target_ref, centre_ref, source_ref, acc_ref, dist_ref)
    near_rows(acc_ref, out_ref, None)
    for l in range(LEAVES):
        far_centre_ref[l], far_target_ref[l] = skel_target(skel_ref[:, l * RANK : (l + 1) * RANK])


def own_next_kernel(
    own_list_ref, points_ref, field_ref, target_ref, centre_ref, out_ref, field_out_ref, source_ref, acc_ref, dist_ref
):
    field_out_ref[...] = field_ref[...]
    fill(source_ref, LEAVES, points_ref)
    set_values(source_ref, LEAVES, field_ref)
    near_self(target_ref, centre_ref, source_ref, acc_ref, dist_ref, lambda l, carry: carry, 0)
    near_pairs(own_list_ref, target_ref, centre_ref, source_ref, acc_ref, dist_ref)
    near_rows(acc_ref, out_ref, None)


def swap(tile):
    return pltpu.roll(tile, 64, 1)


def low_lanes():
    return lanes_of((1, 128)) < 64


def spread(tile):
    other = swap(tile)
    return jnp.where(low_lanes(), tile, other), jnp.where(low_lanes(), other, tile)


def far_partners(far_leaf_ref, l, rows_at):
    for j in range(0, 16, 2):
        yield jnp.where(low_lanes(), rows_at(far_leaf_ref[j, l] & 1023), rows_at(far_leaf_ref[j + 1, l] & 1023))


def far_sums(stack_ref, weight_ref, target_ref, out_ref, dist_ref):
    def distances(l, slot):
        for c in range(4):
            dist_ref[slot, c * RANK : (c + 1) * RANK, :] = squares(target_ref[l], stack_ref[l, :, c * 256 : (c + 1) * 256])

    def products(l, slot):
        total = jnp.zeros((RANK, 128), F32)
        for c in range(4):
            weights = weight_ref[l, :1, c * 256 : (c + 1) * 256]
            total = total + weighted(dist_ref[slot, c * RANK : (c + 1) * RANK, :], weights)
        column = jnp.sum(total, axis=1, keepdims=True)
        out_ref[...] = jnp.where(lanes_of((RANK, 128)) == l, column, out_ref[...])

    def step(i, carry):
        for k in range(STEP):
            distances(jnp.minimum(STEP * i + k + 1, LEAVES - 1), (k + 1) % 2)
            products(STEP * i + k, k % 2)
        return carry

    out_ref[...] = jnp.zeros((RANK, 128), F32)
    distances(0, 0)
    lax.fori_loop(0, LEAVES // STEP, step, 0)


def middle_first_kernel(
    other_list_ref, far_leaf_ref, prev_ref, next_ref, target_ref, centre_ref, own_ref, far_target_ref, far_centre_ref, group_ref,
    near_ref, far_ref, stack_out_ref, source_ref, acc_ref, dist_ref, weight_ref, table_ref, stack_ref, stack_sem,
):
    def table(d, carry):
        for m in range(0, 16, 2):
            low, high = spread(group_ref[d, 4 * m : 4 * m + 8, :])
            for k in range(2):
                table_ref[d * LEAVES + m + k] = low[4 * k : 4 * k + 4]
                table_ref[d * LEAVES + m + k + 16] = high[4 * k : 4 * k + 4]
        return carry

    lax.fori_loop(0, 32, table, 0, unroll=4)

    def gather(l, carry):
        centre = far_centre_ref[l]
        rows = far_partners(far_leaf_ref, l, lambda p: table_ref[p])
        for j, tile in enumerate(rows):
            at = j * 128
            weight_ref[l, :1, at : at + 128] = tile[3:4] * FACTOR
            stack_ref[l, :, at : at + 128] = source_stack(centred(eight(tile), centre))
        return carry

    lax.fori_loop(0, LEAVES, gather, 0, unroll=4)
    stack_copy = pltpu.make_async_copy(stack_ref, stack_out_ref, stack_sem)
    stack_copy.start()
    far_target_ref.wait()
    far_sums(stack_ref, weight_ref, far_target_ref, far_ref, dist_ref)
    for operand in (prev_ref, next_ref, target_ref, centre_ref, own_ref):
        operand.wait()
    fill(source_ref, 0, prev_ref)
    fill(source_ref, 2 * LEAVES, next_ref)
    clear(acc_ref)
    near_pairs(other_list_ref, target_ref, centre_ref, source_ref, acc_ref, dist_ref)
    near_rows(acc_ref, near_ref, own_ref)
    stack_copy.wait()


def middle_next_kernel(
    other_list_ref, far_leaf_ref, prev_ref, next_ref, prev_val_ref, next_val_ref, target_ref, centre_ref, own_ref, far_target_ref,
    stack_ref, group_ref, near_ref, far_ref, source_ref, acc_ref, dist_ref, weight_ref, table_ref,
):
    for d in range(32):
        low, high = spread(group_ref[d, :16, :])
        table_ref[d * LEAVES : d * LEAVES + 16, :] = low
        table_ref[d * LEAVES + 16 : d * LEAVES + 32, :] = high

    def gather(l, carry):
        rows = far_partners(far_leaf_ref, l, lambda p: table_ref[pl.ds(p, 1), :])
        for j, tile in enumerate(rows):
            weight_ref[l, :1, j * 128 : (j + 1) * 128] = tile * FACTOR
        return carry

    lax.fori_loop(0, LEAVES, gather, 0, unroll=4)
    for operand in (prev_ref, next_ref, prev_val_ref, next_val_ref, target_ref, centre_ref, own_ref):
        operand.wait()
    fill(source_ref, 0, prev_ref)
    fill(source_ref, 2 * LEAVES, next_ref)
    set_values(source_ref, 0, prev_val_ref)
    set_values(source_ref, 2 * LEAVES, next_val_ref)
    clear(acc_ref)
    near_pairs(other_list_ref, target_ref, centre_ref, source_ref, acc_ref, dist_ref)
    near_rows(acc_ref, near_ref, own_ref)
    far_target_ref.wait()
    stack_ref.wait()
    far_sums(stack_ref, weight_ref, far_target_ref, far_ref, dist_ref)


def node_down(far_node_ref, node_skel_ref, nodes_ref, weight_ref):
    own = node_skel_ref[...]
    centre, target = skel_target(jnp.concatenate([own[:1], own[2:3], own[1:2]], axis=0))
    total = jnp.zeros((RANK, 128), F32)
    for at in range(0, 32, 4):
        coords, weights = [], []
        for j in (at, at + 2):
            tiles = []
            for p in (far_node_ref[0, j], far_node_ref[0, j + 1]):
                g, d = lax.shift_right_logical(p, 5), p & 31
                rows = [nodes_ref[g, pl.ds(d, 1), :], nodes_ref[g, pl.ds(d + 32, 1), :]]
                if weight_ref is not None:
                    rows.append(weight_ref[g, pl.ds(d, 1), :])
                tiles.append(jnp.concatenate(rows, axis=0))
            even = jnp.where(low_lanes(), tiles[0], swap(tiles[1]))
            odd = jnp.where(low_lanes(), swap(tiles[0]), tiles[1])
            coords.append(eight(jnp.concatenate([even[:2], odd[:2]], axis=0)))
            weights.append(odd[1:2] if weight_ref is None else even[2:3])
        wide = jnp.concatenate([centre, centre], axis=1)
        sources = source_stack(centred(jnp.concatenate(coords, axis=1), wide))
        dist_sq = squares(target, sources)
        total = total + weighted(dist_sq, jnp.concatenate(weights, axis=1) * FACTOR)
    return jnp.sum(total.T, axis=0, keepdims=True)


def leaf_row(l, down, far_ref, near_ref, basis_ref, transfer_ref):
    moved = transfer_ref[l] * down
    total = jnp.where(lanes_of((RANK, 128)) == l, far_ref[...], 0.0) + jnp.concatenate([moved, jnp.zeros((RANK, 64), F32)], axis=1)
    column = jnp.sum(total, axis=1, keepdims=True)
    return row_of(near_ref, l) + jnp.sum(basis_ref[l] * column, axis=0, keepdims=True)


def scalars(values):
    lane = lanes_of((1, 128))
    out = jnp.zeros((1, 128), F32)
    for at, value in enumerate(values):
        out = jnp.where(lane == 64 + at, value, out)
    return out


def dot(a, b):
    return jnp.sum(jnp.sum(a * b, axis=0, keepdims=True), axis=1, keepdims=True)


def finish_first_kernel(
    far_node_ref, node_skel_ref, nodes_ref, near_ref, far_ref, rhs_ref, basis_ref, transfer_ref, out_ref, pay_ref
):
    down = node_down(far_node_ref, node_skel_ref, nodes_ref, None)
    for operand in (near_ref, far_ref, rhs_ref, basis_ref, transfer_ref):
        operand.wait()

    def leaf(l, carry):
        row = leaf_row(l, down, far_ref, near_ref, basis_ref, transfer_ref)
        out_ref[pl.ds(2 * l, 2), :] = pair_of(row)
        return project(carry, l, row, basis_ref, transfer_ref)

    weights, node = project_end(lax.fori_loop(0, LEAVES, leaf, project_start(), unroll=8))
    rhs, image = rhs_ref[...], out_ref[...]
    extra = scalars([dot(rhs, rhs), dot(rhs, image)])
    last = jnp.where(lanes_of((1, 128)) < 64, jnp.concatenate([node, node], axis=1), extra)
    payload = jnp.concatenate([weights, last, jnp.zeros((7, 128), F32)], axis=0)
    for d in range(32):
        pay_ref[d] = payload


def lane(row, at):
    return jnp.sum(jnp.where(lanes_of(row.shape) == at, row, 0.0), axis=1, keepdims=True)


def first_scalars(node_ref):
    total = jnp.sum(jnp.sum(node_ref[...], axis=0), axis=0, keepdims=True)
    norm, inner = lane(total, 64), lane(total, 65)
    energy = NUGGET * norm + inner
    return norm, inner, energy, norm / energy


def finish_next_kernel(
    far_node_ref, node_skel_ref, nodes_ref, node_in_ref, near_ref, far_ref, rhs_ref, field_ref, basis_ref, transfer_ref, out_ref, pay_ref
):
    down = node_down(far_node_ref, node_skel_ref, nodes_ref, node_in_ref)
    for operand in (near_ref, far_ref, rhs_ref, field_ref, basis_ref, transfer_ref):
        operand.wait()

    def leaf(l, carry):
        out_ref[pl.ds(2 * l, 2), :] = pair_of(leaf_row(l, down, far_ref, near_ref, basis_ref, transfer_ref))
        return carry

    lax.fori_loop(0, LEAVES, leaf, 0, unroll=8)
    _, inner, energy, alpha = first_scalars(node_in_ref)
    rhs, field, field2 = rhs_ref[...], field_ref[...], out_ref[...]
    keep = inner / energy
    residual = keep * rhs - alpha * field
    image = NUGGET * residual + keep * field - alpha * field2
    base = NUGGET * rhs + field
    block = scalars([dot(residual, residual), dot(residual, image), dot(residual, base) + dot(rhs, image)])
    pay_ref[...] = jnp.broadcast_to(block[None], pay_ref.shape)


def last_kernel(rhs_ref, field_ref, field2_ref, node_ref, last_ref, solution_ref, residual_ref):
    norm, inner, energy, alpha = first_scalars(node_ref)
    total = jnp.sum(last_ref[...], axis=0)
    norm2 = lane(total, 64)
    beta = norm2 / norm
    alpha2 = norm2 / (lane(total, 65) + beta * lane(total, 66) + beta * beta * energy)
    rhs, field, field2 = rhs_ref[...], field_ref[...], field2_ref[...]
    keep = inner / energy
    residual = keep * rhs - alpha * field
    image = NUGGET * residual + keep * field - alpha * field2
    direction = residual + beta * rhs
    solution_ref[...] = alpha * rhs + alpha2 * direction
    residual_ref[...] = residual - alpha2 * (image + beta * (NUGGET * rhs + field))


class Operand:
    def __init__(self, ref, copy):
        self.ref, self.copy = ref, copy
        self.shape = ref.shape

    def wait(self):
        self.copy.wait()

    def __getitem__(self, at):
        return self.ref[at]


def call(kernel, name, outs, ins, scratch=(), work=0, late=(), apart=()):
    floats = [at for at, array in enumerate(ins) if array.dtype != jnp.int32]

    def whole(shape):
        return pl.BlockSpec(shape, lambda i: (0,) * len(shape))

    def body(*refs):
        operands = list(refs[: len(ins)])
        buffers, sems = refs[-1 - len(floats) : -1], refs[-1]
        for k, at in enumerate(floats):
            operands[at] = Operand(buffers[k], pltpu.make_async_copy(operands[at], buffers[k], sems.at[k]))
        for at in [at for at in floats if at not in late] + list(late):
            operands[at].copy.start()
        for at in floats:
            if at not in late:
                operands[at].wait()
        kernel(*operands, *refs[len(ins) : -1 - len(floats)])

    return pl.pallas_call(
        body,
        grid=(1,),
        out_shape=[jax.ShapeDtypeStruct(shape, dtype) for shape, dtype in outs],
        in_specs=[SMEM if array.dtype == jnp.int32 else pl.BlockSpec(memory_space=pl.ANY) for array in ins],
        out_specs=[
            SMEM if dtype == jnp.int32 else pl.BlockSpec(memory_space=pl.ANY) if at in apart else whole(shape)
            for at, (shape, dtype) in enumerate(outs)
        ],
        scratch_shapes=list(scratch)
        + [pltpu.VMEM(ins[at].shape, ins[at].dtype) for at in floats]
        + [pltpu.SemaphoreType.DMA((len(floats),))],
        compiler_params=params(),
        cost_estimate=pl.CostEstimate(flops=work * 1_000_000_000, bytes_accessed=1_000_000, transcendentals=0),
        name=name,
    )(*ins)


def neighbours(block):
    count = lax.axis_size("grp") * lax.axis_size("dev")
    up = [(i, i + 1) for i in range(count - 1)]
    down = [(i + 1, i) for i in range(count - 1)]
    return lax.ppermute(block, AXES, up), lax.ppermute(block, AXES, down)


def exchange(copies, axes):
    return lax.all_to_all(copies, axes, 0, 0, tiled=True)


def on_device(rhs, points, leaf_basis, transfer, leaf_skel, node_skel, near_ids, near_count, far_leaf, far_node):
    rhs = rhs.reshape(2 * LEAVES, 128)
    basis = jnp.swapaxes(leaf_basis, 1, 2)
    far_leaf = far_leaf.T
    I32 = jnp.int32
    vector = ((2 * LEAVES, 128), F32)
    distances = pltpu.VMEM((2, PTS, 256), F32)
    near_scratch = [pltpu.VMEM((DUMMY + 1, 8, PTS), F32), pltpu.VMEM((LEAVES, PTS, 128), F32), distances]
    far_scratch = [pltpu.VMEM((LEAVES, 8, 1024), F32)]
    (pay,) = call(
        prepare_kernel,
        "prepare",
        [((32, 72, 128), F32)],
        [rhs, basis, transfer, leaf_skel, node_skel],
        work=4,
    )
    group = exchange(pay, "dev")
    targets, centres, far_targets, far_centres, own_list, other_list, own_part, near_pay = call(
        own_first_kernel,
        "own_first",
        [
            ((LEAVES, PTS, 128), BF16),
            ((LEAVES, 8, 128), F32),
            ((LEAVES, RANK, 128), BF16),
            ((LEAVES, 8, 128), F32),
            ((LIST,), I32),
            ((LIST,), I32),
            vector,
            ((4, LEAVES * PTS), F32),
        ],
        [near_ids.T, near_count, points, rhs, leaf_skel],
        near_scratch,
        work=15,
    )
    prev_pay, next_pay = neighbours(near_pay)
    rows = jnp.swapaxes(group[:, 64:66], 0, 1).reshape(1, 64, 128)
    node_pay = jnp.broadcast_to(rows, (8, 64, 128))
    nodes = exchange(node_pay, "grp")
    near_part, far_part, stacks = call(
        middle_first_kernel,
        "middle_first",
        [vector, ((RANK, 128), F32), ((LEAVES, DEPTH, 1024), BF16)],
        [other_list, far_leaf, prev_pay, next_pay, targets, centres, own_part, far_targets, far_centres, group],
        near_scratch + far_scratch + [pltpu.VMEM((1024, 4, 128), F32), pltpu.VMEM((LEAVES, DEPTH, 1024), BF16), pltpu.SemaphoreType.DMA],
        work=20,
        apart=(2,),
        late=(7, 2, 3, 4, 5, 6),
    )
    field, pay = call(
        finish_first_kernel,
        "finish_first",
        [vector, ((32, 24, 128), F32)],
        [far_node, node_skel, nodes, near_part, far_part, rhs, basis, transfer],
        work=4,
        late=(3, 4, 5, 6, 7),
    )
    leaf_in = exchange(pay, "dev")
    own_part, near_field = call(
        own_next_kernel, "own_next", [vector, vector], [own_list, points, field, targets, centres], near_scratch, work=10
    )
    prev_val, next_val = neighbours(near_field)
    node_pay = jnp.broadcast_to(leaf_in[None, :, 16], (8, 32, 128))
    node_in = exchange(node_pay, "grp")
    near_part, far_part = call(
        middle_next_kernel,
        "middle_next",
        [vector, ((RANK, 128), F32)],
        [
            other_list, far_leaf, prev_pay, next_pay, prev_val, next_val, targets, centres, own_part, far_targets, stacks, leaf_in,
        ],
        near_scratch + far_scratch + [pltpu.VMEM((1024, 128), F32)],
        work=20,
        late=(6, 2, 3, 4, 5, 7, 8, 9, 10),
    )
    field2, pay = call(
        finish_next_kernel,
        "finish_next",
        [vector, ((256, 1, 128), F32)],
        [far_node, node_skel, nodes, node_in, near_part, far_part, rhs, field, basis, transfer],
        work=4,
        late=(4, 5, 6, 7, 8, 9),
    )
    last = exchange(pay, AXES)
    answer, residual = call(last_kernel, "last", [vector, vector], [rhs, field, field2, node_in, last], work=1)
    return answer.reshape(-1), residual.reshape(-1)


def solution(mesh):
    placed = (
        P(AXES),
        P(None, AXES),
        P(AXES, None, None),
        P(AXES, None, None),
        P(None, AXES),
        P(None, AXES),
        P(AXES, None),
        P(AXES),
        P(AXES, None),
        P(AXES, None),
    )
    return jax.shard_map(on_device, mesh=mesh, in_specs=placed, out_specs=(P(AXES), P(AXES)), check_vma=False)
```

```python
import math

import jax
import jax.numpy as jnp
from jax import lax
from jax.experimental import pallas as pl
from jax.experimental.pallas import tpu as pltpu
from jax.sharding import PartitionSpec as P

AXES = ("grp", "dev")
F32 = jnp.float32
BF16 = jnp.bfloat16
LN2 = math.log(2.0)
AMPLITUDE = 0.00390625
LENGTH = 0.25
NUGGET = 2.0
SCALE = math.sqrt(5.0) / LENGTH / 3.0
POWER = -3.0 / LN2
FACTOR = AMPLITUDE * 3.0
SMEM = pl.BlockSpec(memory_space=pltpu.SMEM)
LEAVES, PTS, RANK = 32, 256, 64
DEPTH = 48
DUMMY = 96
STEP = 4
LIST = 272


def params():
    return pltpu.CompilerParams(vmem_limit_bytes=64 * 1024 * 1024)


def split(x):
    hi = x.astype(BF16).astype(F32)
    rest = x - hi
    mid = rest.astype(BF16).astype(F32)
    return hi, mid, rest - mid


def rows_of(shape):
    return lax.broadcasted_iota(jnp.int32, shape, 0)


def lanes_of(shape):
    return lax.broadcasted_iota(jnp.int32, shape, 1)


def source_stack(coords):
    row = rows_of(coords.shape)
    norm = jnp.sum(coords * coords, axis=0, keepdims=True)
    full = jnp.where(row < 3, coords, jnp.where(row == 3, norm, jnp.where(row == 4, 1.0, 0.0)))
    hi, mid, low = split(full)
    return jnp.concatenate([hi, hi, mid, mid, hi, low], axis=0).astype(BF16)


def target_stack(coords):
    row = rows_of(coords.shape)
    norm = jnp.sum(coords * coords, axis=0, keepdims=True)
    full = jnp.where(row < 3, -2.0 * coords, jnp.where(row == 3, 1.0, jnp.where(row == 4, norm, 0.0)))
    hi, mid, low = split(full)
    rest = jnp.zeros((128 - DEPTH,) + hi.shape[1:], F32)
    return jnp.concatenate([hi, mid, hi, mid, low, hi, rest], axis=0).T.astype(BF16)


def squares(targets, sources):
    return jnp.dot(targets[:, :DEPTH], sources, preferred_element_type=F32)


def weighted(dist_sq, weights):
    dist_sq = jnp.maximum(dist_sq, 1e-30)
    dist = dist_sq * lax.rsqrt(dist_sq)
    value = (dist_sq + (dist + 1.0 / 3.0)) * jnp.exp2(dist * POWER) * weights
    total = value[:, :128]
    for at in range(128, value.shape[1], 128):
        total = total + value[:, at : at + 128]
    return total


def centred(tile, centre):
    shape = tile.shape
    return jnp.where(rows_of(shape) < 3, (tile - centre) * SCALE, 0.0)


def eight(tile):
    return jnp.concatenate([tile, jnp.zeros((8 - tile.shape[0], tile.shape[1]), F32)], axis=0)


def row_of(ref, l):
    pair = ref[pl.ds(2 * l, 2), :]
    return jnp.concatenate([pair[:1], pair[1:]], axis=1)


def pair_of(row):
    return jnp.concatenate([row[:, :128], row[:, 128:]], axis=0)


def project(carry, l, row, basis_ref, transfer_ref):
    weights, node = carry
    column = jnp.sum(basis_ref[l] * row, axis=1, keepdims=True)
    return jnp.where(lanes_of(weights.shape) == l, column, weights), node + transfer_ref[l] * column


def project_start():
    return jnp.zeros((RANK, 128), F32), jnp.zeros((RANK, RANK), F32)


def project_end(carry):
    rows = carry[0].T
    return jnp.concatenate([rows[:16], rows[16:32]], axis=1), jnp.sum(carry[1], axis=0, keepdims=True)


def prepare_kernel(rhs_ref, basis_ref, transfer_ref, leaf_skel_ref, node_skel_ref, pay_ref):
    weights, node = project_end(
        lax.fori_loop(
            0, LEAVES, lambda l, c: project(c, l, row_of(rhs_ref, l), basis_ref, transfer_ref), project_start(), unroll=8
        )
    )
    skel = leaf_skel_ref[...]
    tiles = []
    for m in range(16):
        low = skel[:, m * RANK : (m + 1) * RANK]
        high = skel[:, (m + 16) * RANK : (m + 17) * RANK]
        tiles.append(jnp.concatenate([low, high], axis=1))
        tiles.append(weights[m : m + 1])
    own = node_skel_ref[...]
    tiles.append(jnp.concatenate([own[:1], own[1:2]], axis=1))
    tiles.append(jnp.concatenate([own[2:3], node], axis=1))
    tiles.append(jnp.zeros((6, 128), F32))
    payload = jnp.concatenate(tiles, axis=0)
    for d in range(32):
        pay_ref[d] = payload


def near_parts(target_ref, centre_ref, source_ref, acc_ref, dist_ref):
    def distances(l, at, slot):
        centre = centre_ref[l]
        coords = centred(source_ref[at], jnp.concatenate([centre, centre], axis=1))
        dist_ref[slot] = squares(target_ref[l], source_stack(coords))

    def products(l, at, slot, first):
        weights = source_ref[at, 3:4, :] * FACTOR
        for row in range(0, PTS, 64):
            value = weighted(dist_ref[slot, row : row + 64, :], weights)
            if first:
                acc_ref[l, row : row + 64, :] = value
            else:
                acc_ref[l, row : row + 64, :] += value

    return distances, products


def near_self(target_ref, centre_ref, source_ref, acc_ref, dist_ref, beside, carry):
    distances, products = near_parts(target_ref, centre_ref, source_ref, acc_ref, dist_ref)

    def step(i, carry):
        for k in range(STEP):
            l = STEP * i + k
            later = jnp.minimum(l + 1, LEAVES - 1)
            distances(later, LEAVES + later, (k + 1) % 2)
            products(l, LEAVES + l, k % 2, True)
            carry = beside(l, carry)
        return carry

    distances(0, LEAVES, 0)
    return lax.fori_loop(0, LEAVES // STEP, step, carry)


def near_pairs(list_ref, target_ref, centre_ref, source_ref, acc_ref, dist_ref):
    distances, products = near_parts(target_ref, centre_ref, source_ref, acc_ref, dist_ref)

    def step(i, carry):
        codes = [list_ref[STEP * i + k + 1] for k in range(STEP + 1)]
        for k in range(STEP):
            distances(lax.shift_right_logical(codes[k + 1], 8), codes[k + 1] & 255, (k + 1) % 2)
            products(lax.shift_right_logical(codes[k], 8), codes[k] & 255, k % 2, False)
        return carry

    distances(lax.shift_right_logical(list_ref[1], 8), list_ref[1] & 255, 0)
    lax.fori_loop(0, (list_ref[0] + STEP - 1) // STEP, step, 0)


def clear(acc_ref):
    def leaf(l, carry):
        acc_ref[l] = jnp.zeros((PTS, 128), F32)
        return carry

    lax.fori_loop(0, LEAVES, leaf, 0, unroll=2)


def near_rows(acc_ref, out_ref, add_ref):
    def leaf(l, carry):
        parts = [jnp.sum(acc_ref[l, h * 128 : (h + 1) * 128, :].T, axis=0, keepdims=True) for h in range(2)]
        value = jnp.concatenate(parts, axis=0)
        if add_ref is not None:
            value = value + add_ref[pl.ds(2 * l, 2), :]
        out_ref[pl.ds(2 * l, 2), :] = value
        return carry

    lax.fori_loop(0, LEAVES, leaf, 0, unroll=4)


def fill(source_ref, at, block_ref):
    for l in range(LEAVES):
        source_ref[at + l] = eight(block_ref[:, l * PTS : (l + 1) * PTS])
    source_ref[DUMMY] = jnp.zeros((8, PTS), F32)


def set_values(source_ref, at, block_ref):
    for l in range(LEAVES):
        pair = block_ref[2 * l : 2 * l + 2, :]
        source_ref[at + l, 3:4, :] = jnp.concatenate([pair[:1], pair[1:]], axis=1)


def skel_target(tile):
    wide = jnp.concatenate([eight(tile), jnp.zeros((8, 64), F32)], axis=1)
    centre = jnp.broadcast_to(jnp.sum(wide, axis=1, keepdims=True) * (1.0 / RANK), wide.shape)
    return centre, target_stack(centred(wide, centre))[:RANK]


def own_first_kernel(
    ids_ref, count_ref, points_ref, rhs_ref, skel_ref, target_ref, centre_ref, far_target_ref, far_centre_ref, own_list_ref, other_list_ref, out_ref, near_ref,
    source_ref, acc_ref, dist_ref,
):
    here = lax.shift_right_logical(ids_ref[0, 0], 5)
    base = (here - 1) * LEAVES

    near_ref[:3, :] = points_ref[...]
    for half in range(2 * LEAVES):
        near_ref[3:4, half * 128 : (half + 1) * 128] = rhs_ref[half : half + 1, :]
    fill(source_ref, LEAVES, points_ref)
    set_values(source_ref, LEAVES, rhs_ref)

    def targets(l, carry):
        tile = source_ref[LEAVES + l]
        centre = jnp.broadcast_to(jnp.sum(tile, axis=1, keepdims=True) * (1.0 / PTS), (8, 128))
        centre_ref[l] = centre
        target_ref[l] = target_stack(centred(tile, jnp.concatenate([centre, centre], axis=1)))
        return carry

    lax.fori_loop(0, LEAVES, targets, 0, unroll=4)

    def slots(l, counts):
        own, other = counts
        used = count_ref[l]
        for j in range(1, 8):
            n = ids_ref[j, l]
            code = l * 256 + (n - base)
            own_list_ref[own] = code
            other_list_ref[other] = code
            is_used = (j < used).astype(jnp.int32)
            is_own = (lax.shift_right_logical(n, 5) == here).astype(jnp.int32) * is_used
            own, other = own + is_own, other + is_used - is_own
        return own, other

    one = jnp.int32(1)
    own, other = near_self(target_ref, centre_ref, source_ref, acc_ref, dist_ref, slots, (one, one))
    for k in range(STEP + 1):
        own_list_ref[own + k] = DUMMY
        other_list_ref[other + k] = DUMMY
    own_list_ref[0] = own - 1
    other_list_ref[0] = other - 1
    near_pairs(own_list_ref, target_ref, centre_ref, source_ref, acc_ref, dist_ref)
    near_rows(acc_ref, out_ref, None)
    for l in range(LEAVES):
        far_centre_ref[l], far_target_ref[l] = skel_target(skel_ref[:, l * RANK : (l + 1) * RANK])


def own_next_kernel(
    own_list_ref, points_ref, field_ref, target_ref, centre_ref, out_ref, field_out_ref, source_ref, acc_ref, dist_ref
):
    field_out_ref[...] = field_ref[...]
    fill(source_ref, LEAVES, points_ref)
    set_values(source_ref, LEAVES, field_ref)
    near_self(target_ref, centre_ref, source_ref, acc_ref, dist_ref, lambda l, carry: carry, 0)
    near_pairs(own_list_ref, target_ref, centre_ref, source_ref, acc_ref, dist_ref)
    near_rows(acc_ref, out_ref, None)


def swap(tile):
    return pltpu.roll(tile, 64, 1)


def low_lanes():
    return lanes_of((1, 128)) < 64


def spread(tile):
    other = swap(tile)
    return jnp.where(low_lanes(), tile, other), jnp.where(low_lanes(), other, tile)


def far_partners(far_leaf_ref, l, rows_at):
    for j in range(0, 16, 2):
        yield jnp.where(low_lanes(), rows_at(far_leaf_ref[j, l] & 1023), rows_at(far_leaf_ref[j + 1, l] & 1023))


def far_sums(stack_ref, weight_ref, target_ref, out_ref, dist_ref):
    def distances(l, slot):
        for c in range(4):
            dist_ref[slot, c * RANK : (c + 1) * RANK, :] = squares(target_ref[l], stack_ref[l, :, c * 256 : (c + 1) * 256])

    def products(l, slot):
        total = jnp.zeros((RANK, 128), F32)
        for c in range(4):
            weights = weight_ref[l, :1, c * 256 : (c + 1) * 256]
            total = total + weighted(dist_ref[slot, c * RANK : (c + 1) * RANK, :], weights)
        column = jnp.sum(total, axis=1, keepdims=True)
        out_ref[...] = jnp.where(lanes_of((RANK, 128)) == l, column, out_ref[...])

    def step(i, carry):
        for k in range(STEP):
            distances(jnp.minimum(STEP * i + k + 1, LEAVES - 1), (k + 1) % 2)
            products(STEP * i + k, k % 2)
        return carry

    out_ref[...] = jnp.zeros((RANK, 128), F32)
    distances(0, 0)
    lax.fori_loop(0, LEAVES // STEP, step, 0)


def middle_first_kernel(
    other_list_ref, far_leaf_ref, prev_ref, next_ref, target_ref, centre_ref, own_ref, far_target_ref, far_centre_ref, group_ref,
    near_ref, far_ref, stack_out_ref, source_ref, acc_ref, dist_ref, weight_ref, table_ref, stack_ref, stack_sem,
):
    def table(d, carry):
        for m in range(0, 16, 2):
            low, high = spread(group_ref[d, 4 * m : 4 * m + 8, :])
            for k in range(2):
                table_ref[d * LEAVES + m + k] = low[4 * k : 4 * k + 4]
                table_ref[d * LEAVES + m + k + 16] = high[4 * k : 4 * k + 4]
        return carry

    lax.fori_loop(0, 32, table, 0, unroll=4)

    def gather(l, carry):
        centre = far_centre_ref[l]
        rows = far_partners(far_leaf_ref, l, lambda p: table_ref[p])
        for j, tile in enumerate(rows):
            at = j * 128
            weight_ref[l, :1, at : at + 128] = tile[3:4] * FACTOR
            stack_ref[l, :, at : at + 128] = source_stack(centred(eight(tile), centre))
        return carry

    lax.fori_loop(0, LEAVES, gather, 0, unroll=4)
    stack_copy = pltpu.make_async_copy(stack_ref, stack_out_ref, stack_sem)
    stack_copy.start()
    far_target_ref.wait()
    far_sums(stack_ref, weight_ref, far_target_ref, far_ref, dist_ref)
    for operand in (prev_ref, next_ref, target_ref, centre_ref, own_ref):
        operand.wait()
    fill(source_ref, 0, prev_ref)
    fill(source_ref, 2 * LEAVES, next_ref)
    clear(acc_ref)
    near_pairs(other_list_ref, target_ref, centre_ref, source_ref, acc_ref, dist_ref)
    near_rows(acc_ref, near_ref, own_ref)
    stack_copy.wait()


def middle_next_kernel(
    other_list_ref, far_leaf_ref, prev_ref, next_ref, prev_val_ref, next_val_ref, target_ref, centre_ref, own_ref, far_target_ref,
    stack_ref, group_ref, near_ref, far_ref, source_ref, acc_ref, dist_ref, weight_ref, table_ref,
):
    for d in range(32):
        low, high = spread(group_ref[d, :16, :])
        table_ref[d * LEAVES : d * LEAVES + 16, :] = low
        table_ref[d * LEAVES + 16 : d * LEAVES + 32, :] = high

    def gather(l, carry):
        rows = far_partners(far_leaf_ref, l, lambda p: table_ref[pl.ds(p, 1), :])
        for j, tile in enumerate(rows):
            weight_ref[l, :1, j * 128 : (j + 1) * 128] = tile * FACTOR
        return carry

    lax.fori_loop(0, LEAVES, gather, 0, unroll=4)
    for operand in (prev_ref, next_ref, prev_val_ref, next_val_ref, target_ref, centre_ref, own_ref):
        operand.wait()
    fill(source_ref, 0, prev_ref)
    fill(source_ref, 2 * LEAVES, next_ref)
    set_values(source_ref, 0, prev_val_ref)
    set_values(source_ref, 2 * LEAVES, next_val_ref)
    clear(acc_ref)
    near_pairs(other_list_ref, target_ref, centre_ref, source_ref, acc_ref, dist_ref)
    near_rows(acc_ref, near_ref, own_ref)
    far_target_ref.wait()
    stack_ref.wait()
    far_sums(stack_ref, weight_ref, far_target_ref, far_ref, dist_ref)


def node_down(far_node_ref, node_skel_ref, nodes_ref, weight_ref):
    own = node_skel_ref[...]
    centre, target = skel_target(jnp.concatenate([own[:1], own[2:3], own[1:2]], axis=0))
    total = jnp.zeros((RANK, 128), F32)
    for at in range(0, 32, 4):
        coords, weights = [], []
        for j in (at, at + 2):
            tiles = []
            for p in (far_node_ref[0, j], far_node_ref[0, j + 1]):
                g, d = lax.shift_right_logical(p, 5), p & 31
                rows = [nodes_ref[g, pl.ds(d, 1), :], nodes_ref[g, pl.ds(d + 32, 1), :]]
                if weight_ref is not None:
                    rows.append(weight_ref[g, pl.ds(d, 1), :])
                tiles.append(jnp.concatenate(rows, axis=0))
            even = jnp.where(low_lanes(), tiles[0], swap(tiles[1]))
            odd = jnp.where(low_lanes(), swap(tiles[0]), tiles[1])
            coords.append(eight(jnp.concatenate([even[:2], odd[:2]], axis=0)))
            weights.append(odd[1:2] if weight_ref is None else even[2:3])
        wide = jnp.concatenate([centre, centre], axis=1)
        sources = source_stack(centred(jnp.concatenate(coords, axis=1), wide))
        dist_sq = squares(target, sources)
        total = total + weighted(dist_sq, jnp.concatenate(weights, axis=1) * FACTOR)
    return jnp.sum(total.T, axis=0, keepdims=True)


def leaf_row(l, down, far_ref, near_ref, basis_ref, transfer_ref):
    moved = transfer_ref[l] * down
    total = jnp.where(lanes_of((RANK, 128)) == l, far_ref[...], 0.0) + jnp.concatenate([moved, jnp.zeros((RANK, 64), F32)], axis=1)
    column = jnp.sum(total, axis=1, keepdims=True)
    return row_of(near_ref, l) + jnp.sum(basis_ref[l] * column, axis=0, keepdims=True)


def scalars(values):
    lane = lanes_of((1, 128))
    out = jnp.zeros((1, 128), F32)
    for at, value in enumerate(values):
        out = jnp.where(lane == 64 + at, value, out)
    return out


def dot(a, b):
    return jnp.sum(jnp.sum(a * b, axis=0, keepdims=True), axis=1, keepdims=True)


def finish_first_kernel(
    far_node_ref, node_skel_ref, nodes_ref, near_ref, far_ref, rhs_ref, basis_ref, transfer_ref, out_ref, pay_ref
):
    down = node_down(far_node_ref, node_skel_ref, nodes_ref, None)
    for operand in (near_ref, far_ref, rhs_ref, basis_ref, transfer_ref):
        operand.wait()

    def leaf(l, carry):
        row = leaf_row(l, down, far_ref, near_ref, basis_ref, transfer_ref)
        out_ref[pl.ds(2 * l, 2), :] = pair_of(row)
        return project(carry, l, row, basis_ref, transfer_ref)

    weights, node = project_end(lax.fori_loop(0, LEAVES, leaf, project_start(), unroll=8))
    rhs, image = rhs_ref[...], out_ref[...]
    extra = scalars([dot(rhs, rhs), dot(rhs, image)])
    last = jnp.where(lanes_of((1, 128)) < 64, jnp.concatenate([node, node], axis=1), extra)
    payload = jnp.concatenate([weights, last, jnp.zeros((7, 128), F32)], axis=0)
    for d in range(32):
        pay_ref[d] = payload


def lane(row, at):
    return jnp.sum(jnp.where(lanes_of(row.shape) == at, row, 0.0), axis=1, keepdims=True)


def first_scalars(node_ref):
    total = jnp.sum(jnp.sum(node_ref[...], axis=0), axis=0, keepdims=True)
    norm, inner = lane(total, 64), lane(total, 65)
    energy = NUGGET * norm + inner
    return norm, inner, energy, norm / energy


def finish_next_kernel(
    far_node_ref, node_skel_ref, nodes_ref, node_in_ref, near_ref, far_ref, rhs_ref, field_ref, basis_ref, transfer_ref, out_ref, pay_ref
):
    down = node_down(far_node_ref, node_skel_ref, nodes_ref, node_in_ref)
    for operand in (near_ref, far_ref, rhs_ref, field_ref, basis_ref, transfer_ref):
        operand.wait()

    def leaf(l, carry):
        out_ref[pl.ds(2 * l, 2), :] = pair_of(leaf_row(l, down, far_ref, near_ref, basis_ref, transfer_ref))
        return carry

    lax.fori_loop(0, LEAVES, leaf, 0, unroll=8)
    _, inner, energy, alpha = first_scalars(node_in_ref)
    rhs, field, field2 = rhs_ref[...], field_ref[...], out_ref[...]
    keep = inner / energy
    residual = keep * rhs - alpha * field
    image = NUGGET * residual + keep * field - alpha * field2
    base = NUGGET * rhs + field
    block = scalars([dot(residual, residual), dot(residual, image), dot(residual, base) + dot(rhs, image)])
    pay_ref[...] = jnp.broadcast_to(block[None], pay_ref.shape)


def last_kernel(rhs_ref, field_ref, field2_ref, node_ref, last_ref, solution_ref, residual_ref):
    norm, inner, energy, alpha = first_scalars(node_ref)
    total = jnp.sum(last_ref[...], axis=0)
    norm2 = lane(total, 64)
    beta = norm2 / norm
    alpha2 = norm2 / (lane(total, 65) + beta * lane(total, 66) + beta * beta * energy)
    rhs, field, field2 = rhs_ref[...], field_ref[...], field2_ref[...]
    keep = inner / energy
    residual = keep * rhs - alpha * field
    image = NUGGET * residual + keep * field - alpha * field2
    direction = residual + beta * rhs
    solution_ref[...] = alpha * rhs + alpha2 * direction
    residual_ref[...] = residual - alpha2 * (image + beta * (NUGGET * rhs + field))


class Operand:
    def __init__(self, ref, copy):
        self.ref, self.copy = ref, copy
        self.shape = ref.shape

    def wait(self):
        self.copy.wait()

    def __getitem__(self, at):
        return self.ref[at]


def call(kernel, name, outs, ins, scratch=(), work=0, late=(), apart=()):
    floats = [at for at, array in enumerate(ins) if array.dtype != jnp.int32]

    def whole(shape):
        return pl.BlockSpec(shape, lambda i: (0,) * len(shape))

    def body(*refs):
        operands = list(refs[: len(ins)])
        buffers, sems = refs[-1 - len(floats) : -1], refs[-1]
        for k, at in enumerate(floats):
            operands[at] = Operand(buffers[k], pltpu.make_async_copy(operands[at], buffers[k], sems.at[k]))
        for at in [at for at in floats if at not in late] + list(late):
            operands[at].copy.start()
        for at in floats:
            if at not in late:
                operands[at].wait()
        kernel(*operands, *refs[len(ins) : -1 - len(floats)])

    return pl.pallas_call(
        body,
        grid=(1,),
        out_shape=[jax.ShapeDtypeStruct(shape, dtype) for shape, dtype in outs],
        in_specs=[SMEM if array.dtype == jnp.int32 else pl.BlockSpec(memory_space=pl.ANY) for array in ins],
        out_specs=[
            SMEM if dtype == jnp.int32 else pl.BlockSpec(memory_space=pl.ANY) if at in apart else whole(shape)
            for at, (shape, dtype) in enumerate(outs)
        ],
        scratch_shapes=list(scratch)
        + [pltpu.VMEM(ins[at].shape, ins[at].dtype) for at in floats]
        + [pltpu.SemaphoreType.DMA((len(floats),))],
        compiler_params=params(),
        cost_estimate=pl.CostEstimate(flops=work * 1_000_000_000, bytes_accessed=1_000_000, transcendentals=0),
        name=name,
    )(*ins)


def neighbours(block):
    count = lax.axis_size("grp") * lax.axis_size("dev")
    up = [(i, i + 1) for i in range(count - 1)]
    down = [(i + 1, i) for i in range(count - 1)]
    return lax.ppermute(block, AXES, up), lax.ppermute(block, AXES, down)


def exchange(copies, axes):
    return lax.all_to_all(copies, axes, 0, 0, tiled=True)


def on_device(rhs, points, leaf_basis, transfer, leaf_skel, node_skel, near_ids, near_count, far_leaf, far_node):
    rhs = rhs.reshape(2 * LEAVES, 128)
    basis = jnp.swapaxes(leaf_basis, 1, 2)
    far_leaf = far_leaf.T
    I32 = jnp.int32
    vector = ((2 * LEAVES, 128), F32)
    distances = pltpu.VMEM((2, PTS, 256), F32)
    near_scratch = [pltpu.VMEM((DUMMY + 1, 8, PTS), F32), pltpu.VMEM((LEAVES, PTS, 128), F32), distances]
    far_scratch = [pltpu.VMEM((LEAVES, 8, 1024), F32)]
    (pay,) = call(
        prepare_kernel,
        "prepare",
        [((32, 72, 128), F32)],
        [rhs, basis, transfer, leaf_skel, node_skel],
        work=4,
    )
    group = exchange(pay, "dev")
    targets, centres, far_targets, far_centres, own_list, other_list, own_part, near_pay = call(
        own_first_kernel,
        "own_first",
        [
            ((LEAVES, PTS, 128), BF16),
            ((LEAVES, 8, 128), F32),
            ((LEAVES, RANK, 128), BF16),
            ((LEAVES, 8, 128), F32),
            ((LIST,), I32),
            ((LIST,), I32),
            vector,
            ((4, LEAVES * PTS), F32),
        ],
        [near_ids.T, near_count, points, rhs, leaf_skel],
        near_scratch,
        work=15,
    )
    prev_pay, next_pay = neighbours(near_pay)
    rows = jnp.swapaxes(group[:, 64:66], 0, 1).reshape(1, 64, 128)
    node_pay = jnp.broadcast_to(rows, (8, 64, 128))
    nodes = exchange(node_pay, "grp")
    near_part, far_part, stacks = call(
        middle_first_kernel,
        "middle_first",
        [vector, ((RANK, 128), F32), ((LEAVES, DEPTH, 1024), BF16)],
        [other_list, far_leaf, prev_pay, next_pay, targets, centres, own_part, far_targets, far_centres, group],
        near_scratch + far_scratch + [pltpu.VMEM((1024, 4, 128), F32), pltpu.VMEM((LEAVES, DEPTH, 1024), BF16), pltpu.SemaphoreType.DMA],
        work=20,
        apart=(2,),
        late=(7, 2, 3, 4, 5, 6),
    )
    field, pay = call(
        finish_first_kernel,
        "finish_first",
        [vector, ((32, 24, 128), F32)],
        [far_node, node_skel, nodes, near_part, far_part, rhs, basis, transfer],
        work=4,
        late=(3, 4, 5, 6, 7),
    )
    leaf_in = exchange(pay, "dev")
    own_part, near_field = call(
        own_next_kernel, "own_next", [vector, vector], [own_list, points, field, targets, centres], near_scratch, work=10
    )
    prev_val, next_val = neighbours(near_field)
    node_pay = jnp.broadcast_to(leaf_in[None, :, 16], (8, 32, 128))
    node_in = exchange(node_pay, "grp")
    near_part, far_part = call(
        middle_next_kernel,
        "middle_next",
        [vector, ((RANK, 128), F32)],
        [
            other_list, far_leaf, prev_pay, next_pay, prev_val, next_val, targets, centres, own_part, far_targets, stacks, leaf_in,
        ],
        near_scratch + far_scratch + [pltpu.VMEM((1024, 128), F32)],
        work=20,
        late=(6, 2, 3, 4, 5, 7, 8, 9, 10),
    )
    field2, pay = call(
        finish_next_kernel,
        "finish_next",
        [vector, ((256, 1, 128), F32)],
        [far_node, node_skel, nodes, node_in, near_part, far_part, rhs, field, basis, transfer],
        work=4,
        late=(4, 5, 6, 7, 8, 9),
    )
    last = exchange(pay, AXES)
    answer, residual = call(last_kernel, "last", [vector, vector], [rhs, field, field2, node_in, last], work=1)
    return answer.reshape(-1), residual.reshape(-1)


def solution(mesh):
    placed = (
        P(AXES),
        P(None, AXES),
        P(AXES, None, None),
        P(AXES, None, None),
        P(None, AXES),
        P(None, AXES),
        P(AXES, None),
        P(AXES),
        P(AXES, None),
        P(AXES, None),
    )
    return jax.shard_map(on_device, mesh=mesh, in_specs=placed, out_specs=(P(AXES), P(AXES)), check_vma=False)
```

```python
import math

import jax
import jax.numpy as jnp
from jax import lax
from jax.experimental import pallas as pl
from jax.experimental.pallas import tpu as pltpu
from jax.sharding import PartitionSpec as P

AXES = ("grp", "dev")
F32 = jnp.float32
BF16 = jnp.bfloat16
LN2 = math.log(2.0)
AMPLITUDE = 0.00390625
LENGTH = 0.25
NUGGET = 2.0
SCALE = math.sqrt(5.0) / LENGTH / 3.0
POWER = -3.0 / LN2
FACTOR = AMPLITUDE * 3.0
SMEM = pl.BlockSpec(memory_space=pltpu.SMEM)
LEAVES, PTS, RANK = 32, 256, 64
DEPTH = 48
DUMMY = 96
STEP = 4
LIST = 272
PARTS = 4


def params():
    return pltpu.CompilerParams(vmem_limit_bytes=64 * 1024 * 1024)


def split(x):
    hi = x.astype(BF16).astype(F32)
    rest = x - hi
    mid = rest.astype(BF16).astype(F32)
    return hi, mid, rest - mid


def rows_of(shape):
    return lax.broadcasted_iota(jnp.int32, shape, 0)


def lanes_of(shape):
    return lax.broadcasted_iota(jnp.int32, shape, 1)


def source_stack(coords):
    row = rows_of(coords.shape)
    norm = jnp.sum(coords * coords, axis=0, keepdims=True)
    full = jnp.where(row < 3, coords, jnp.where(row == 3, norm, jnp.where(row == 4, 1.0, 0.0)))
    hi, mid, low = split(full)
    return jnp.concatenate([hi, hi, mid, mid, hi, low], axis=0).astype(BF16)


def target_stack(coords):
    row = rows_of(coords.shape)
    norm = jnp.sum(coords * coords, axis=0, keepdims=True)
    full = jnp.where(row < 3, -2.0 * coords, jnp.where(row == 3, 1.0, jnp.where(row == 4, norm, 0.0)))
    hi, mid, low = split(full)
    rest = jnp.zeros((128 - DEPTH,) + hi.shape[1:], F32)
    return jnp.concatenate([hi, mid, hi, mid, low, hi, rest], axis=0).T.astype(BF16)


def squares(targets, sources):
    return jnp.dot(targets[:, :DEPTH], sources, preferred_element_type=F32)


def weighted(dist_sq, weights):
    dist_sq = jnp.maximum(dist_sq, 1e-30)
    dist = dist_sq * lax.rsqrt(dist_sq)
    value = (dist_sq + (dist + 1.0 / 3.0)) * jnp.exp2(dist * POWER) * weights
    total = value[:, :128]
    for at in range(128, value.shape[1], 128):
        total = total + value[:, at : at + 128]
    return total


def centred(tile, centre):
    shape = tile.shape
    return jnp.where(rows_of(shape) < 3, (tile - centre) * SCALE, 0.0)


def eight(tile):
    return jnp.concatenate([tile, jnp.zeros((8 - tile.shape[0], tile.shape[1]), F32)], axis=0)


def row_of(ref, l):
    pair = ref[pl.ds(2 * l, 2), :]
    return jnp.concatenate([pair[:1], pair[1:]], axis=1)


def pair_of(row):
    return jnp.concatenate([row[:, :128], row[:, 128:]], axis=0)


def project(carry, l, row, basis_ref, transfer_ref):
    weights, node = carry
    column = jnp.sum(basis_ref[l] * row, axis=1, keepdims=True)
    return jnp.where(lanes_of(weights.shape) == l, column, weights), node + transfer_ref[l] * column


def project_start():
    return jnp.zeros((RANK, 128), F32), jnp.zeros((RANK, RANK), F32)


def leaves_in_parts(operands, body, carry):
    count = LEAVES // PARTS
    for part in range(PARTS):
        for operand in operands:
            operand.wait(part)
        carry = lax.fori_loop(part * count, (part + 1) * count, body, carry, unroll=count)
    return carry


def project_end(carry):
    rows = carry[0].T
    return jnp.concatenate([rows[:16], rows[16:32]], axis=1), jnp.sum(carry[1], axis=0, keepdims=True)


def prepare_kernel(rhs_ref, basis_ref, transfer_ref, leaf_skel_ref, node_skel_ref, pay_ref):
    weights, node = project_end(
        leaves_in_parts(
            (basis_ref, transfer_ref), lambda l, c: project(c, l, row_of(rhs_ref, l), basis_ref, transfer_ref), project_start()
        )
    )
    skel = leaf_skel_ref[...]
    tiles = []
    for m in range(16):
        low = skel[:, m * RANK : (m + 1) * RANK]
        high = skel[:, (m + 16) * RANK : (m + 17) * RANK]
        tiles.append(jnp.concatenate([low, high], axis=1))
        tiles.append(weights[m : m + 1])
    own = node_skel_ref[...]
    tiles.append(jnp.concatenate([own[:1], own[1:2]], axis=1))
    tiles.append(jnp.concatenate([own[2:3], node], axis=1))
    tiles.append(jnp.zeros((6, 128), F32))
    payload = jnp.concatenate(tiles, axis=0)
    for d in range(32):
        pay_ref[d] = payload


def near_parts(target_ref, centre_ref, source_ref, acc_ref, dist_ref):
    def distances(l, at, slot):
        centre = centre_ref[l]
        coords = centred(source_ref[at], jnp.concatenate([centre, centre], axis=1))
        dist_ref[slot] = squares(target_ref[l], source_stack(coords))

    def products(l, at, slot, first):
        weights = source_ref[at, 3:4, :] * FACTOR
        for row in range(0, PTS, 64):
            value = weighted(dist_ref[slot, row : row + 64, :], weights)
            if first:
                acc_ref[l, row : row + 64, :] = value
            else:
                acc_ref[l, row : row + 64, :] += value

    return distances, products


def near_self(target_ref, centre_ref, source_ref, acc_ref, dist_ref, beside, carry):
    distances, products = near_parts(target_ref, centre_ref, source_ref, acc_ref, dist_ref)

    def step(i, carry):
        for k in range(STEP):
            l = STEP * i + k
            later = jnp.minimum(l + 1, LEAVES - 1)
            distances(later, LEAVES + later, (k + 1) % 2)
            products(l, LEAVES + l, k % 2, True)
            carry = beside(l, carry)
        return carry

    distances(0, LEAVES, 0)
    return lax.fori_loop(0, LEAVES // STEP, step, carry)


def near_pairs(list_ref, target_ref, centre_ref, source_ref, acc_ref, dist_ref):
    distances, products = near_parts(target_ref, centre_ref, source_ref, acc_ref, dist_ref)

    def step(i, carry):
        codes = [list_ref[STEP * i + k + 1] for k in range(STEP + 1)]
        for k in range(STEP):
            distances(lax.shift_right_logical(codes[k + 1], 8), codes[k + 1] & 255, (k + 1) % 2)
            products(lax.shift_right_logical(codes[k], 8), codes[k] & 255, k % 2, False)
        return carry

    distances(lax.shift_right_logical(list_ref[1], 8), list_ref[1] & 255, 0)
    lax.fori_loop(0, (list_ref[0] + STEP - 1) // STEP, step, 0)


def clear(acc_ref):
    def leaf(l, carry):
        acc_ref[l] = jnp.zeros((PTS, 128), F32)
        return carry

    lax.fori_loop(0, LEAVES, leaf, 0, unroll=2)


def near_rows(acc_ref, out_ref, add_ref):
    def leaf(l, carry):
        parts = [jnp.sum(acc_ref[l, h * 128 : (h + 1) * 128, :].T, axis=0, keepdims=True) for h in range(2)]
        value = jnp.concatenate(parts, axis=0)
        if add_ref is not None:
            value = value + add_ref[pl.ds(2 * l, 2), :]
        out_ref[pl.ds(2 * l, 2), :] = value
        return carry

    lax.fori_loop(0, LEAVES, leaf, 0, unroll=4)


def fill(source_ref, at, block_ref):
    for l in range(LEAVES):
        source_ref[at + l] = eight(block_ref[:, l * PTS : (l + 1) * PTS])
    source_ref[DUMMY] = jnp.zeros((8, PTS), F32)


def set_values(source_ref, at, block_ref):
    for l in range(LEAVES):
        pair = block_ref[2 * l : 2 * l + 2, :]
        source_ref[at + l, 3:4, :] = jnp.concatenate([pair[:1], pair[1:]], axis=1)


def skel_target(tile):
    wide = jnp.concatenate([eight(tile), jnp.zeros((8, 64), F32)], axis=1)
    centre = jnp.broadcast_to(jnp.sum(wide, axis=1, keepdims=True) * (1.0 / RANK), wide.shape)
    return centre, target_stack(centred(wide, centre))[:RANK]


def own_first_kernel(
    ids_ref, count_ref, points_ref, rhs_ref, skel_ref, target_out_ref, centre_ref, far_target_out_ref, far_centre_ref, own_list_ref, other_list_ref, out_ref,
    near_ref, source_ref, acc_ref, dist_ref, target_ref, far_target_ref, out_sems,
):
    here = lax.shift_right_logical(ids_ref[0, 0], 5)
    base = (here - 1) * LEAVES

    near_ref[:3, :] = points_ref[...]
    for half in range(2 * LEAVES):
        near_ref[3:4, half * 128 : (half + 1) * 128] = rhs_ref[half : half + 1, :]
    fill(source_ref, LEAVES, points_ref)
    set_values(source_ref, LEAVES, rhs_ref)

    def targets(l, carry):
        tile = source_ref[LEAVES + l]
        centre = jnp.broadcast_to(jnp.sum(tile, axis=1, keepdims=True) * (1.0 / PTS), (8, 128))
        centre_ref[l] = centre
        target_ref[l] = target_stack(centred(tile, jnp.concatenate([centre, centre], axis=1)))
        return carry

    lax.fori_loop(0, LEAVES, targets, 0, unroll=4)
    for l in range(LEAVES):
        far_centre_ref[l], far_target_ref[l] = skel_target(skel_ref[:, l * RANK : (l + 1) * RANK])
    copies = [
        pltpu.make_async_copy(target_ref, target_out_ref, out_sems.at[0]),
        pltpu.make_async_copy(far_target_ref, far_target_out_ref, out_sems.at[1]),
    ]
    for copy in copies:
        copy.start()

    def slots(l, counts):
        own, other = counts
        used = count_ref[l]
        for j in range(1, 8):
            n = ids_ref[j, l]
            code = l * 256 + (n - base)
            own_list_ref[own] = code
            other_list_ref[other] = code
            is_used = (j < used).astype(jnp.int32)
            is_own = (lax.shift_right_logical(n, 5) == here).astype(jnp.int32) * is_used
            own, other = own + is_own, other + is_used - is_own
        return own, other

    one = jnp.int32(1)
    own, other = near_self(target_ref, centre_ref, source_ref, acc_ref, dist_ref, slots, (one, one))
    for k in range(STEP + 1):
        own_list_ref[own + k] = DUMMY
        other_list_ref[other + k] = DUMMY
    own_list_ref[0] = own - 1
    other_list_ref[0] = other - 1
    near_pairs(own_list_ref, target_ref, centre_ref, source_ref, acc_ref, dist_ref)
    near_rows(acc_ref, out_ref, None)
    for copy in copies:
        copy.wait()


def own_next_kernel(
    own_list_ref, points_ref, field_ref, target_ref, centre_ref, out_ref, field_out_ref, source_ref, acc_ref, dist_ref
):
    field_out_ref[...] = field_ref[...]
    fill(source_ref, LEAVES, points_ref)
    set_values(source_ref, LEAVES, field_ref)
    near_self(target_ref, centre_ref, source_ref, acc_ref, dist_ref, lambda l, carry: carry, 0)
    near_pairs(own_list_ref, target_ref, centre_ref, source_ref, acc_ref, dist_ref)
    near_rows(acc_ref, out_ref, None)


def swap(tile):
    return pltpu.roll(tile, 64, 1)


def low_lanes():
    return lanes_of((1, 128)) < 64


def spread(tile):
    other = swap(tile)
    return jnp.where(low_lanes(), tile, other), jnp.where(low_lanes(), other, tile)


def far_partners(far_leaf_ref, l, rows_at):
    for j in range(0, 16, 2):
        yield jnp.where(low_lanes(), rows_at(far_leaf_ref[j, l] & 1023), rows_at(far_leaf_ref[j + 1, l] & 1023))


def far_sums(stack_ref, weight_ref, target_ref, out_ref, dist_ref):
    def distances(l, slot):
        for c in range(4):
            dist_ref[slot, c * RANK : (c + 1) * RANK, :] = squares(target_ref[l], stack_ref[l, :, c * 256 : (c + 1) * 256])

    def products(l, slot):
        total = jnp.zeros((RANK, 128), F32)
        for c in range(4):
            weights = weight_ref[l, :1, c * 256 : (c + 1) * 256]
            total = total + weighted(dist_ref[slot, c * RANK : (c + 1) * RANK, :], weights)
        column = jnp.sum(total, axis=1, keepdims=True)
        out_ref[...] = jnp.where(lanes_of((RANK, 128)) == l, column, out_ref[...])

    def step(i, carry):
        for k in range(STEP):
            distances(jnp.minimum(STEP * i + k + 1, LEAVES - 1), (k + 1) % 2)
            products(STEP * i + k, k % 2)
        return carry

    out_ref[...] = jnp.zeros((RANK, 128), F32)
    distances(0, 0)
    lax.fori_loop(0, LEAVES // STEP, step, 0)


def middle_first_kernel(
    other_list_ref, far_leaf_ref, prev_ref, next_ref, target_ref, centre_ref, own_ref, far_target_ref, far_centre_ref, group_ref,
    near_ref, far_ref, stack_out_ref, source_ref, acc_ref, dist_ref, weight_ref, table_ref, stack_ref, stack_sem,
):
    def table(d, carry):
        for m in range(0, 16, 2):
            low, high = spread(group_ref[d, 4 * m : 4 * m + 8, :])
            for k in range(2):
                table_ref[d * LEAVES + m + k] = low[4 * k : 4 * k + 4]
                table_ref[d * LEAVES + m + k + 16] = high[4 * k : 4 * k + 4]
        return carry

    lax.fori_loop(0, 32, table, 0, unroll=4)

    def gather(l, carry):
        centre = far_centre_ref[l]
        rows = far_partners(far_leaf_ref, l, lambda p: table_ref[p])
        for j, tile in enumerate(rows):
            at = j * 128
            weight_ref[l, :1, at : at + 128] = tile[3:4] * FACTOR
            stack_ref[l, :, at : at + 128] = source_stack(centred(eight(tile), centre))
        return carry

    lax.fori_loop(0, LEAVES, gather, 0, unroll=4)
    stack_copy = pltpu.make_async_copy(stack_ref, stack_out_ref, stack_sem)
    stack_copy.start()
    far_target_ref.wait()
    far_sums(stack_ref, weight_ref, far_target_ref, far_ref, dist_ref)
    for operand in (prev_ref, next_ref, target_ref, centre_ref, own_ref):
        operand.wait()
    fill(source_ref, 0, prev_ref)
    fill(source_ref, 2 * LEAVES, next_ref)
    clear(acc_ref)
    near_pairs(other_list_ref, target_ref, centre_ref, source_ref, acc_ref, dist_ref)
    near_rows(acc_ref, near_ref, own_ref)
    stack_copy.wait()


def middle_next_kernel(
    other_list_ref, far_leaf_ref, prev_ref, next_ref, prev_val_ref, next_val_ref, target_ref, centre_ref, own_ref, far_target_ref,
    stack_ref, group_ref, near_ref, far_ref, source_ref, acc_ref, dist_ref, weight_ref, table_ref,
):
    for d in range(32):
        low, high = spread(group_ref[d, :16, :])
        table_ref[d * LEAVES : d * LEAVES + 16, :] = low
        table_ref[d * LEAVES + 16 : d * LEAVES + 32, :] = high

    def gather(l, carry):
        rows = far_partners(far_leaf_ref, l, lambda p: table_ref[pl.ds(p, 1), :])
        for j, tile in enumerate(rows):
            weight_ref[l, :1, j * 128 : (j + 1) * 128] = tile * FACTOR
        return carry

    lax.fori_loop(0, LEAVES, gather, 0, unroll=4)
    for operand in (prev_ref, next_ref, prev_val_ref, next_val_ref, target_ref, centre_ref, own_ref):
        operand.wait()
    fill(source_ref, 0, prev_ref)
    fill(source_ref, 2 * LEAVES, next_ref)
    set_values(source_ref, 0, prev_val_ref)
    set_values(source_ref, 2 * LEAVES, next_val_ref)
    clear(acc_ref)
    near_pairs(other_list_ref, target_ref, centre_ref, source_ref, acc_ref, dist_ref)
    near_rows(acc_ref, near_ref, own_ref)
    far_target_ref.wait()
    stack_ref.wait()
    far_sums(stack_ref, weight_ref, far_target_ref, far_ref, dist_ref)


def node_down(far_node_ref, node_skel_ref, nodes_ref, weight_ref):
    own = node_skel_ref[...]
    centre, target = skel_target(jnp.concatenate([own[:1], own[2:3], own[1:2]], axis=0))
    total = jnp.zeros((RANK, 128), F32)
    for at in range(0, 32, 4):
        coords, weights = [], []
        for j in (at, at + 2):
            tiles = []
            for p in (far_node_ref[0, j], far_node_ref[0, j + 1]):
                g, d = lax.shift_right_logical(p, 5), p & 31
                rows = [nodes_ref[g, pl.ds(d, 1), :], nodes_ref[g, pl.ds(d + 32, 1), :]]
                if weight_ref is not None:
                    rows.append(weight_ref[g, pl.ds(d, 1), :])
                tiles.append(jnp.concatenate(rows, axis=0))
            even = jnp.where(low_lanes(), tiles[0], swap(tiles[1]))
            odd = jnp.where(low_lanes(), swap(tiles[0]), tiles[1])
            coords.append(eight(jnp.concatenate([even[:2], odd[:2]], axis=0)))
            weights.append(odd[1:2] if weight_ref is None else even[2:3])
        wide = jnp.concatenate([centre, centre], axis=1)
        sources = source_stack(centred(jnp.concatenate(coords, axis=1), wide))
        dist_sq = squares(target, sources)
        total = total + weighted(dist_sq, jnp.concatenate(weights, axis=1) * FACTOR)
    return jnp.sum(total.T, axis=0, keepdims=True)


def leaf_row(l, down, far_ref, near_ref, basis_ref, transfer_ref):
    moved = transfer_ref[l] * down
    total = jnp.where(lanes_of((RANK, 128)) == l, far_ref[...], 0.0) + jnp.concatenate([moved, jnp.zeros((RANK, 64), F32)], axis=1)
    column = jnp.sum(total, axis=1, keepdims=True)
    return row_of(near_ref, l) + jnp.sum(basis_ref[l] * column, axis=0, keepdims=True)


def scalars(values):
    lane = lanes_of((1, 128))
    out = jnp.zeros((1, 128), F32)
    for at, value in enumerate(values):
        out = jnp.where(lane == 64 + at, value, out)
    return out


def dot(a, b):
    return jnp.sum(jnp.sum(a * b, axis=0, keepdims=True), axis=1, keepdims=True)


def finish_first_kernel(
    far_node_ref, node_skel_ref, nodes_ref, near_ref, far_ref, rhs_ref, basis_ref, transfer_ref, out_ref, pay_ref
):
    down = node_down(far_node_ref, node_skel_ref, nodes_ref, None)
    for operand in (near_ref, far_ref, rhs_ref):
        operand.wait()

    def leaf(l, carry):
        row = leaf_row(l, down, far_ref, near_ref, basis_ref, transfer_ref)
        out_ref[pl.ds(2 * l, 2), :] = pair_of(row)
        return project(carry, l, row, basis_ref, transfer_ref)

    weights, node = project_end(leaves_in_parts((basis_ref, transfer_ref), leaf, project_start()))
    rhs, image = rhs_ref[...], out_ref[...]
    extra = scalars([dot(rhs, rhs), dot(rhs, image)])
    last = jnp.where(lanes_of((1, 128)) < 64, jnp.concatenate([node, node], axis=1), extra)
    payload = jnp.concatenate([weights, last, jnp.zeros((7, 128), F32)], axis=0)
    for d in range(32):
        pay_ref[d] = payload


def lane(row, at):
    return jnp.sum(jnp.where(lanes_of(row.shape) == at, row, 0.0), axis=1, keepdims=True)


def first_scalars(node_ref):
    total = jnp.sum(jnp.sum(node_ref[...], axis=0), axis=0, keepdims=True)
    norm, inner = lane(total, 64), lane(total, 65)
    energy = NUGGET * norm + inner
    return norm, inner, energy, norm / energy


def finish_next_kernel(
    far_node_ref, node_skel_ref, nodes_ref, node_in_ref, near_ref, far_ref, rhs_ref, field_ref, basis_ref, transfer_ref, out_ref, pay_ref
):
    down = node_down(far_node_ref, node_skel_ref, nodes_ref, node_in_ref)
    for operand in (near_ref, far_ref, rhs_ref, field_ref):
        operand.wait()

    def leaf(l, carry):
        out_ref[pl.ds(2 * l, 2), :] = pair_of(leaf_row(l, down, far_ref, near_ref, basis_ref, transfer_ref))
        return carry

    leaves_in_parts((basis_ref, transfer_ref), leaf, 0)
    _, inner, energy, alpha = first_scalars(node_in_ref)
    rhs, field, field2 = rhs_ref[...], field_ref[...], out_ref[...]
    keep = inner / energy
    residual = keep * rhs - alpha * field
    image = NUGGET * residual + keep * field - alpha * field2
    base = NUGGET * rhs + field
    block = scalars([dot(residual, residual), dot(residual, image), dot(residual, base) + dot(rhs, image)])
    pay_ref[...] = jnp.broadcast_to(block[None], pay_ref.shape)


def last_kernel(rhs_ref, field_ref, field2_ref, node_ref, last_ref, solution_ref, residual_ref):
    norm, inner, energy, alpha = first_scalars(node_ref)
    total = jnp.sum(last_ref[...], axis=0)
    norm2 = lane(total, 64)
    beta = norm2 / norm
    alpha2 = norm2 / (lane(total, 65) + beta * lane(total, 66) + beta * beta * energy)
    rhs, field, field2 = rhs_ref[...], field_ref[...], field2_ref[...]
    keep = inner / energy
    residual = keep * rhs - alpha * field
    image = NUGGET * residual + keep * field - alpha * field2
    direction = residual + beta * rhs
    solution_ref[...] = alpha * rhs + alpha2 * direction
    residual_ref[...] = residual - alpha2 * (image + beta * (NUGGET * rhs + field))


class Operand:
    def __init__(self, source, ref, sems, parts):
        self.ref, self.shape = ref, ref.shape
        if parts == 1:
            self.copies = [pltpu.make_async_copy(source, ref, sems.at[0])]
        else:
            spans = [pl.ds(part * (ref.shape[0] // parts), ref.shape[0] // parts) for part in range(parts)]
            self.copies = [pltpu.make_async_copy(source.at[span], ref.at[span], sems.at[n]) for n, span in enumerate(spans)]

    def wait(self, part=0):
        self.copies[part].wait()

    def __getitem__(self, at):
        return self.ref[at]


def call(kernel, name, outs, ins, scratch=(), work=0, late=(), apart=(), split_up=()):
    floats = [at for at, array in enumerate(ins) if array.dtype != jnp.int32]

    def whole(shape):
        return pl.BlockSpec(shape, lambda i: (0,) * len(shape))

    def body(*refs):
        operands = list(refs[: len(ins)])
        buffers, sems = refs[-1 - len(floats) : -1], refs[-1]
        for k, at in enumerate(floats):
            operands[at] = Operand(operands[at], buffers[k], sems.at[k], PARTS if at in split_up else 1)
        for at in [at for at in floats if at not in late] + [at for at in late if at not in split_up]:
            operands[at].copies[0].start()
        for part in range(PARTS if split_up else 0):
            for at in split_up:
                operands[at].copies[part].start()
        for at in floats:
            if at not in late:
                operands[at].wait()
        kernel(*operands, *refs[len(ins) : -1 - len(floats)])

    return pl.pallas_call(
        body,
        grid=(1,),
        out_shape=[jax.ShapeDtypeStruct(shape, dtype) for shape, dtype in outs],
        in_specs=[SMEM if array.dtype == jnp.int32 else pl.BlockSpec(memory_space=pl.ANY) for array in ins],
        out_specs=[
            SMEM if dtype == jnp.int32 else pl.BlockSpec(memory_space=pl.ANY) if at in apart else whole(shape)
            for at, (shape, dtype) in enumerate(outs)
        ],
        scratch_shapes=list(scratch)
        + [pltpu.VMEM(ins[at].shape, ins[at].dtype) for at in floats]
        + [pltpu.SemaphoreType.DMA((len(floats), PARTS))],
        compiler_params=params(),
        cost_estimate=pl.CostEstimate(flops=work * 1_000_000_000, bytes_accessed=1_000_000, transcendentals=0),
        name=name,
    )(*ins)


def neighbours(block):
    count = lax.axis_size("grp") * lax.axis_size("dev")
    up = [(i, i + 1) for i in range(count - 1)]
    down = [(i + 1, i) for i in range(count - 1)]
    return lax.ppermute(block, AXES, up), lax.ppermute(block, AXES, down)


def exchange(copies, axes):
    return lax.all_to_all(copies, axes, 0, 0, tiled=True)


def on_device(rhs, points, leaf_basis, transfer, leaf_skel, node_skel, near_ids, near_count, far_leaf, far_node):
    rhs = rhs.reshape(2 * LEAVES, 128)
    basis = jnp.swapaxes(leaf_basis, 1, 2)
    far_leaf = far_leaf.T
    I32 = jnp.int32
    vector = ((2 * LEAVES, 128), F32)
    distances = pltpu.VMEM((2, PTS, 256), F32)
    near_scratch = [pltpu.VMEM((DUMMY + 1, 8, PTS), F32), pltpu.VMEM((LEAVES, PTS, 128), F32), distances]
    far_scratch = [pltpu.VMEM((LEAVES, 8, 1024), F32)]
    (pay,) = call(
        prepare_kernel,
        "prepare",
        [((32, 72, 128), F32)],
        [rhs, basis, transfer, leaf_skel, node_skel],
        work=4,
        late=(1, 2),
        split_up=(1, 2),
    )
    group = exchange(pay, "dev")
    targets, centres, far_targets, far_centres, own_list, other_list, own_part, near_pay = call(
        own_first_kernel,
        "own_first",
        [
            ((LEAVES, PTS, 128), BF16),
            ((LEAVES, 8, 128), F32),
            ((LEAVES, RANK, 128), BF16),
            ((LEAVES, 8, 128), F32),
            ((LIST,), I32),
            ((LIST,), I32),
            vector,
            ((4, LEAVES * PTS), F32),
        ],
        [near_ids.T, near_count, points, rhs, leaf_skel],
        near_scratch
        + [pltpu.VMEM((LEAVES, PTS, 128), BF16), pltpu.VMEM((LEAVES, RANK, 128), BF16), pltpu.SemaphoreType.DMA((2,))],
        work=15,
        apart=(0, 2),
    )
    prev_pay, next_pay = neighbours(near_pay)
    rows = jnp.swapaxes(group[:, 64:66], 0, 1).reshape(1, 64, 128)
    node_pay = jnp.broadcast_to(rows, (8, 64, 128))
    nodes = exchange(node_pay, "grp")
    near_part, far_part, stacks = call(
        middle_first_kernel,
        "middle_first",
        [vector, ((RANK, 128), F32), ((LEAVES, DEPTH, 1024), BF16)],
        [other_list, far_leaf, prev_pay, next_pay, targets, centres, own_part, far_targets, far_centres, group],
        near_scratch + far_scratch + [pltpu.VMEM((1024, 4, 128), F32), pltpu.VMEM((LEAVES, DEPTH, 1024), BF16), pltpu.SemaphoreType.DMA],
        work=20,
        apart=(2,),
        late=(7, 2, 3, 4, 5, 6),
    )
    field, pay = call(
        finish_first_kernel,
        "finish_first",
        [vector, ((32, 24, 128), F32)],
        [far_node, node_skel, nodes, near_part, far_part, rhs, basis, transfer],
        work=4,
        late=(3, 4, 5, 6, 7),
        split_up=(6, 7),
    )
    leaf_in = exchange(pay, "dev")
    own_part, near_field = call(
        own_next_kernel, "own_next", [vector, vector], [own_list, points, field, targets, centres], near_scratch, work=10
    )
    prev_val, next_val = neighbours(near_field)
    node_pay = jnp.broadcast_to(leaf_in[None, :, 16], (8, 32, 128))
    node_in = exchange(node_pay, "grp")
    near_part, far_part = call(
        middle_next_kernel,
        "middle_next",
        [vector, ((RANK, 128), F32)],
        [
            other_list, far_leaf, prev_pay, next_pay, prev_val, next_val, targets, centres, own_part, far_targets, stacks, leaf_in,
        ],
        near_scratch + far_scratch + [pltpu.VMEM((1024, 128), F32)],
        work=20,
        late=(6, 2, 3, 4, 5, 7, 8, 9, 10),
    )
    field2, pay = call(
        finish_next_kernel,
        "finish_next",
        [vector, ((256, 1, 128), F32)],
        [far_node, node_skel, nodes, node_in, near_part, far_part, rhs, field, basis, transfer],
        work=4,
        late=(4, 5, 6, 7, 8, 9),
        split_up=(8, 9),
    )
    last = exchange(pay, AXES)
    answer, residual = call(last_kernel, "last", [vector, vector], [rhs, field, field2, node_in, last], work=1)
    return answer.reshape(-1), residual.reshape(-1)


def solution(mesh):
    placed = (
        P(AXES),
        P(None, AXES),
        P(AXES, None, None),
        P(AXES, None, None),
        P(None, AXES),
        P(None, AXES),
        P(AXES, None),
        P(AXES),
        P(AXES, None),
        P(AXES, None),
    )
    return jax.shard_map(on_device, mesh=mesh, in_specs=placed, out_specs=(P(AXES), P(AXES)), check_vma=False)
```

```python
import math

import jax
import jax.numpy as jnp
from jax import lax
from jax.experimental import pallas as pl
from jax.experimental.pallas import tpu as pltpu
from jax.sharding import PartitionSpec as P

AXES = ("grp", "dev")
F32 = jnp.float32
BF16 = jnp.bfloat16
LN2 = math.log(2.0)
AMPLITUDE = 0.00390625
LENGTH = 0.25
NUGGET = 2.0
SCALE = math.sqrt(5.0) / LENGTH / 3.0
POWER = -3.0 / LN2
FACTOR = AMPLITUDE * 3.0
SMEM = pl.BlockSpec(memory_space=pltpu.SMEM)
LEAVES, PTS, RANK = 32, 256, 64
DEPTH = 48
DUMMY = 96
STEP = 4
LIST = 272
PARTS = 4


def params():
    return pltpu.CompilerParams(vmem_limit_bytes=64 * 1024 * 1024)


def split(x):
    hi = x.astype(BF16).astype(F32)
    rest = x - hi
    mid = rest.astype(BF16).astype(F32)
    return hi, mid, rest - mid


def rows_of(shape):
    return lax.broadcasted_iota(jnp.int32, shape, 0)


def lanes_of(shape):
    return lax.broadcasted_iota(jnp.int32, shape, 1)


def source_stack(coords):
    row = rows_of(coords.shape)
    norm = jnp.sum(coords * coords, axis=0, keepdims=True)
    full = jnp.where(row < 3, coords, jnp.where(row == 3, norm, jnp.where(row == 4, 1.0, 0.0)))
    hi, mid, low = split(full)
    return jnp.concatenate([hi, hi, mid, mid, hi, low], axis=0).astype(BF16)


def target_stack(coords):
    row = rows_of(coords.shape)
    norm = jnp.sum(coords * coords, axis=0, keepdims=True)
    full = jnp.where(row < 3, -2.0 * coords, jnp.where(row == 3, 1.0, jnp.where(row == 4, norm, 0.0)))
    hi, mid, low = split(full)
    rest = jnp.zeros((128 - DEPTH,) + hi.shape[1:], F32)
    return jnp.concatenate([hi, mid, hi, mid, low, hi, rest], axis=0).T.astype(BF16)


def squares(targets, sources):
    return jnp.dot(targets[:, :DEPTH], sources, preferred_element_type=F32)


def weighted(dist_sq, weights):
    dist_sq = jnp.maximum(dist_sq, 1e-30)
    dist = dist_sq * lax.rsqrt(dist_sq)
    value = (dist_sq + (dist + 1.0 / 3.0)) * jnp.exp2(dist * POWER) * weights
    total = value[:, :128]
    for at in range(128, value.shape[1], 128):
        total = total + value[:, at : at + 128]
    return total


def centred(tile, centre):
    shape = tile.shape
    return jnp.where(rows_of(shape) < 3, (tile - centre) * SCALE, 0.0)


def eight(tile):
    return jnp.concatenate([tile, jnp.zeros((8 - tile.shape[0], tile.shape[1]), F32)], axis=0)


def row_of(ref, l):
    pair = ref[pl.ds(2 * l, 2), :]
    return jnp.concatenate([pair[:1], pair[1:]], axis=1)


def pair_of(row):
    return jnp.concatenate([row[:, :128], row[:, 128:]], axis=0)


def project(carry, l, row, basis_ref, transfer_ref):
    weights, node = carry
    column = jnp.sum(basis_ref[l] * row, axis=1, keepdims=True)
    return jnp.where(lanes_of(weights.shape) == l, column, weights), node + transfer_ref[l] * column


def project_start():
    return jnp.zeros((RANK, 128), F32), jnp.zeros((RANK, RANK), F32)


def leaves_in_parts(operands, body, carry):
    count = LEAVES // PARTS
    for part in range(PARTS):
        for operand in operands:
            operand.wait(part)
        carry = lax.fori_loop(part * count, (part + 1) * count, body, carry, unroll=count)
    return carry


def project_end(carry):
    rows = carry[0].T
    return jnp.concatenate([rows[:16], rows[16:32]], axis=1), jnp.sum(carry[1], axis=0, keepdims=True)


def prepare_kernel(rhs_ref, basis_ref, transfer_ref, leaf_skel_ref, node_skel_ref, pay_ref):
    weights, node = project_end(
        leaves_in_parts(
            (basis_ref, transfer_ref), lambda l, c: project(c, l, row_of(rhs_ref, l), basis_ref, transfer_ref), project_start()
        )
    )
    skel = leaf_skel_ref[...]
    tiles = []
    for m in range(16):
        low = skel[:, m * RANK : (m + 1) * RANK]
        high = skel[:, (m + 16) * RANK : (m + 17) * RANK]
        tiles.append(jnp.concatenate([low, high], axis=1))
        tiles.append(weights[m : m + 1])
    own = node_skel_ref[...]
    tiles.append(jnp.concatenate([own[:1], own[1:2]], axis=1))
    tiles.append(jnp.concatenate([own[2:3], node], axis=1))
    tiles.append(jnp.zeros((6, 128), F32))
    payload = jnp.concatenate(tiles, axis=0)
    for d in range(32):
        pay_ref[d] = payload


def near_parts(target_ref, centre_ref, source_ref, acc_ref, dist_ref):
    def distances(l, at, slot):
        centre = centre_ref[l]
        coords = centred(source_ref[at], jnp.concatenate([centre, centre], axis=1))
        dist_ref[slot] = squares(target_ref[l], source_stack(coords))

    def products(l, at, slot, first):
        weights = source_ref[at, 3:4, :] * FACTOR
        for row in range(0, PTS, 64):
            value = weighted(dist_ref[slot, row : row + 64, :], weights)
            if first:
                acc_ref[l, row : row + 64, :] = value
            else:
                acc_ref[l, row : row + 64, :] += value

    return distances, products


def near_self(target_ref, centre_ref, source_ref, acc_ref, dist_ref, beside, carry):
    distances, products = near_parts(target_ref, centre_ref, source_ref, acc_ref, dist_ref)

    def step(i, carry):
        for k in range(STEP):
            l = STEP * i + k
            later = jnp.minimum(l + 1, LEAVES - 1)
            distances(later, LEAVES + later, (k + 1) % 2)
            products(l, LEAVES + l, k % 2, True)
            carry = beside(l, carry)
        return carry

    distances(0, LEAVES, 0)
    return lax.fori_loop(0, LEAVES // STEP, step, carry)


def near_pairs(list_ref, target_ref, centre_ref, source_ref, acc_ref, dist_ref):
    distances, products = near_parts(target_ref, centre_ref, source_ref, acc_ref, dist_ref)

    def step(i, carry):
        codes = [list_ref[STEP * i + k + 1] for k in range(STEP + 1)]
        for k in range(STEP):
            distances(lax.shift_right_logical(codes[k + 1], 8), codes[k + 1] & 255, (k + 1) % 2)
            products(lax.shift_right_logical(codes[k], 8), codes[k] & 255, k % 2, False)
        return carry

    distances(lax.shift_right_logical(list_ref[1], 8), list_ref[1] & 255, 0)
    lax.fori_loop(0, (list_ref[0] + STEP - 1) // STEP, step, 0)


def clear(acc_ref):
    def leaf(l, carry):
        acc_ref[l] = jnp.zeros((PTS, 128), F32)
        return carry

    lax.fori_loop(0, LEAVES, leaf, 0, unroll=2)


def near_rows(acc_ref, out_ref, add_ref):
    def leaf(l, carry):
        parts = [jnp.sum(acc_ref[l, h * 128 : (h + 1) * 128, :].T, axis=0, keepdims=True) for h in range(2)]
        value = jnp.concatenate(parts, axis=0)
        if add_ref is not None:
            value = value + add_ref[pl.ds(2 * l, 2), :]
        out_ref[pl.ds(2 * l, 2), :] = value
        return carry

    lax.fori_loop(0, LEAVES, leaf, 0, unroll=16)


def fill(source_ref, at, block_ref):
    for l in range(LEAVES):
        source_ref[at + l] = eight(block_ref[:, l * PTS : (l + 1) * PTS])
    source_ref[DUMMY] = jnp.zeros((8, PTS), F32)


def set_values(source_ref, at, block_ref):
    for l in range(LEAVES):
        pair = block_ref[2 * l : 2 * l + 2, :]
        source_ref[at + l, 3:4, :] = jnp.concatenate([pair[:1], pair[1:]], axis=1)


def skel_target(tile):
    wide = jnp.concatenate([eight(tile), jnp.zeros((8, 64), F32)], axis=1)
    centre = jnp.broadcast_to(jnp.sum(wide, axis=1, keepdims=True) * (1.0 / RANK), wide.shape)
    return centre, target_stack(centred(wide, centre))[:RANK]


def own_first_kernel(
    ids_ref, count_ref, points_ref, rhs_ref, skel_ref, target_out_ref, centre_ref, far_target_out_ref, far_centre_ref, own_list_ref, other_list_ref, out_ref,
    near_ref, source_ref, acc_ref, dist_ref, target_ref, far_target_ref, out_sems,
):
    here = lax.shift_right_logical(ids_ref[0, 0], 5)
    base = (here - 1) * LEAVES

    near_ref[:3, :] = points_ref[...]
    for half in range(2 * LEAVES):
        near_ref[3:4, half * 128 : (half + 1) * 128] = rhs_ref[half : half + 1, :]
    fill(source_ref, LEAVES, points_ref)
    set_values(source_ref, LEAVES, rhs_ref)

    def targets(l, carry):
        tile = source_ref[LEAVES + l]
        centre = jnp.broadcast_to(jnp.sum(tile, axis=1, keepdims=True) * (1.0 / PTS), (8, 128))
        centre_ref[l] = centre
        target_ref[l] = target_stack(centred(tile, jnp.concatenate([centre, centre], axis=1)))
        return carry

    lax.fori_loop(0, LEAVES, targets, 0, unroll=4)
    for l in range(LEAVES):
        far_centre_ref[l], far_target_ref[l] = skel_target(skel_ref[:, l * RANK : (l + 1) * RANK])
    copies = [
        pltpu.make_async_copy(target_ref, target_out_ref, out_sems.at[0]),
        pltpu.make_async_copy(far_target_ref, far_target_out_ref, out_sems.at[1]),
    ]
    for copy in copies:
        copy.start()

    def slots(l, counts):
        own, other = counts
        used = count_ref[l]
        for j in range(1, 8):
            n = ids_ref[j, l]
            code = l * 256 + (n - base)
            own_list_ref[own] = code
            other_list_ref[other] = code
            is_used = (j < used).astype(jnp.int32)
            is_own = (lax.shift_right_logical(n, 5) == here).astype(jnp.int32) * is_used
            own, other = own + is_own, other + is_used - is_own
        return own, other

    one = jnp.int32(1)
    own, other = near_self(target_ref, centre_ref, source_ref, acc_ref, dist_ref, slots, (one, one))
    for k in range(STEP + 1):
        own_list_ref[own + k] = DUMMY
        other_list_ref[other + k] = DUMMY
    own_list_ref[0] = own - 1
    other_list_ref[0] = other - 1
    near_pairs(own_list_ref, target_ref, centre_ref, source_ref, acc_ref, dist_ref)
    near_rows(acc_ref, out_ref, None)
    for copy in copies:
        copy.wait()


def own_next_kernel(
    own_list_ref, points_ref, field_ref, target_ref, centre_ref, out_ref, field_out_ref, source_ref, acc_ref, dist_ref
):
    field_out_ref[...] = field_ref[...]
    fill(source_ref, LEAVES, points_ref)
    set_values(source_ref, LEAVES, field_ref)
    near_self(target_ref, centre_ref, source_ref, acc_ref, dist_ref, lambda l, carry: carry, 0)
    near_pairs(own_list_ref, target_ref, centre_ref, source_ref, acc_ref, dist_ref)
    near_rows(acc_ref, out_ref, None)


def swap(tile):
    return pltpu.roll(tile, 64, 1)


def low_lanes():
    return lanes_of((1, 128)) < 64


def spread(tile):
    other = swap(tile)
    return jnp.where(low_lanes(), tile, other), jnp.where(low_lanes(), other, tile)


def far_partners(far_leaf_ref, l, rows_at):
    for j in range(0, 16, 2):
        yield jnp.where(low_lanes(), rows_at(far_leaf_ref[j, l] & 1023), rows_at(far_leaf_ref[j + 1, l] & 1023))


def far_sums(stack_ref, weight_ref, target_ref, out_ref, dist_ref):
    def distances(l, slot):
        for c in range(4):
            dist_ref[slot, c * RANK : (c + 1) * RANK, :] = squares(target_ref[l], stack_ref[l, :, c * 256 : (c + 1) * 256])

    def products(l, slot):
        total = jnp.zeros((RANK, 128), F32)
        for c in range(4):
            weights = weight_ref[l, :1, c * 256 : (c + 1) * 256]
            total = total + weighted(dist_ref[slot, c * RANK : (c + 1) * RANK, :], weights)
        column = jnp.sum(total, axis=1, keepdims=True)
        out_ref[...] = jnp.where(lanes_of((RANK, 128)) == l, column, out_ref[...])

    def step(i, carry):
        for k in range(STEP):
            distances(jnp.minimum(STEP * i + k + 1, LEAVES - 1), (k + 1) % 2)
            products(STEP * i + k, k % 2)
        return carry

    out_ref[...] = jnp.zeros((RANK, 128), F32)
    distances(0, 0)
    lax.fori_loop(0, LEAVES // STEP, step, 0)


def middle_first_kernel(
    other_list_ref, far_leaf_ref, prev_ref, next_ref, target_ref, centre_ref, own_ref, far_target_ref, far_centre_ref, group_ref,
    near_ref, far_ref, stack_out_ref, source_ref, acc_ref, dist_ref, weight_ref, table_ref, stack_ref, stack_sem,
):
    def table(d, carry):
        for m in range(0, 16, 2):
            low, high = spread(group_ref[d, 4 * m : 4 * m + 8, :])
            for k in range(2):
                table_ref[d * LEAVES + m + k] = low[4 * k : 4 * k + 4]
                table_ref[d * LEAVES + m + k + 16] = high[4 * k : 4 * k + 4]
        return carry

    lax.fori_loop(0, 32, table, 0, unroll=4)

    def gather(l, carry):
        centre = far_centre_ref[l]
        rows = far_partners(far_leaf_ref, l, lambda p: table_ref[p])
        for j, tile in enumerate(rows):
            at = j * 128
            weight_ref[l, :1, at : at + 128] = tile[3:4] * FACTOR
            stack_ref[l, :, at : at + 128] = source_stack(centred(eight(tile), centre))
        return carry

    lax.fori_loop(0, LEAVES, gather, 0, unroll=4)
    stack_copy = pltpu.make_async_copy(stack_ref, stack_out_ref, stack_sem)
    stack_copy.start()
    far_target_ref.wait()
    far_sums(stack_ref, weight_ref, far_target_ref, far_ref, dist_ref)
    for operand in (prev_ref, next_ref, target_ref, centre_ref, own_ref):
        operand.wait()
    fill(source_ref, 0, prev_ref)
    fill(source_ref, 2 * LEAVES, next_ref)
    clear(acc_ref)
    near_pairs(other_list_ref, target_ref, centre_ref, source_ref, acc_ref, dist_ref)
    near_rows(acc_ref, near_ref, own_ref)
    stack_copy.wait()


def middle_next_kernel(
    other_list_ref, far_leaf_ref, prev_ref, next_ref, prev_val_ref, next_val_ref, target_ref, centre_ref, own_ref, far_target_ref,
    stack_ref, group_ref, near_ref, far_ref, source_ref, acc_ref, dist_ref, weight_ref, table_ref,
):
    for d in range(32):
        low, high = spread(group_ref[d, :16, :])
        table_ref[d * LEAVES : d * LEAVES + 16, :] = low
        table_ref[d * LEAVES + 16 : d * LEAVES + 32, :] = high

    def gather(l, carry):
        rows = far_partners(far_leaf_ref, l, lambda p: table_ref[pl.ds(p, 1), :])
        for j, tile in enumerate(rows):
            weight_ref[l, :1, j * 128 : (j + 1) * 128] = tile * FACTOR
        return carry

    lax.fori_loop(0, LEAVES, gather, 0, unroll=4)
    for operand in (prev_ref, next_ref, prev_val_ref, next_val_ref, target_ref, centre_ref, own_ref):
        operand.wait()
    fill(source_ref, 0, prev_ref)
    fill(source_ref, 2 * LEAVES, next_ref)
    set_values(source_ref, 0, prev_val_ref)
    set_values(source_ref, 2 * LEAVES, next_val_ref)
    clear(acc_ref)
    near_pairs(other_list_ref, target_ref, centre_ref, source_ref, acc_ref, dist_ref)
    near_rows(acc_ref, near_ref, own_ref)
    far_target_ref.wait()
    stack_ref.wait()
    far_sums(stack_ref, weight_ref, far_target_ref, far_ref, dist_ref)


def node_down(far_node_ref, node_skel_ref, nodes_ref, weight_ref):
    own = node_skel_ref[...]
    centre, target = skel_target(jnp.concatenate([own[:1], own[2:3], own[1:2]], axis=0))
    total = jnp.zeros((RANK, 128), F32)
    for at in range(0, 32, 4):
        coords, weights = [], []
        for j in (at, at + 2):
            tiles = []
            for p in (far_node_ref[0, j], far_node_ref[0, j + 1]):
                g, d = lax.shift_right_logical(p, 5), p & 31
                rows = [nodes_ref[g, pl.ds(d, 1), :], nodes_ref[g, pl.ds(d + 32, 1), :]]
                if weight_ref is not None:
                    rows.append(weight_ref[g, pl.ds(d, 1), :])
                tiles.append(jnp.concatenate(rows, axis=0))
            even = jnp.where(low_lanes(), tiles[0], swap(tiles[1]))
            odd = jnp.where(low_lanes(), swap(tiles[0]), tiles[1])
            coords.append(eight(jnp.concatenate([even[:2], odd[:2]], axis=0)))
            weights.append(odd[1:2] if weight_ref is None else even[2:3])
        wide = jnp.concatenate([centre, centre], axis=1)
        sources = source_stack(centred(jnp.concatenate(coords, axis=1), wide))
        dist_sq = squares(target, sources)
        total = total + weighted(dist_sq, jnp.concatenate(weights, axis=1) * FACTOR)
    return jnp.sum(total.T, axis=0, keepdims=True)


def leaf_row(l, down, far_ref, near_ref, basis_ref, transfer_ref):
    moved = transfer_ref[l] * down
    total = jnp.where(lanes_of((RANK, 128)) == l, far_ref[...], 0.0) + jnp.concatenate([moved, jnp.zeros((RANK, 64), F32)], axis=1)
    column = jnp.sum(total, axis=1, keepdims=True)
    return row_of(near_ref, l) + jnp.sum(basis_ref[l] * column, axis=0, keepdims=True)


def scalars(values):
    lane = lanes_of((1, 128))
    out = jnp.zeros((1, 128), F32)
    for at, value in enumerate(values):
        out = jnp.where(lane == 64 + at, value, out)
    return out


def dot(a, b):
    return jnp.sum(jnp.sum(a * b, axis=0, keepdims=True), axis=1, keepdims=True)


def finish_first_kernel(
    far_node_ref, node_skel_ref, nodes_ref, near_ref, far_ref, rhs_ref, basis_ref, transfer_ref, out_ref, pay_ref
):
    down = node_down(far_node_ref, node_skel_ref, nodes_ref, None)
    for operand in (near_ref, far_ref, rhs_ref):
        operand.wait()

    def leaf(l, carry):
        row = leaf_row(l, down, far_ref, near_ref, basis_ref, transfer_ref)
        out_ref[pl.ds(2 * l, 2), :] = pair_of(row)
        return project(carry, l, row, basis_ref, transfer_ref)

    weights, node = project_end(leaves_in_parts((basis_ref, transfer_ref), leaf, project_start()))
    rhs, image = rhs_ref[...], out_ref[...]
    extra = scalars([dot(rhs, rhs), dot(rhs, image)])
    last = jnp.where(lanes_of((1, 128)) < 64, jnp.concatenate([node, node], axis=1), extra)
    payload = jnp.concatenate([weights, last, jnp.zeros((7, 128), F32)], axis=0)
    for d in range(32):
        pay_ref[d] = payload


def lane(row, at):
    return jnp.sum(jnp.where(lanes_of(row.shape) == at, row, 0.0), axis=1, keepdims=True)


def first_scalars(node_ref):
    total = jnp.sum(jnp.sum(node_ref[...], axis=0), axis=0, keepdims=True)
    norm, inner = lane(total, 64), lane(total, 65)
    energy = NUGGET * norm + inner
    return norm, inner, energy, norm / energy


def finish_next_kernel(
    far_node_ref, node_skel_ref, nodes_ref, node_in_ref, near_ref, far_ref, rhs_ref, field_ref, basis_ref, transfer_ref, out_ref, pay_ref
):
    down = node_down(far_node_ref, node_skel_ref, nodes_ref, node_in_ref)
    for operand in (near_ref, far_ref, rhs_ref, field_ref):
        operand.wait()

    def leaf(l, carry):
        out_ref[pl.ds(2 * l, 2), :] = pair_of(leaf_row(l, down, far_ref, near_ref, basis_ref, transfer_ref))
        return carry

    leaves_in_parts((basis_ref, transfer_ref), leaf, 0)
    _, inner, energy, alpha = first_scalars(node_in_ref)
    rhs, field, field2 = rhs_ref[...], field_ref[...], out_ref[...]
    keep = inner / energy
    residual = keep * rhs - alpha * field
    image = NUGGET * residual + keep * field - alpha * field2
    base = NUGGET * rhs + field
    block = scalars([dot(residual, residual), dot(residual, image), dot(residual, base) + dot(rhs, image)])
    pay_ref[...] = jnp.broadcast_to(block[None], pay_ref.shape)


def last_kernel(rhs_ref, field_ref, field2_ref, node_ref, last_ref, solution_ref, residual_ref):
    norm, inner, energy, alpha = first_scalars(node_ref)
    total = jnp.sum(last_ref[...], axis=0)
    norm2 = lane(total, 64)
    beta = norm2 / norm
    alpha2 = norm2 / (lane(total, 65) + beta * lane(total, 66) + beta * beta * energy)
    rhs, field, field2 = rhs_ref[...], field_ref[...], field2_ref[...]
    keep = inner / energy
    residual = keep * rhs - alpha * field
    image = NUGGET * residual + keep * field - alpha * field2
    direction = residual + beta * rhs
    solution_ref[...] = alpha * rhs + alpha2 * direction
    residual_ref[...] = residual - alpha2 * (image + beta * (NUGGET * rhs + field))


class Operand:
    def __init__(self, source, ref, sems, parts):
        self.ref, self.shape = ref, ref.shape
        if parts == 1:
            self.copies = [pltpu.make_async_copy(source, ref, sems.at[0])]
        else:
            spans = [pl.ds(part * (ref.shape[0] // parts), ref.shape[0] // parts) for part in range(parts)]
            self.copies = [pltpu.make_async_copy(source.at[span], ref.at[span], sems.at[n]) for n, span in enumerate(spans)]

    def wait(self, part=0):
        self.copies[part].wait()

    def __getitem__(self, at):
        return self.ref[at]


def call(kernel, name, outs, ins, scratch=(), work=0, late=(), apart=(), split_up=()):
    floats = [at for at, array in enumerate(ins) if array.dtype != jnp.int32]

    def whole(shape):
        return pl.BlockSpec(shape, lambda i: (0,) * len(shape))

    def body(*refs):
        operands = list(refs[: len(ins)])
        buffers, sems = refs[-1 - len(floats) : -1], refs[-1]
        for k, at in enumerate(floats):
            operands[at] = Operand(operands[at], buffers[k], sems.at[k], PARTS if at in split_up else 1)
        for at in [at for at in floats if at not in late] + [at for at in late if at not in split_up]:
            operands[at].copies[0].start()
        for part in range(PARTS if split_up else 0):
            for at in split_up:
                operands[at].copies[part].start()
        for at in floats:
            if at not in late:
                operands[at].wait()
        kernel(*operands, *refs[len(ins) : -1 - len(floats)])

    return pl.pallas_call(
        body,
        grid=(1,),
        out_shape=[jax.ShapeDtypeStruct(shape, dtype) for shape, dtype in outs],
        in_specs=[SMEM if array.dtype == jnp.int32 else pl.BlockSpec(memory_space=pl.ANY) for array in ins],
        out_specs=[
            SMEM if dtype == jnp.int32 else pl.BlockSpec(memory_space=pl.ANY) if at in apart else whole(shape)
            for at, (shape, dtype) in enumerate(outs)
        ],
        scratch_shapes=list(scratch)
        + [pltpu.VMEM(ins[at].shape, ins[at].dtype) for at in floats]
        + [pltpu.SemaphoreType.DMA((len(floats), PARTS))],
        compiler_params=params(),
        cost_estimate=pl.CostEstimate(flops=work * 1_000_000_000, bytes_accessed=1_000_000, transcendentals=0),
        name=name,
    )(*ins)


def neighbours(block):
    count = lax.axis_size("grp") * lax.axis_size("dev")
    up = [(i, i + 1) for i in range(count - 1)]
    down = [(i + 1, i) for i in range(count - 1)]
    return lax.ppermute(block, AXES, up), lax.ppermute(block, AXES, down)


def exchange(copies, axes):
    return lax.all_to_all(copies, axes, 0, 0, tiled=True)


def on_device(rhs, points, leaf_basis, transfer, leaf_skel, node_skel, near_ids, near_count, far_leaf, far_node):
    rhs = rhs.reshape(2 * LEAVES, 128)
    basis = jnp.swapaxes(leaf_basis, 1, 2)
    far_leaf = far_leaf.T
    I32 = jnp.int32
    vector = ((2 * LEAVES, 128), F32)
    distances = pltpu.VMEM((2, PTS, 256), F32)
    near_scratch = [pltpu.VMEM((DUMMY + 1, 8, PTS), F32), pltpu.VMEM((LEAVES, PTS, 128), F32), distances]
    far_scratch = [pltpu.VMEM((LEAVES, 8, 1024), F32)]
    (pay,) = call(
        prepare_kernel,
        "prepare",
        [((32, 72, 128), F32)],
        [rhs, basis, transfer, leaf_skel, node_skel],
        work=4,
        late=(1, 2),
        split_up=(1, 2),
    )
    group = exchange(pay, "dev")
    targets, centres, far_targets, far_centres, own_list, other_list, own_part, near_pay = call(
        own_first_kernel,
        "own_first",
        [
            ((LEAVES, PTS, 128), BF16),
            ((LEAVES, 8, 128), F32),
            ((LEAVES, RANK, 128), BF16),
            ((LEAVES, 8, 128), F32),
            ((LIST,), I32),
            ((LIST,), I32),
            vector,
            ((4, LEAVES * PTS), F32),
        ],
        [near_ids.T, near_count, points, rhs, leaf_skel],
        near_scratch
        + [pltpu.VMEM((LEAVES, PTS, 128), BF16), pltpu.VMEM((LEAVES, RANK, 128), BF16), pltpu.SemaphoreType.DMA((2,))],
        work=15,
        apart=(0, 2),
    )
    prev_pay, next_pay = neighbours(near_pay)
    rows = jnp.swapaxes(group[:, 64:66], 0, 1).reshape(1, 64, 128)
    node_pay = jnp.broadcast_to(rows, (8, 64, 128))
    nodes = exchange(node_pay, "grp")
    near_part, far_part, stacks = call(
        middle_first_kernel,
        "middle_first",
        [vector, ((RANK, 128), F32), ((LEAVES, DEPTH, 1024), BF16)],
        [other_list, far_leaf, prev_pay, next_pay, targets, centres, own_part, far_targets, far_centres, group],
        near_scratch + far_scratch + [pltpu.VMEM((1024, 4, 128), F32), pltpu.VMEM((LEAVES, DEPTH, 1024), BF16), pltpu.SemaphoreType.DMA],
        work=20,
        apart=(2,),
        late=(7, 2, 3, 4, 5, 6),
    )
    field, pay = call(
        finish_first_kernel,
        "finish_first",
        [vector, ((32, 24, 128), F32)],
        [far_node, node_skel, nodes, near_part, far_part, rhs, basis, transfer],
        work=4,
        late=(3, 4, 5, 6, 7),
        split_up=(6, 7),
    )
    leaf_in = exchange(pay, "dev")
    own_part, near_field = call(
        own_next_kernel, "own_next", [vector, vector], [own_list, points, field, targets, centres], near_scratch, work=10
    )
    prev_val, next_val = neighbours(near_field)
    node_pay = jnp.broadcast_to(leaf_in[None, :, 16], (8, 32, 128))
    node_in = exchange(node_pay, "grp")
    near_part, far_part = call(
        middle_next_kernel,
        "middle_next",
        [vector, ((RANK, 128), F32)],
        [
            other_list, far_leaf, prev_pay, next_pay, prev_val, next_val, targets, centres, own_part, far_targets, stacks, leaf_in,
        ],
        near_scratch + far_scratch + [pltpu.VMEM((1024, 128), F32)],
        work=20,
        late=(6, 2, 3, 4, 5, 7, 8, 9, 10),
    )
    field2, pay = call(
        finish_next_kernel,
        "finish_next",
        [vector, ((256, 1, 128), F32)],
        [far_node, node_skel, nodes, node_in, near_part, far_part, rhs, field, basis, transfer],
        work=4,
        late=(4, 5, 6, 7, 8, 9),
        split_up=(8, 9),
    )
    last = exchange(pay, AXES)
    answer, residual = call(last_kernel, "last", [vector, vector], [rhs, field, field2, node_in, last], work=1)
    return answer.reshape(-1), residual.reshape(-1)


def solution(mesh):
    placed = (
        P(AXES),
        P(None, AXES),
        P(AXES, None, None),
        P(AXES, None, None),
        P(None, AXES),
        P(None, AXES),
        P(AXES, None),
        P(AXES),
        P(AXES, None),
        P(AXES, None),
    )
    return jax.shard_map(on_device, mesh=mesh, in_specs=placed, out_specs=(P(AXES), P(AXES)), check_vma=False)
```

```python
import math

import jax
import jax.numpy as jnp
from jax import lax
from jax.experimental import pallas as pl
from jax.experimental.pallas import tpu as pltpu
from jax.sharding import PartitionSpec as P

AXES = ("grp", "dev")
F32 = jnp.float32
BF16 = jnp.bfloat16
LN2 = math.log(2.0)
AMPLITUDE = 0.00390625
LENGTH = 0.25
NUGGET = 2.0
SCALE = math.sqrt(5.0) / LENGTH / 3.0
POWER = -3.0 / LN2
FACTOR = AMPLITUDE * 3.0
SMEM = pl.BlockSpec(memory_space=pltpu.SMEM)
LEAVES, PTS, RANK = 32, 256, 64
DEPTH = 48
DUMMY = 96
STEP = 4
LIST = 272
PARTS = 4


def params():
    return pltpu.CompilerParams(vmem_limit_bytes=64 * 1024 * 1024)


def split(x):
    hi = x.astype(BF16).astype(F32)
    rest = x - hi
    mid = rest.astype(BF16).astype(F32)
    return hi, mid, rest - mid


def rows_of(shape):
    return lax.broadcasted_iota(jnp.int32, shape, 0)


def lanes_of(shape):
    return lax.broadcasted_iota(jnp.int32, shape, 1)


def source_stack(coords):
    row = rows_of(coords.shape)
    norm = jnp.sum(coords * coords, axis=0, keepdims=True)
    full = jnp.where(row < 3, coords, jnp.where(row == 3, norm, jnp.where(row == 4, 1.0, 0.0)))
    hi, mid, low = split(full)
    return jnp.concatenate([hi, hi, mid, mid, hi, low], axis=0).astype(BF16)


def target_stack(coords):
    row = rows_of(coords.shape)
    norm = jnp.sum(coords * coords, axis=0, keepdims=True)
    full = jnp.where(row < 3, -2.0 * coords, jnp.where(row == 3, 1.0, jnp.where(row == 4, norm, 0.0)))
    hi, mid, low = split(full)
    rest = jnp.zeros((128 - DEPTH,) + hi.shape[1:], F32)
    return jnp.concatenate([hi, mid, hi, mid, low, hi, rest], axis=0).T.astype(BF16)


def squares(targets, sources):
    return jnp.dot(targets[:, :DEPTH], sources, preferred_element_type=F32)


def weighted(dist_sq, weights):
    dist_sq = jnp.maximum(dist_sq, 1e-30)
    dist = dist_sq * lax.rsqrt(dist_sq)
    value = (dist_sq + (dist + 1.0 / 3.0)) * jnp.exp2(dist * POWER) * weights
    total = value[:, :128]
    for at in range(128, value.shape[1], 128):
        total = total + value[:, at : at + 128]
    return total


def centred(tile, centre):
    shape = tile.shape
    return jnp.where(rows_of(shape) < 3, (tile - centre) * SCALE, 0.0)


def less(tile, centre):
    return jnp.where(rows_of(tile.shape) < 3, tile - centre, 0.0)


def eight(tile):
    return jnp.concatenate([tile, jnp.zeros((8 - tile.shape[0], tile.shape[1]), F32)], axis=0)


def row_of(ref, l):
    pair = ref[pl.ds(2 * l, 2), :]
    return jnp.concatenate([pair[:1], pair[1:]], axis=1)


def pair_of(row):
    return jnp.concatenate([row[:, :128], row[:, 128:]], axis=0)


def project(carry, l, row, basis_ref, transfer_ref):
    weights, node = carry
    column = jnp.sum(basis_ref[l] * row, axis=1, keepdims=True)
    return jnp.where(lanes_of(weights.shape) == l, column, weights), node + transfer_ref[l] * column


def project_start():
    return jnp.zeros((RANK, 128), F32), jnp.zeros((RANK, RANK), F32)


def leaves_in_parts(operands, body, carry):
    count = LEAVES // PARTS
    for part in range(PARTS):
        for operand in operands:
            operand.wait(part)
        carry = lax.fori_loop(part * count, (part + 1) * count, body, carry, unroll=count)
    return carry


def project_end(carry):
    rows = carry[0].T
    return jnp.concatenate([rows[:16], rows[16:32]], axis=1), jnp.sum(carry[1], axis=0, keepdims=True)


def prepare_kernel(rhs_ref, basis_ref, transfer_ref, leaf_skel_ref, node_skel_ref, pay_ref):
    weights, node = project_end(
        leaves_in_parts(
            (basis_ref, transfer_ref), lambda l, c: project(c, l, row_of(rhs_ref, l), basis_ref, transfer_ref), project_start()
        )
    )
    skel = leaf_skel_ref[...]
    tiles = []
    for m in range(16):
        low = skel[:, m * RANK : (m + 1) * RANK]
        high = skel[:, (m + 16) * RANK : (m + 17) * RANK]
        tiles.append(jnp.concatenate([low, high], axis=1))
        tiles.append(weights[m : m + 1])
    own = node_skel_ref[...]
    tiles.append(jnp.concatenate([own[:1], own[1:2]], axis=1))
    tiles.append(jnp.concatenate([own[2:3], node], axis=1))
    tiles.append(jnp.zeros((6, 128), F32))
    payload = jnp.concatenate(tiles, axis=0)
    for d in range(32):
        pay_ref[d] = payload


def near_parts(target_ref, centre_ref, source_ref, acc_ref, dist_ref):
    def distances(l, at, slot):
        centre = centre_ref[l]
        coords = less(source_ref[at], jnp.concatenate([centre, centre], axis=1))
        dist_ref[slot] = squares(target_ref[l], source_stack(coords))

    def products(l, at, slot, first):
        weights = source_ref[at, 3:4, :]
        for row in range(0, PTS, 64):
            value = weighted(dist_ref[slot, row : row + 64, :], weights)
            if first:
                acc_ref[l, row : row + 64, :] = value
            else:
                acc_ref[l, row : row + 64, :] += value

    return distances, products


def near_self(target_ref, centre_ref, source_ref, acc_ref, dist_ref, beside, carry):
    distances, products = near_parts(target_ref, centre_ref, source_ref, acc_ref, dist_ref)

    def step(i, carry):
        for k in range(STEP):
            l = STEP * i + k
            later = jnp.minimum(l + 1, LEAVES - 1)
            distances(later, LEAVES + later, (k + 1) % 2)
            products(l, LEAVES + l, k % 2, True)
            carry = beside(l, carry)
        return carry

    distances(0, LEAVES, 0)
    return lax.fori_loop(0, LEAVES // STEP, step, carry)


def near_pairs(list_ref, target_ref, centre_ref, source_ref, acc_ref, dist_ref):
    distances, products = near_parts(target_ref, centre_ref, source_ref, acc_ref, dist_ref)

    def step(i, carry):
        codes = [list_ref[STEP * i + k + 1] for k in range(STEP + 1)]
        for k in range(STEP):
            distances(lax.shift_right_logical(codes[k + 1], 8), codes[k + 1] & 255, (k + 1) % 2)
            products(lax.shift_right_logical(codes[k], 8), codes[k] & 255, k % 2, False)
        return carry

    distances(lax.shift_right_logical(list_ref[1], 8), list_ref[1] & 255, 0)
    lax.fori_loop(0, (list_ref[0] + STEP - 1) // STEP, step, 0)


def clear(acc_ref):
    def leaf(l, carry):
        acc_ref[l] = jnp.zeros((PTS, 128), F32)
        return carry

    lax.fori_loop(0, LEAVES, leaf, 0, unroll=2)


def near_rows(acc_ref, out_ref, add_ref):
    def leaf(l, carry):
        parts = [jnp.sum(acc_ref[l, h * 128 : (h + 1) * 128, :].T, axis=0, keepdims=True) for h in range(2)]
        value = jnp.concatenate(parts, axis=0)
        if add_ref is not None:
            value = value + add_ref[pl.ds(2 * l, 2), :]
        out_ref[pl.ds(2 * l, 2), :] = value
        return carry

    lax.fori_loop(0, LEAVES, leaf, 0, unroll=16)


def fill(source_ref, at, block_ref):
    for l in range(LEAVES):
        tile = eight(block_ref[:, l * PTS : (l + 1) * PTS])
        source_ref[at + l] = tile * jnp.where(rows_of(tile.shape) < 3, SCALE, FACTOR)
    source_ref[DUMMY] = jnp.zeros((8, PTS), F32)


def set_values(source_ref, at, block_ref):
    for l in range(LEAVES):
        pair = block_ref[2 * l : 2 * l + 2, :]
        source_ref[at + l, 3:4, :] = jnp.concatenate([pair[:1], pair[1:]], axis=1) * FACTOR


def skel_target(tile):
    wide = jnp.concatenate([eight(tile), jnp.zeros((8, 64), F32)], axis=1)
    centre = jnp.broadcast_to(jnp.sum(wide, axis=1, keepdims=True) * (1.0 / RANK), wide.shape)
    return centre, target_stack(centred(wide, centre))[:RANK]


def own_first_kernel(
    ids_ref, count_ref, points_ref, rhs_ref, skel_ref, target_out_ref, centre_ref, far_target_out_ref, far_centre_ref, own_list_ref, other_list_ref, out_ref,
    near_ref, source_ref, acc_ref, dist_ref, target_ref, far_target_ref, out_sems,
):
    here = lax.shift_right_logical(ids_ref[0, 0], 5)
    base = (here - 1) * LEAVES

    near_ref[:3, :] = points_ref[...]
    for half in range(2 * LEAVES):
        near_ref[3:4, half * 128 : (half + 1) * 128] = rhs_ref[half : half + 1, :]
    fill(source_ref, LEAVES, points_ref)
    set_values(source_ref, LEAVES, rhs_ref)

    def targets(l, carry):
        tile = source_ref[LEAVES + l]
        centre = jnp.broadcast_to(jnp.sum(tile, axis=1, keepdims=True) * (1.0 / PTS), (8, 128))
        centre_ref[l] = centre
        target_ref[l] = target_stack(less(tile, jnp.concatenate([centre, centre], axis=1)))
        return carry

    lax.fori_loop(0, LEAVES, targets, 0, unroll=4)
    for l in range(LEAVES):
        far_centre_ref[l], far_target_ref[l] = skel_target(skel_ref[:, l * RANK : (l + 1) * RANK])
    copies = [
        pltpu.make_async_copy(target_ref, target_out_ref, out_sems.at[0]),
        pltpu.make_async_copy(far_target_ref, far_target_out_ref, out_sems.at[1]),
    ]
    for copy in copies:
        copy.start()

    def slots(l, counts):
        own, other = counts
        used = count_ref[l]
        for j in range(1, 8):
            n = ids_ref[j, l]
            code = l * 256 + (n - base)
            own_list_ref[own] = code
            other_list_ref[other] = code
            is_used = (j < used).astype(jnp.int32)
            is_own = (lax.shift_right_logical(n, 5) == here).astype(jnp.int32) * is_used
            own, other = own + is_own, other + is_used - is_own
        return own, other

    one = jnp.int32(1)
    own, other = near_self(target_ref, centre_ref, source_ref, acc_ref, dist_ref, slots, (one, one))
    for k in range(STEP + 1):
        own_list_ref[own + k] = DUMMY
        other_list_ref[other + k] = DUMMY
    own_list_ref[0] = own - 1
    other_list_ref[0] = other - 1
    near_pairs(own_list_ref, target_ref, centre_ref, source_ref, acc_ref, dist_ref)
    near_rows(acc_ref, out_ref, None)
    for copy in copies:
        copy.wait()


def own_next_kernel(
    own_list_ref, points_ref, field_ref, target_ref, centre_ref, out_ref, field_out_ref, source_ref, acc_ref, dist_ref
):
    field_out_ref[...] = field_ref[...]
    fill(source_ref, LEAVES, points_ref)
    set_values(source_ref, LEAVES, field_ref)
    near_self(target_ref, centre_ref, source_ref, acc_ref, dist_ref, lambda l, carry: carry, 0)
    near_pairs(own_list_ref, target_ref, centre_ref, source_ref, acc_ref, dist_ref)
    near_rows(acc_ref, out_ref, None)


def swap(tile):
    return pltpu.roll(tile, 64, 1)


def low_lanes():
    return lanes_of((1, 128)) < 64


def spread(tile):
    other = swap(tile)
    return jnp.where(low_lanes(), tile, other), jnp.where(low_lanes(), other, tile)


def far_partners(far_leaf_ref, l, rows_at):
    for j in range(0, 16, 2):
        yield jnp.where(low_lanes(), rows_at(far_leaf_ref[j, l] & 1023), rows_at(far_leaf_ref[j + 1, l] & 1023))


def far_sums(stack_ref, weight_ref, target_ref, out_ref, dist_ref):
    def distances(l, slot):
        for c in range(4):
            dist_ref[slot, c * RANK : (c + 1) * RANK, :] = squares(target_ref[l], stack_ref[l, :, c * 256 : (c + 1) * 256])

    def products(l, slot):
        total = jnp.zeros((RANK, 128), F32)
        for c in range(4):
            weights = weight_ref[l, :1, c * 256 : (c + 1) * 256]
            total = total + weighted(dist_ref[slot, c * RANK : (c + 1) * RANK, :], weights)
        column = jnp.sum(total, axis=1, keepdims=True)
        out_ref[...] = jnp.where(lanes_of((RANK, 128)) == l, column, out_ref[...])

    def step(i, carry):
        for k in range(STEP):
            distances(jnp.minimum(STEP * i + k + 1, LEAVES - 1), (k + 1) % 2)
            products(STEP * i + k, k % 2)
        return carry

    out_ref[...] = jnp.zeros((RANK, 128), F32)
    distances(0, 0)
    lax.fori_loop(0, LEAVES // STEP, step, 0)


def middle_first_kernel(
    other_list_ref, far_leaf_ref, prev_ref, next_ref, target_ref, centre_ref, own_ref, far_target_ref, far_centre_ref, group_ref,
    near_ref, far_ref, stack_out_ref, source_ref, acc_ref, dist_ref, weight_ref, table_ref, stack_ref, stack_sem,
):
    def table(d, carry):
        for m in range(0, 16, 2):
            low, high = spread(group_ref[d, 4 * m : 4 * m + 8, :])
            for k in range(2):
                table_ref[d * LEAVES + m + k] = low[4 * k : 4 * k + 4]
                table_ref[d * LEAVES + m + k + 16] = high[4 * k : 4 * k + 4]
        return carry

    lax.fori_loop(0, 32, table, 0, unroll=4)

    def gather(l, carry):
        centre = far_centre_ref[l]
        rows = far_partners(far_leaf_ref, l, lambda p: table_ref[p])
        for j, tile in enumerate(rows):
            at = j * 128
            weight_ref[l, :1, at : at + 128] = tile[3:4] * FACTOR
            stack_ref[l, :, at : at + 128] = source_stack(centred(eight(tile), centre))
        return carry

    lax.fori_loop(0, LEAVES, gather, 0, unroll=4)
    stack_copy = pltpu.make_async_copy(stack_ref, stack_out_ref, stack_sem)
    stack_copy.start()
    far_target_ref.wait()
    far_sums(stack_ref, weight_ref, far_target_ref, far_ref, dist_ref)
    for operand in (prev_ref, next_ref, target_ref, centre_ref, own_ref):
        operand.wait()
    fill(source_ref, 0, prev_ref)
    fill(source_ref, 2 * LEAVES, next_ref)
    clear(acc_ref)
    near_pairs(other_list_ref, target_ref, centre_ref, source_ref, acc_ref, dist_ref)
    near_rows(acc_ref, near_ref, own_ref)
    stack_copy.wait()


def middle_next_kernel(
    other_list_ref, far_leaf_ref, prev_ref, next_ref, prev_val_ref, next_val_ref, target_ref, centre_ref, own_ref, far_target_ref,
    stack_ref, group_ref, near_ref, far_ref, source_ref, acc_ref, dist_ref, weight_ref, table_ref,
):
    for d in range(32):
        low, high = spread(group_ref[d, :16, :])
        table_ref[d * LEAVES : d * LEAVES + 16, :] = low
        table_ref[d * LEAVES + 16 : d * LEAVES + 32, :] = high

    def gather(l, carry):
        rows = far_partners(far_leaf_ref, l, lambda p: table_ref[pl.ds(p, 1), :])
        for j, tile in enumerate(rows):
            weight_ref[l, :1, j * 128 : (j + 1) * 128] = tile * FACTOR
        return carry

    lax.fori_loop(0, LEAVES, gather, 0, unroll=4)
    for operand in (prev_ref, next_ref, prev_val_ref, next_val_ref, target_ref, centre_ref, own_ref):
        operand.wait()
    fill(source_ref, 0, prev_ref)
    fill(source_ref, 2 * LEAVES, next_ref)
    set_values(source_ref, 0, prev_val_ref)
    set_values(source_ref, 2 * LEAVES, next_val_ref)
    clear(acc_ref)
    near_pairs(other_list_ref, target_ref, centre_ref, source_ref, acc_ref, dist_ref)
    near_rows(acc_ref, near_ref, own_ref)
    far_target_ref.wait()
    stack_ref.wait()
    far_sums(stack_ref, weight_ref, far_target_ref, far_ref, dist_ref)


def node_down(far_node_ref, node_skel_ref, nodes_ref, weight_ref):
    own = node_skel_ref[...]
    centre, target = skel_target(jnp.concatenate([own[:1], own[2:3], own[1:2]], axis=0))
    total = jnp.zeros((RANK, 128), F32)
    for at in range(0, 32, 4):
        coords, weights = [], []
        for j in (at, at + 2):
            tiles = []
            for p in (far_node_ref[0, j], far_node_ref[0, j + 1]):
                g, d = lax.shift_right_logical(p, 5), p & 31
                rows = [nodes_ref[g, pl.ds(d, 1), :], nodes_ref[g, pl.ds(d + 32, 1), :]]
                if weight_ref is not None:
                    rows.append(weight_ref[g, pl.ds(d, 1), :])
                tiles.append(jnp.concatenate(rows, axis=0))
            even = jnp.where(low_lanes(), tiles[0], swap(tiles[1]))
            odd = jnp.where(low_lanes(), swap(tiles[0]), tiles[1])
            coords.append(eight(jnp.concatenate([even[:2], odd[:2]], axis=0)))
            weights.append(odd[1:2] if weight_ref is None else even[2:3])
        wide = jnp.concatenate([centre, centre], axis=1)
        sources = source_stack(centred(jnp.concatenate(coords, axis=1), wide))
        dist_sq = squares(target, sources)
        total = total + weighted(dist_sq, jnp.concatenate(weights, axis=1) * FACTOR)
    return jnp.sum(total.T, axis=0, keepdims=True)


def leaf_row(l, down, far_ref, near_ref, basis_ref, transfer_ref):
    moved = transfer_ref[l] * down
    total = jnp.where(lanes_of((RANK, 128)) == l, far_ref[...], 0.0) + jnp.concatenate([moved, jnp.zeros((RANK, 64), F32)], axis=1)
    column = jnp.sum(total, axis=1, keepdims=True)
    return row_of(near_ref, l) + jnp.sum(basis_ref[l] * column, axis=0, keepdims=True)


def scalars(values):
    lane = lanes_of((1, 128))
    out = jnp.zeros((1, 128), F32)
    for at, value in enumerate(values):
        out = jnp.where(lane == 64 + at, value, out)
    return out


def dot(a, b):
    return jnp.sum(jnp.sum(a * b, axis=0, keepdims=True), axis=1, keepdims=True)


def finish_first_kernel(
    far_node_ref, node_skel_ref, nodes_ref, near_ref, far_ref, rhs_ref, basis_ref, transfer_ref, out_ref, pay_ref
):
    down = node_down(far_node_ref, node_skel_ref, nodes_ref, None)
    for operand in (near_ref, far_ref, rhs_ref):
        operand.wait()

    def leaf(l, carry):
        row = leaf_row(l, down, far_ref, near_ref, basis_ref, transfer_ref)
        out_ref[pl.ds(2 * l, 2), :] = pair_of(row)
        return project(carry, l, row, basis_ref, transfer_ref)

    weights, node = project_end(leaves_in_parts((basis_ref, transfer_ref), leaf, project_start()))
    rhs, image = rhs_ref[...], out_ref[...]
    extra = scalars([dot(rhs, rhs), dot(rhs, image)])
    last = jnp.where(lanes_of((1, 128)) < 64, jnp.concatenate([node, node], axis=1), extra)
    payload = jnp.concatenate([weights, last, jnp.zeros((7, 128), F32)], axis=0)
    for d in range(32):
        pay_ref[d] = payload


def lane(row, at):
    return jnp.sum(jnp.where(lanes_of(row.shape) == at, row, 0.0), axis=1, keepdims=True)


def first_scalars(node_ref):
    total = jnp.sum(jnp.sum(node_ref[...], axis=0), axis=0, keepdims=True)
    norm, inner = lane(total, 64), lane(total, 65)
    energy = NUGGET * norm + inner
    return norm, inner, energy, norm / energy


def finish_next_kernel(
    far_node_ref, node_skel_ref, nodes_ref, node_in_ref, near_ref, far_ref, rhs_ref, field_ref, basis_ref, transfer_ref, out_ref, pay_ref
):
    down = node_down(far_node_ref, node_skel_ref, nodes_ref, node_in_ref)
    for operand in (near_ref, far_ref, rhs_ref, field_ref):
        operand.wait()

    def leaf(l, carry):
        out_ref[pl.ds(2 * l, 2), :] = pair_of(leaf_row(l, down, far_ref, near_ref, basis_ref, transfer_ref))
        return carry

    leaves_in_parts((basis_ref, transfer_ref), leaf, 0)
    _, inner, energy, alpha = first_scalars(node_in_ref)
    rhs, field, field2 = rhs_ref[...], field_ref[...], out_ref[...]
    keep = inner / energy
    residual = keep * rhs - alpha * field
    image = NUGGET * residual + keep * field - alpha * field2
    base = NUGGET * rhs + field
    block = scalars([dot(residual, residual), dot(residual, image), dot(residual, base) + dot(rhs, image)])
    pay_ref[...] = jnp.broadcast_to(block[None], pay_ref.shape)


def last_kernel(rhs_ref, field_ref, field2_ref, node_ref, last_ref, solution_ref, residual_ref):
    norm, inner, energy, alpha = first_scalars(node_ref)
    total = jnp.sum(last_ref[...], axis=0)
    norm2 = lane(total, 64)
    beta = norm2 / norm
    alpha2 = norm2 / (lane(total, 65) + beta * lane(total, 66) + beta * beta * energy)
    rhs, field, field2 = rhs_ref[...], field_ref[...], field2_ref[...]
    keep = inner / energy
    residual = keep * rhs - alpha * field
    image = NUGGET * residual + keep * field - alpha * field2
    direction = residual + beta * rhs
    solution_ref[...] = alpha * rhs + alpha2 * direction
    residual_ref[...] = residual - alpha2 * (image + beta * (NUGGET * rhs + field))


class Operand:
    def __init__(self, source, ref, sems, parts):
        self.ref, self.shape = ref, ref.shape
        if parts == 1:
            self.copies = [pltpu.make_async_copy(source, ref, sems.at[0])]
        else:
            spans = [pl.ds(part * (ref.shape[0] // parts), ref.shape[0] // parts) for part in range(parts)]
            self.copies = [pltpu.make_async_copy(source.at[span], ref.at[span], sems.at[n]) for n, span in enumerate(spans)]

    def wait(self, part=0):
        self.copies[part].wait()

    def __getitem__(self, at):
        return self.ref[at]


def call(kernel, name, outs, ins, scratch=(), work=0, late=(), apart=(), split_up=()):
    floats = [at for at, array in enumerate(ins) if array.dtype != jnp.int32]

    def whole(shape):
        return pl.BlockSpec(shape, lambda i: (0,) * len(shape))

    def body(*refs):
        operands = list(refs[: len(ins)])
        buffers, sems = refs[-1 - len(floats) : -1], refs[-1]
        for k, at in enumerate(floats):
            operands[at] = Operand(operands[at], buffers[k], sems.at[k], PARTS if at in split_up else 1)
        for at in [at for at in floats if at not in late] + [at for at in late if at not in split_up]:
            operands[at].copies[0].start()
        for part in range(PARTS if split_up else 0):
            for at in split_up:
                operands[at].copies[part].start()
        for at in floats:
            if at not in late:
                operands[at].wait()
        kernel(*operands, *refs[len(ins) : -1 - len(floats)])

    return pl.pallas_call(
        body,
        grid=(1,),
        out_shape=[jax.ShapeDtypeStruct(shape, dtype) for shape, dtype in outs],
        in_specs=[SMEM if array.dtype == jnp.int32 else pl.BlockSpec(memory_space=pl.ANY) for array in ins],
        out_specs=[
            SMEM if dtype == jnp.int32 else pl.BlockSpec(memory_space=pl.ANY) if at in apart else whole(shape)
            for at, (shape, dtype) in enumerate(outs)
        ],
        scratch_shapes=list(scratch)
        + [pltpu.VMEM(ins[at].shape, ins[at].dtype) for at in floats]
        + [pltpu.SemaphoreType.DMA((len(floats), PARTS))],
        compiler_params=params(),
        cost_estimate=pl.CostEstimate(flops=work * 1_000_000_000, bytes_accessed=1_000_000, transcendentals=0),
        name=name,
    )(*ins)


def neighbours(block):
    count = lax.axis_size("grp") * lax.axis_size("dev")
    up = [(i, i + 1) for i in range(count - 1)]
    down = [(i + 1, i) for i in range(count - 1)]
    return lax.ppermute(block, AXES, up), lax.ppermute(block, AXES, down)


def exchange(copies, axes):
    return lax.all_to_all(copies, axes, 0, 0, tiled=True)


def on_device(rhs, points, leaf_basis, transfer, leaf_skel, node_skel, near_ids, near_count, far_leaf, far_node):
    rhs = rhs.reshape(2 * LEAVES, 128)
    basis = jnp.swapaxes(leaf_basis, 1, 2)
    far_leaf = far_leaf.T
    I32 = jnp.int32
    vector = ((2 * LEAVES, 128), F32)
    distances = pltpu.VMEM((2, PTS, 256), F32)
    near_scratch = [pltpu.VMEM((DUMMY + 1, 8, PTS), F32), pltpu.VMEM((LEAVES, PTS, 128), F32), distances]
    far_scratch = [pltpu.VMEM((LEAVES, 8, 1024), F32)]
    (pay,) = call(
        prepare_kernel,
        "prepare",
        [((32, 72, 128), F32)],
        [rhs, basis, transfer, leaf_skel, node_skel],
        work=4,
        late=(1, 2),
        split_up=(1, 2),
    )
    group = exchange(pay, "dev")
    targets, centres, far_targets, far_centres, own_list, other_list, own_part, near_pay = call(
        own_first_kernel,
        "own_first",
        [
            ((LEAVES, PTS, 128), BF16),
            ((LEAVES, 8, 128), F32),
            ((LEAVES, RANK, 128), BF16),
            ((LEAVES, 8, 128), F32),
            ((LIST,), I32),
            ((LIST,), I32),
            vector,
            ((4, LEAVES * PTS), F32),
        ],
        [near_ids.T, near_count, points, rhs, leaf_skel],
        near_scratch
        + [pltpu.VMEM((LEAVES, PTS, 128), BF16), pltpu.VMEM((LEAVES, RANK, 128), BF16), pltpu.SemaphoreType.DMA((2,))],
        work=15,
        apart=(0, 2),
    )
    prev_pay, next_pay = neighbours(near_pay)
    rows = jnp.swapaxes(group[:, 64:66], 0, 1).reshape(1, 64, 128)
    node_pay = jnp.broadcast_to(rows, (8, 64, 128))
    nodes = exchange(node_pay, "grp")
    near_part, far_part, stacks = call(
        middle_first_kernel,
        "middle_first",
        [vector, ((RANK, 128), F32), ((LEAVES, DEPTH, 1024), BF16)],
        [other_list, far_leaf, prev_pay, next_pay, targets, centres, own_part, far_targets, far_centres, group],
        near_scratch + far_scratch + [pltpu.VMEM((1024, 4, 128), F32), pltpu.VMEM((LEAVES, DEPTH, 1024), BF16), pltpu.SemaphoreType.DMA],
        work=20,
        apart=(2,),
        late=(7, 2, 3, 4, 5, 6),
    )
    field, pay = call(
        finish_first_kernel,
        "finish_first",
        [vector, ((32, 24, 128), F32)],
        [far_node, node_skel, nodes, near_part, far_part, rhs, basis, transfer],
        work=4,
        late=(3, 4, 5, 6, 7),
        split_up=(6, 7),
    )
    leaf_in = exchange(pay, "dev")
    own_part, near_field = call(
        own_next_kernel, "own_next", [vector, vector], [own_list, points, field, targets, centres], near_scratch, work=10
    )
    prev_val, next_val = neighbours(near_field)
    node_pay = jnp.broadcast_to(leaf_in[None, :, 16], (8, 32, 128))
    node_in = exchange(node_pay, "grp")
    near_part, far_part = call(
        middle_next_kernel,
        "middle_next",
        [vector, ((RANK, 128), F32)],
        [
            other_list, far_leaf, prev_pay, next_pay, prev_val, next_val, targets, centres, own_part, far_targets, stacks, leaf_in,
        ],
        near_scratch + far_scratch + [pltpu.VMEM((1024, 128), F32)],
        work=20,
        late=(6, 2, 3, 4, 5, 7, 8, 9, 10),
    )
    field2, pay = call(
        finish_next_kernel,
        "finish_next",
        [vector, ((256, 1, 128), F32)],
        [far_node, node_skel, nodes, node_in, near_part, far_part, rhs, field, basis, transfer],
        work=4,
        late=(4, 5, 6, 7, 8, 9),
        split_up=(8, 9),
    )
    last = exchange(pay, AXES)
    answer, residual = call(last_kernel, "last", [vector, vector], [rhs, field, field2, node_in, last], work=1)
    return answer.reshape(-1), residual.reshape(-1)


def solution(mesh):
    placed = (
        P(AXES),
        P(None, AXES),
        P(AXES, None, None),
        P(AXES, None, None),
        P(None, AXES),
        P(None, AXES),
        P(AXES, None),
        P(AXES),
        P(AXES, None),
        P(AXES, None),
    )
    return jax.shard_map(on_device, mesh=mesh, in_specs=placed, out_specs=(P(AXES), P(AXES)), check_vma=False)
```
